32 devices in a mesh: seq: 16 (over z, y, x), tensor: 2 (over core).
Axes of the slice: x: 2, y: 2, z: 4, core: 2. Of those that a mesh axis runs over, the one named last changes fastest.
Arguments:
- text_in: bfloat16 [4096, 768], P('seq'), may hold values from -6 to 6
- layout_in: bfloat16 [4096, 192], P('seq'), may hold values from -6 to 6
- text_cot: bfloat16 [4096, 768], P('seq'), may hold values from -6 to 6
- layout_cot: bfloat16 [4096, 192], P('seq'), may hold values from -6 to 6
- doc_ids: int32 [4096], P('seq'), may hold values from 0 to 3, as said below
- span_ids: int32 [4096], P('seq'), may hold values from 0 to 15, as said below
- intersection_flags: int32 [4096], P('seq'), may hold values 0 or 1
- text_qkv: bfloat16 [3, 768, 768], P(None, None, 'tensor'), may hold values from -0.21875 to 0.21875
- text_qv_bias: bfloat16 [2, 768], P(None, 'tensor'), may hold values from -3 to 3
- text_out: bfloat16 [768, 768], P('tensor'), may hold values from -3.5 to 3.5
- text_out_bias: bfloat16 [2, 768], replicated, may hold values from -3 to 3
- text_gains: bfloat16 [2, 768], replicated, may hold values from 0.25 to 1.75
- text_shifts: bfloat16 [2, 768], replicated, may hold values from -3 to 3
- text_up: bfloat16 [768, 3072], P(None, 'tensor'), may hold values from -0.21875 to 0.21875
- text_up_bias: bfloat16 [3072], P('tensor'), may hold values from -3 to 3
- text_down: bfloat16 [3072, 768], P('tensor'), may hold values from -0.109375 to 0.109375
- layout_qkv: bfloat16 [3, 192, 192], P(None, None, 'tensor'), may hold values from -0.4375 to 0.4375
- layout_qv_bias: bfloat16 [2, 192], P(None, 'tensor'), may hold values from -3 to 3
- layout_out: bfloat16 [192, 192], P('tensor'), may hold values from -6 to 6
- layout_out_bias: bfloat16 [2, 192], replicated, may hold values from -3 to 3
- layout_gains: bfloat16 [2, 192], replicated, may hold values from 0.25 to 1.75
- layout_shifts: bfloat16 [2, 192], replicated, may hold values from -3 to 3
- layout_up: bfloat16 [192, 768], P(None, 'tensor'), may hold values from -0.4375 to 0.4375
- layout_up_bias: bfloat16 [768], P('tensor'), may hold values from -3 to 3
- layout_down: bfloat16 [768, 192], P('tensor'), may hold values from -0.21875 to 0.21875
Outputs:
- text_result: bfloat16 [4096, 768], P('seq')
- layout_result: bfloat16 [4096, 192], P('seq')
- text_in_grad: bfloat16 [4096, 768], P('seq')
- layout_in_grad: bfloat16 [4096, 192], P('seq')
- text_qkv_grad: float32 [3, 768, 768], P(None, None, 'tensor')
- text_qv_bias_grad: float32 [2, 768], P(None, 'tensor')
- text_out_grad: float32 [768, 768], P('tensor')
- text_out_bias_grad: float32 [2, 768], replicated
- text_gains_grad: float32 [2, 768], replicated
- text_shifts_grad: float32 [2, 768], replicated
- text_up_grad: float32 [768, 3072], P(None, 'tensor')
- text_up_bias_grad: float32 [3072], P('tensor')
- text_down_grad: float32 [3072, 768], P('tensor')
- layout_qkv_grad: float32 [3, 192, 192], P(None, None, 'tensor')
- layout_qv_bias_grad: float32 [2, 192], P(None, 'tensor')
- layout_out_grad: float32 [192, 192], P('tensor')
- layout_out_bias_grad: float32 [2, 192], replicated
- layout_gains_grad: float32 [2, 192], replicated
- layout_shifts_grad: float32 [2, 192], replicated
- layout_up_grad: float32 [192, 768], P(None, 'tensor')
- layout_up_bias_grad: float32 [768], P('tensor')
- layout_down_grad: float32 [768, 192], P('tensor')
The draws below stay inside these ranges and needn't reach their ends.
Inputs may be any that keep to these rules, and one draw needn't show every extreme that they name: `doc_ids`: never falls along the rows; every document lies inside one aligned block of 2048 rows and has at most 2048 rows; the first such block is one whole document. `span_ids`: never falls along the rows; each aligned block of 512 rows holds exactly two windows, each with an id of its own that no other row carries, and neither window has exactly 256 rows.
All inputs are finite; a program needn't handle non-finite values. No bound on the sum of `intersection_flags` on one device may be relied on, other than what follows from the above.
Results may differ from the reference program's by a relative error of at most 0.017.
The reference program's roundings to bfloat16 on the way count: a program that leaves them out, or rounds other values in their place, can miss the bound.
Values may be sent and summed in bfloat16 or wider, within the bound.
No kernel may reach another device: no remote copies, remote signals or barrier semaphores. Data moves between devices by JAX's collectives and lax.ppermute only.
A program may use at most 128 MiB of HBM per device.

```python
import math
import jax
import jax.numpy as jnp
from jax import lax

H = 12
HT = 64
HL = 16
FF = 3072
FFL = 768
D = 768
DL = 192
SPAN = 512
DOC = 2048
TOKENS = 4096


def draw_doc_ids(key, part):
    key = jax.random.fold_in(key, 11)
    block_count = TOKENS // DOC
    cuts = jax.random.randint(key, (block_count,), 1, DOC)
    cuts = cuts.at[0].set(DOC)
    positions = jnp.arange(TOKENS, dtype=jnp.int32)
    block = positions // DOC
    return (2 * block + (positions % DOC >= cuts[block]).astype(jnp.int32)).astype(jnp.int32)


def draw_span_ids(key, part):
    key = jax.random.fold_in(key, 23)
    block_count = TOKENS // SPAN
    cuts = jax.random.randint(key, (block_count,), 1, SPAN - 1)
    cuts = cuts + (cuts >= SPAN // 2).astype(jnp.int32)
    positions = jnp.arange(TOKENS, dtype=jnp.int32)
    block = positions // SPAN
    return (2 * block + (positions % SPAN >= cuts[block]).astype(jnp.int32)).astype(jnp.int32)


def set_ends(array, stream_key, smallest, largest):
    index_at = [jax.random.randint(jax.random.fold_in(stream_key, axis), (), 0, length) for axis, length in enumerate(array.shape)]
    longest = array.shape.index(max(array.shape))
    next_to = index_at[:longest] + [(index_at[longest] + 1) % array.shape[longest]] + index_at[longest + 1:]
    return array.at[tuple(index_at)].set(smallest).at[tuple(next_to)].set(largest)


def levels(key, shape, shards, smallest, high):
    def one(axis_at, blocks):
        heights = jax.random.uniform(jax.random.fold_in(jax.random.fold_in(key, 6), axis_at), (blocks,), jnp.float32, smallest / len(shards), high / len(shards))
        return jnp.repeat(jnp.exp(heights), shape[axis_at] // blocks).reshape((-1,) + (1,) * (len(shape) - axis_at - 1))

    level = one(*shards[0])
    for cut in shards[1:]:
        level = level * one(*cut)
    return level


def noise(stream_key, extent, deviation, bound, pieces=(), held_as=jnp.bfloat16):
    drawn = deviation * jax.random.normal(stream_key, extent, jnp.float32)
    if pieces:
        drawn = drawn * levels(stream_key, extent, pieces, -0.22, 0.18)
    return jnp.clip(drawn, -bound, bound).astype(held_as)


def setup_inputs(seed: int = 0) -> dict:
    key_of = jax.random.split(jax.random.key(seed), 26)
    text_in = noise(key_of[0], (TOKENS, D), 1.0, 6.0, ((0, 16),))
    layout_in = noise(key_of[1], (TOKENS, DL), 1.0, 6.0, ((0, 16),))
    text_cot = noise(key_of[2], (TOKENS, D), 1.0, 6.0, ((0, 16),))
    layout_cot = noise(key_of[3], (TOKENS, DL), 1.0, 6.0, ((0, 16),))
    doc_ids = draw_doc_ids(jax.random.fold_in(key_of[25], 71), 0)
    span_ids = draw_span_ids(jax.random.fold_in(key_of[25], 71), 0)
    intersection_flags = set_ends((jax.random.randint(key_of[6], (TOKENS,), 0, 8) < 1).astype(jnp.int32), jax.random.fold_in(key_of[6], 1), 0, 1)
    text_qkv = noise(key_of[7], (3, D, D), D ** -0.5, 0.21875, ((2, 2),))
    text_qv_bias = noise(key_of[8], (2, D), 0.5, 3.0, ((1, 2),))
    text_out = noise(key_of[9], (D, D), (max(2 * D // SPAN, 1)) ** -0.5, 3.5, ((0, 2),))
    text_out_bias = noise(key_of[10], (2, D), 0.5, 3.0)
    text_gains = jnp.clip(1.0 + 0.15 * jax.random.normal(key_of[11], (2, D), jnp.float32), 0.25, 1.75).astype(jnp.bfloat16)
    text_shifts = noise(key_of[12], (2, D), 0.5, 3.0)
    text_up = noise(key_of[13], (D, FF), D ** -0.5, 0.21875, ((1, 2),))
    text_up_bias = noise(key_of[14], (FF,), 0.5, 3.0, ((0, 2),))
    text_down = noise(key_of[15], (FF, D), FF ** -0.5, 0.109375, ((0, 2),))
    layout_qkv = noise(key_of[16], (3, DL, DL), DL ** -0.5, 0.4375, ((2, 2),))
    layout_qv_bias = noise(key_of[17], (2, DL), 0.5, 3.0, ((1, 2),))
    layout_out = noise(key_of[18], (DL, DL), (max(2 * DL // SPAN, 1)) ** -0.5, 6.0, ((0, 2),))
    layout_out_bias = noise(key_of[19], (2, DL), 0.5, 3.0)
    layout_gains = jnp.clip(1.0 + 0.15 * jax.random.normal(key_of[20], (2, DL), jnp.float32), 0.25, 1.75).astype(jnp.bfloat16)
    layout_shifts = noise(key_of[21], (2, DL), 0.5, 3.0)
    layout_up = noise(key_of[22], (DL, FFL), DL ** -0.5, 0.4375, ((1, 2),))
    layout_up_bias = noise(key_of[23], (FFL,), 0.5, 3.0, ((0, 2),))
    layout_down = noise(key_of[24], (FFL, DL), FFL ** -0.5, 0.21875, ((0, 2),))
    return dict(text_in=text_in, layout_in=layout_in, text_cot=text_cot, layout_cot=layout_cot, doc_ids=doc_ids, span_ids=span_ids, intersection_flags=intersection_flags, text_qkv=text_qkv, text_qv_bias=text_qv_bias, text_out=text_out, text_out_bias=text_out_bias, text_gains=text_gains, text_shifts=text_shifts, text_up=text_up, text_up_bias=text_up_bias, text_down=text_down, layout_qkv=layout_qkv, layout_qv_bias=layout_qv_bias, layout_out=layout_out, layout_out_bias=layout_out_bias, layout_gains=layout_gains, layout_shifts=layout_shifts, layout_up=layout_up, layout_up_bias=layout_up_bias, layout_down=layout_down)


EPS = 1e-06
NEG = -1e+30
HIGH = lax.Precision.HIGHEST

@jax.custom_vjp
def low(v):
    return lax.optimization_barrier(v.astype(jnp.bfloat16)).astype(jnp.float32)

@jax.custom_vjp
def low_back(v):
    return v

def low_keep(v):
    return (low(v), None)

def low_pass(kept, grad):
    return (grad,)

def back_keep(v):
    return (v, None)

def back_low(kept, grad):
    return (low(grad),)
low.defvjp(low_keep, low_pass)
low_back.defvjp(back_keep, back_low)

def matmul(left, right):
    return jnp.dot(left, right, precision=HIGH)

def layer_norm(total, gain, shift):
    center = total - lax.optimization_barrier(jnp.mean(total, axis=-1, keepdims=True))
    return center * lax.rsqrt(lax.optimization_barrier(jnp.mean(center * center, axis=-1, keepdims=True)) + EPS) * gain + shift

def project(inputs, params):
    qkv_weight, qv_bias = (params[0], params[1])
    queries = low_back(low(matmul(inputs, qkv_weight[0]) + qv_bias[0]))
    key_rows = low_back(low(matmul(inputs, qkv_weight[1])))
    values = low_back(low(matmul(inputs, qkv_weight[2]) + qv_bias[1]))
    return (queries, key_rows, values)

def attention(text_side, layout_side, doc_ids, span_ids):
    query_text, key_text, value_text = text_side
    query_layout, key_layout, value_layout = layout_side
    row_count = query_text.shape[0]
    block_rows = math.gcd(row_count, 512)
    block_count = row_count // block_rows
    key_heads_text = key_text.reshape(row_count, H, HT)
    key_heads_layout = key_layout.reshape(row_count, H, HL)
    value_heads_text = value_text.reshape(row_count, H, HT)
    value_heads_layout = value_layout.reshape(row_count, H, HL)

    def one_block(items):
        block_text, block_layout, block_doc, block_span = items
        text_part = jnp.einsum('qhe,khe->hqk', block_text.reshape(block_rows, H, HT), key_heads_text, precision=HIGH)
        layout_part = jnp.einsum('qhe,khe->hqk', block_layout.reshape(block_rows, H, HL), key_heads_layout, precision=HIGH)
        scores = low_back(text_part * HT ** (-0.5) + layout_part * HL ** (-0.5))
        visible = (block_doc[:, None] == doc_ids[None, :]) & (block_span[:, None] == span_ids[None, :])
        masked = jnp.where(visible[None], scores, NEG)
        highest = lax.optimization_barrier(jnp.max(masked, axis=2, keepdims=True))
        weights = jnp.where(visible[None], jnp.exp(masked - highest), 0.0)
        probs_low = low(weights / lax.optimization_barrier(jnp.sum(weights, axis=2, keepdims=True)))
        context_text = jnp.einsum('hqk,khe->qhe', probs_low, value_heads_text, precision=HIGH)
        context_layout = jnp.einsum('hqk,khe->qhe', probs_low, value_heads_layout, precision=HIGH)
        return (context_text.reshape(block_rows, H * HT), context_layout.reshape(block_rows, H * HL))
    context_text, context_layout = lax.map(jax.checkpoint(one_block), (query_text.reshape(block_count, block_rows, H * HT), query_layout.reshape(block_count, block_rows, H * HL), doc_ids.reshape(block_count, block_rows), span_ids.reshape(block_count, block_rows)))
    context_text = low_back(low(context_text.reshape(row_count, H * HT)))
    context_layout = low_back(low(context_layout.reshape(row_count, H * HL)))
    return (context_text, context_layout)

def finish(inputs, context, params):
    out_weight, out_bias, norm_gains, norm_shifts = (params[2], params[3], params[4], params[5])
    up_weight, up_bias, down_weight = (params[6], params[7], params[8])
    attended = low_back(matmul(context, out_weight) + out_bias[0])
    hidden = layer_norm(inputs + attended, norm_gains[0], norm_shifts[0])
    before = low_back(matmul(low(hidden), up_weight) + up_bias)
    activated = low(jax.nn.gelu(before, approximate=False))
    ffn_rows = low_back(matmul(activated, down_weight) + out_bias[1])
    return layer_norm(hidden + ffn_rows, norm_gains[1], norm_shifts[1])

def reference(text_in, layout_in, text_cot, layout_cot, doc_ids, span_ids, intersection_flags, text_qkv, text_qv_bias, text_out, text_out_bias, text_gains, text_shifts, text_up, text_up_bias, text_down, layout_qkv, layout_qv_bias, layout_out, layout_out_bias, layout_gains, layout_shifts, layout_up, layout_up_bias, layout_down):
    text_params = tuple((weight.astype(jnp.float32) for weight in (text_qkv, text_qv_bias, text_out, text_out_bias, text_gains, text_shifts, text_up, text_up_bias, text_down)))
    layout_params = tuple((weight.astype(jnp.float32) for weight in (layout_qkv, layout_qv_bias, layout_out, layout_out_bias, layout_gains, layout_shifts, layout_up, layout_up_bias, layout_down)))

    def forward(text_rows, layout_rows, text_weights, layout_weights):
        text_side = project(text_rows, text_weights)
        layout_side = project(layout_rows, layout_weights)
        context_text, context_layout = attention(text_side, layout_side, doc_ids, span_ids)
        return (finish(text_rows, context_text, text_weights), finish(layout_rows, context_layout, layout_weights))
    outputs, pullback = jax.vjp(forward, text_in.astype(jnp.float32), layout_in.astype(jnp.float32), text_params, layout_params)
    keep_rows = (1 - intersection_flags).astype(jnp.float32)[:, None]
    text_grad, layout_grad, text_grads, layout_grads = pullback((text_cot.astype(jnp.float32) * keep_rows, layout_cot.astype(jnp.float32) * keep_rows))
    return (outputs[0].astype(jnp.bfloat16), outputs[1].astype(jnp.bfloat16), text_grad.astype(jnp.bfloat16), layout_grad.astype(jnp.bfloat16), text_grads[0], text_grads[1], text_grads[2], text_grads[3], text_grads[4], text_grads[5], text_grads[6], text_grads[7], text_grads[8], layout_grads[0], layout_grads[1], layout_grads[2], layout_grads[3], layout_grads[4], layout_grads[5], layout_grads[6], layout_grads[7], layout_grads[8])
```

```python
from functools import partial

import jax
import jax.numpy as jnp
from jax import lax
from jax.experimental import pallas as pl
from jax.experimental.pallas import tpu as pltpu
from jax.sharding import PartitionSpec as P

HT = 64
HL = 16
EPS = 1e-06
NEG = -1e30
BF = jnp.bfloat16
F32 = jnp.float32
LANES = 128


def exchange(shard, mask, axis="seq"):
    return lax.ppermute(shard, axis, [(i, i ^ mask) for i in range(lax.axis_size(axis))])


def over_cores(shard):
    return exchange(shard, 1, "tensor")


def dot(left, right):
    return lax.dot_general(left, right, (((1,), (0,)), ((), ())), preferred_element_type=F32)


def dot_nt(left, right):
    return lax.dot_general(left, right, (((1,), (1,)), ((), ())), preferred_element_type=F32)


def dot_tn(left, right):
    return lax.dot_general(left, right, (((0,), (0,)), ((), ())), preferred_element_type=F32)


def call(kernel, outs, *args, scratch=(), smem=0, anys=(), flops=10**8):
    specs = []
    for at in range(len(args)):
        if at < smem:
            specs.append(pl.BlockSpec(memory_space=pltpu.SMEM))
        elif at in anys:
            specs.append(pl.BlockSpec(memory_space=pl.ANY))
        else:
            specs.append(pl.BlockSpec(memory_space=pltpu.VMEM))
    moved = sum(a.size * a.dtype.itemsize for a in args) + sum(
        o.size * o.dtype.itemsize for o in outs
    )
    return pl.pallas_call(
        kernel,
        out_shape=tuple(outs),
        in_specs=specs,
        out_specs=tuple(pl.BlockSpec(memory_space=pltpu.VMEM) for _ in outs),
        scratch_shapes=list(scratch),
        compiler_params=pltpu.CompilerParams(vmem_limit_bytes=48 * 1024 * 1024),
        cost_estimate=pl.CostEstimate(flops=flops, bytes_accessed=moved, transcendentals=0),
    )(*args)


def shape(dims, dtype):
    return jax.ShapeDtypeStruct(tuple(dims), dtype)


def project_rows(text_rows, layout_rows, weight_t, bias_t, weight_l, bias_l, which, write):
    text_part = dot(text_rows, weight_t[which])
    layout_part = dot(layout_rows, weight_l[which])
    if which != 1:
        row = which // 2
        text_part = text_part + bias_t[row : row + 1, :].astype(F32)
        layout_part = layout_part + bias_l[row : row + 1, :].astype(F32)
    pad = jnp.zeros((layout_part.shape[0], LANES - layout_part.shape[1]), F32)
    write(text_part.astype(BF), jnp.concatenate([layout_part, pad], axis=1).astype(BF))


def project_kernel(xt, xl, wt, bt, wl, bl, q_out, k_out, v_out):
    width = wt.shape[2]
    for which, out in enumerate((q_out, k_out, v_out)):

        def write(text_part, layout_part, out=out):
            out[:, :width] = text_part
            out[:, width:] = layout_part

        project_rows(xt[...], xl[...], wt, bt, wl, bl, which, write)


def hidden_bias(keys, columns):
    rows = keys.shape[1]
    down = jnp.broadcast_to(keys, (LANES, rows)).T
    parts = [
        jnp.where(down == keys[:, at : at + LANES], 0.0, NEG).astype(F32)
        for at in range(0, columns, LANES)
    ]
    return jnp.concatenate(parts, axis=1)


def head_mask(member, head, text_value, layout_value, axis):
    dims = (1, 2 * LANES) if axis == 1 else (2 * LANES, 1)
    at = lax.broadcasted_iota(jnp.int32, dims, axis)
    text = (at >= member * HT) & (at < (member + 1) * HT)
    layout = (at >= LANES + head * HL) & (at < LANES + (head + 1) * HL)
    return jnp.where(text, text_value, jnp.where(layout, layout_value, 0.0)).astype(F32)


def pair_of(ref, pair, width):
    return jnp.concatenate([ref[:, LANES * pair : LANES * (pair + 1)], ref[:, width:]], axis=1)


def probabilities(key_pair, query_head, bias):
    scores = dot_nt(key_pair, query_head) + bias
    weights = jnp.exp(scores - jnp.max(scores, axis=0, keepdims=True))
    return weights * (1.0 / jnp.sum(weights, axis=0, keepdims=True))


SCALE_T = HT ** (-0.5)
SCALE_L = HL ** (-0.5)


def attend_kernel(
    q_own, k_own, v_own, xt, xl, wt, bt, wl, bl, keys, out_t, out_l, part_out, k_all, v_all, context
):
    rows, width = q_own.shape[0], wt.shape[2]
    for which, own, target in ((1, k_own, k_all), (2, v_own, v_all)):
        target[:rows, :] = own[...]

        def write(text_part, layout_part, target=target):
            target[rows:, :width] = text_part
            target[rows:, width:] = layout_part

        project_rows(xt[...], xl[...], wt, bt, wl, bl, which, write)
    bias = hidden_bias(keys[...], rows)
    layout_sum = jnp.zeros((LANES, rows), F32)
    for pair in range(width // LANES):
        query_pair, key_pair = pair_of(q_own, pair, width), pair_of(k_all, pair, width)
        value_turned = pair_of(v_all, pair, width).T
        text_sum = jnp.zeros((LANES, rows), F32)
        for member in range(2):
            head = 2 * pair + member
            mask = head_mask(member, head, SCALE_T, SCALE_L, 1).astype(BF)
            probs_low = probabilities(key_pair, query_pair * mask, bias).astype(BF)
            turned = dot(value_turned, probs_low) * head_mask(member, head, 1.0, 1.0, 0)
            text_sum += turned[:LANES]
            layout_sum += turned[LANES:]
        context[:, LANES * pair : LANES * (pair + 1)] = text_sum.T.astype(BF)
    context[:, width:] = layout_sum.T.astype(BF)
    text_width = out_t.shape[1]
    part_out[:, :text_width] = dot(context[:, :width], out_t[...])
    part_out[:, text_width:] = dot(
        context[:, width : width + out_l.shape[0]], out_l[...]
    )


def norm_parts(total):
    center = total - jnp.mean(total, axis=1, keepdims=True)
    inverse = lax.rsqrt(jnp.mean(center * center, axis=1, keepdims=True) + EPS)
    return center * inverse, inverse


def norm_back(upstream, normed, inverse, gain):
    scaled = upstream * gain
    return inverse * (
        scaled
        - jnp.mean(scaled, axis=1, keepdims=True)
        - normed * jnp.mean(scaled * normed, axis=1, keepdims=True)
    )


def gelu_parts(before):
    share = 0.5 * (1.0 + lax.erf(before * (0.5**0.5)))
    slope = share + before * (jnp.exp(-0.5 * before * before) * 0.3989422804014327)
    return before * share, slope


def forward_kernel(
    idx, xt, xl, part, back, ob_t, ob_l, g_t, g_l, s_t, s_l, up_t, ub_t, dn_t, up_l, ub_l, dn_l,
    hidden_out, normed_out, inverse_out, mine_out, low_out, slope_t, slope_l, ffn_out,
):
    width = xt.shape[1]
    whole = part.shape[1]
    half = mine_out.shape[0]
    streams = (
        (0, width, xt, ob_t, g_t, s_t, up_t, ub_t, dn_t, slope_t),
        (width, whole, xl, ob_l, g_l, s_l, up_l, ub_l, dn_l, slope_l),
    )
    for at, (lo, hi, x, ob, g, s, up, ub, dn, slope_out) in enumerate(streams):
        total = x[...].astype(F32) + (part[:, lo:hi] + back[:, lo:hi]) + ob[0:1, :].astype(F32)
        normed, inverse = norm_parts(total)
        hidden = normed * g[0:1, :].astype(F32) + s[0:1, :].astype(F32)
        hidden_out[:, lo:hi] = hidden
        normed_out[:, lo:hi] = normed
        inverse_out[:, LANES * at : LANES * (at + 1)] = jnp.broadcast_to(
            inverse, (inverse.shape[0], LANES)
        )
        low_out[:, lo:hi] = hidden.astype(BF)
    mine_out[...] = low_out[pl.ds(pl.multiple_of(idx[3] * half, half), half), :]
    for lo, hi, x, ob, g, s, up, ub, dn, slope_out in streams:
        rows_low = low_out[:, lo:hi]
        units = up.shape[1]
        step = min(units, 384)
        total = None
        for cut in range(0, units, step):
            before = dot(rows_low, up[:, cut : cut + step]) + ub[:, cut : cut + step].astype(F32)
            activated, slope = gelu_parts(before)
            slope_out[:, cut : cut + step] = slope
            term = dot(activated.astype(BF), dn[cut : cut + step, :])
            total = term if total is None else total + term
        ffn_out[:, lo:hi] = total


def second_norm_kernel(
    idx, hidden, part, back, ct, cl, keep, ob_t, ob_l, g_t, g_l, s_t, s_l,
    rt_out, rl_out, second_out, low_out, mine_out, sums_out,
):
    width, whole = ct.shape[1], hidden.shape[1]
    half = mine_out.shape[0]
    for lo, hi, cot, ob, g, s, result in (
        (0, width, ct, ob_t, g_t, s_t, rt_out),
        (width, whole, cl, ob_l, g_l, s_l, rl_out),
    ):
        total = hidden[:, lo:hi] + (part[:, lo:hi] + back[:, lo:hi]) + ob[1:2, :].astype(F32)
        normed, inverse = norm_parts(total)
        gain = g[1:2, :].astype(F32)
        result[...] = (normed * gain + s[1:2, :].astype(F32)).astype(BF)
        upstream = cot[...].astype(F32) * keep[...]
        grad = norm_back(upstream, normed, inverse, gain)
        second_out[:, lo:hi] = grad
        low = grad.astype(BF)
        low_out[:, lo:hi] = low
        sums_out[0:1, lo:hi] = jnp.sum(upstream * normed, axis=0, keepdims=True)
        sums_out[1:2, lo:hi] = jnp.sum(upstream, axis=0, keepdims=True)
        sums_out[2:3, lo:hi] = jnp.sum(low.astype(F32), axis=0, keepdims=True)
    mine_out[...] = low_out[pl.ds(pl.multiple_of(idx[3] * half, half), half), :]


def ffn_back_kernel(grad, slope_t, slope_l, up_t, dn_t, up_l, dn_l, part_out, bias_t, bias_l):
    width = up_t.shape[0]
    whole = grad.shape[1]
    for lo, hi, slope, up, dn, bias in (
        (0, width, slope_t, up_t, dn_t, bias_t),
        (width, whole, slope_l, up_l, dn_l, bias_l),
    ):
        rows = grad[:, lo:hi]
        units = up.shape[1]
        step = min(units, 384)
        total = None
        for cut in range(0, units, step):
            act_grad = dot_nt(rows, dn[cut : cut + step, :])
            before_grad = (act_grad * slope[:, cut : cut + step]).astype(BF)
            bias[:, cut : cut + step] = jnp.sum(before_grad.astype(F32), axis=0, keepdims=True)
            term = dot_nt(before_grad, up[:, cut : cut + step])
            total = term if total is None else total + term
        part_out[:, lo:hi] = total


def first_norm_kernel(
    second, part, back, normed_in, inverse_in, g_t, g_l, first_out, low_out, sums_out
):
    width, whole = g_t.shape[1], second.shape[1]
    for at, (lo, hi, g) in enumerate(((0, width, g_t), (width, whole, g_l))):
        upstream = second[:, lo:hi] + (part[:, lo:hi] + back[:, lo:hi])
        normed = normed_in[:, lo:hi]
        inverse = inverse_in[:, LANES * at : LANES * at + 1]
        grad = norm_back(upstream, normed, inverse, g[0:1, :].astype(F32))
        first_out[:, lo:hi] = grad
        low = grad.astype(BF)
        low_out[:, lo:hi] = low
        sums_out[0:1, lo:hi] = jnp.sum(upstream * normed, axis=0, keepdims=True)
        sums_out[1:2, lo:hi] = jnp.sum(upstream, axis=0, keepdims=True)
        sums_out[2:3, lo:hi] = jnp.sum(low.astype(F32), axis=0, keepdims=True)


def unit_grads_kernel(idx, *refs):
    (
        low_parts, grad_parts, (up_t, dn_t, dn_l, ub_t, up_l, ub_l),
        (up_keep, up_send, dn_keep, dn_send),
        (low, grad, w_up, w_dn, w_dnl, held, sems),
    ) = refs[:7], refs[7:14], refs[14:20], refs[20:24], refs[24:]
    quarter = idx[1] * 2 + idx[0]
    zz = idx[2]
    copies = []
    for parts, target in ((low_parts, low), (grad_parts, grad)):
        at = 0
        for part in parts:
            count = part.shape[0]
            copies.append((part, target.at[pl.ds(at, count), :]))
            at += count
    units, units_l = w_dn.shape[0], w_dnl.shape[0]
    start = pl.multiple_of(quarter * units, units)
    copies.append((up_t.at[:, pl.ds(start, units)], w_up))
    copies.append((dn_t.at[pl.ds(start, units), :], w_dn))
    copies.append((dn_l.at[pl.ds(pl.multiple_of(quarter * units_l, units_l), units_l), :], w_dnl))
    copies = [pltpu.make_async_copy(s, d, sems.at[k]) for k, (s, d) in enumerate(copies)]
    for c in copies:
        c.start()
    for c in copies:
        c.wait()
    width = w_up.shape[0]
    piece = width // 4
    slot_rows = 16

    def grads(lo, hi, up, bias, down):
        before = dot(low[:, lo:hi], up) + bias
        activated, slope = gelu_parts(before)
        before_grad = (dot_nt(grad[:, lo:hi], down) * slope).astype(BF)
        return activated.astype(BF), before_grad

    act_t, back_t = grads(0, width, w_up[...], ub_t[:, pl.ds(start, units)].astype(F32), w_dn[...])
    act_l, back_l = grads(width, low.shape[1], up_l[...], ub_l[...].astype(F32), w_dnl[...])

    def place_layout(matrix):
        pad = jnp.zeros((matrix.shape[0], LANES - matrix.shape[1]), F32)
        padded = jnp.concatenate([matrix, pad], axis=1)
        for k in range(4):
            for slot in range(3):
                first = slot_rows * (3 * k + slot)
                held[k ^ zz, piece : piece + slot_rows, LANES * slot : LANES * (slot + 1)] = padded[
                    first : first + slot_rows
                ]

    def hand_out(keep, send):
        for at in range(2):
            keep[at] = held[2 * at]
            send[at] = held[2 * at + 1].astype(BF)

    up_grad = dot_tn(low[:, :width], back_t)
    for k in range(4):
        held[k ^ zz, :piece, :] = up_grad[piece * k : piece * (k + 1)]
    place_layout(dot_tn(low[:, width:], back_l))
    hand_out(up_keep, up_send)
    down_grad = dot_tn(act_t, grad[:, :width])
    part = piece // 2
    for k in range(4):
        for side in range(2):
            held[k ^ zz, part * side : part * (side + 1), :] = down_grad[
                part * k : part * (k + 1), units * side : units * (side + 1)
            ]
    place_layout(dot_tn(grad[:, width:], act_l))
    hand_out(dn_keep, dn_send)


def attention_back_kernel(
    idx, q_own, k_all, v_all, xt, xl, xt_p, xl_p, wt, bt, wl, bl, keys, out_t, out_l, ag_own, ag_p,
    sums_two, sums_one, bias_t, bias_l,
    keep_out, send_out, part_out, small_out,
    q_all, g_all, x_all, ag_all, context, dq, dk, dv, matrices, held,
):
    rows, width = q_own.shape[0], wt.shape[2]
    wide, whole = xt.shape[1], ag_own.shape[1]
    bx, by, zz = idx[0], idx[1], idx[2]
    x_all[:rows, :wide] = xt[...]
    x_all[:rows, wide:] = xl[...]
    x_all[rows:, :wide] = xt_p[...]
    x_all[rows:, wide:] = xl_p[...]
    ag_all[:rows, :] = ag_own[...]
    ag_all[rows:, :] = ag_p[...]
    q_all[:rows, :] = q_own[...]

    def write(text_part, layout_part):
        q_all[rows:, :width] = text_part
        q_all[rows:, width:] = layout_part

    project_rows(xt_p[...], xl_p[...], wt, bt, wl, bl, 0, write)
    g_all[:, :width] = dot_nt(ag_all[:, :wide], out_t[...]).astype(BF)
    layout_grad = dot_nt(ag_all[:, wide:], out_l[...])
    pad = jnp.zeros((2 * rows, LANES - layout_grad.shape[1]), F32)
    g_all[:, width:] = jnp.concatenate([layout_grad, pad], axis=1).astype(BF)
    bias = hidden_bias(keys[...], 2 * rows)
    zero_turned, zero = jnp.zeros((LANES, 2 * rows), F32), jnp.zeros((2 * rows, LANES), F32)
    layout_context, layout_dq, layout_dk, layout_dv = zero_turned, zero_turned, zero, zero
    for pair in range(width // LANES):
        query_pair, key_pair = pair_of(q_all, pair, width), pair_of(k_all, pair, width)
        grad_pair, value_pair = pair_of(g_all, pair, width), pair_of(v_all, pair, width)
        key_turned, value_turned = key_pair.T, value_pair.T
        text_context, text_dq, text_dk, text_dv = zero_turned, zero_turned, zero, zero
        for member in range(2):
            head = 2 * pair + member
            query_head = query_pair * head_mask(member, head, SCALE_T, SCALE_L, 1).astype(BF)
            grad_head = grad_pair * head_mask(member, head, 1.0, 1.0, 1).astype(BF)
            probs = probabilities(key_pair, query_head, bias)
            probs_low = probs.astype(BF)
            prob_grads = dot_nt(value_pair, grad_head)
            delta = jnp.sum(probs * prob_grads, axis=0, keepdims=True)
            score_grads = (probs * (prob_grads - delta)).astype(BF)
            value_part = dot(probs_low, grad_head)
            text_dv += value_part[:, :LANES]
            layout_dv += value_part[:, LANES:]
            key_part = dot(score_grads, query_head)
            text_dk += key_part[:, :LANES]
            layout_dk += key_part[:, LANES:]
            query_part = dot(key_turned, score_grads) * head_mask(member, head, SCALE_T, SCALE_L, 0)
            text_dq += query_part[:LANES]
            layout_dq += query_part[LANES:]
            context_part = dot(value_turned, probs_low) * head_mask(member, head, 1.0, 1.0, 0)
            text_context += context_part[:LANES]
            layout_context += context_part[LANES:]
        columns = slice(LANES * pair, LANES * (pair + 1))
        context[:, columns] = text_context.T.astype(BF)
        dq[:, columns] = text_dq.T.astype(BF)
        dk[:, columns] = text_dk.astype(BF)
        dv[:, columns] = text_dv.astype(BF)
    context[:, width:] = layout_context.T.astype(BF)
    dq[:, width:] = layout_dq.T.astype(BF)
    dk[:, width:] = layout_dk.astype(BF)
    dv[:, width:] = layout_dv.astype(BF)

    heads_l = wl.shape[2]
    total_t = total_l = None
    for which, grad in enumerate((dq, dk, dv)):
        term_t = dot_nt(grad[:rows, :width], wt[which])
        term_l = dot_nt(grad[:rows, width : width + heads_l], wl[which])
        total_t = term_t if which == 0 else total_t + term_t
        total_l = term_l if which == 0 else total_l + term_l
    part_out[:, :wide] = total_t
    part_out[:, wide:] = total_l

    small_out[...] = jnp.zeros_like(small_out)
    small_out[0:3, :whole] = sums_two[...]
    small_out[3:6, :whole] = sums_one[...]
    units, room = bias_t.shape[1], small_out.shape[1]
    small_out[6:7, :] = bias_t[:, :room]
    small_out[7:8, : units - room] = bias_t[:, room:]
    small_out[8:9, : bias_l.shape[1]] = bias_l[...]
    small_out[9:10, : dq.shape[1]] = jnp.sum(dq[:rows, :].astype(F32), axis=0, keepdims=True)
    small_out[10:11, : dv.shape[1]] = jnp.sum(dv[:rows, :].astype(F32), axis=0, keepdims=True)

    side = wide // 2
    start = pl.multiple_of(bx * side, side)
    x_side = x_all[:, pl.ds(start, side)]
    thin = side // 8

    def place(matrix, lowest):
        for y in range(2):
            for z in range(4):
                first = thin * (4 * y + z)
                held[(y ^ by) * 4 + (z ^ zz), lowest : lowest + thin, :] = matrix[
                    first : first + thin
                ]

    for which, grad in enumerate((dq, dk, dv)):
        place(dot_tn(x_side, grad[:, :width]), thin * which)
        matrices[which] = dot_tn(x_all[:, wide:], grad[:, width:])
    place(dot_tn(context[:, :width], ag_all[:, pl.ds(start, side)]), 3 * thin)
    matrices[3] = dot_tn(ag_all[:, wide:], context[:, width:])
    left, right = matrices[2 * bx], matrices[2 * bx + 1]
    strip = left.shape[0] // 8
    for y in range(2):
        for z in range(4):
            first = strip * (4 * y + z)
            both = jnp.concatenate(
                [left[first : first + strip], right[first : first + strip]], axis=0
            )
            for slot in range(3):
                held[
                    (y ^ by) * 4 + (z ^ zz), 4 * thin : 4 * thin + 16, LANES * slot : LANES * (slot + 1)
                ] = both[16 * slot : 16 * slot + 16]
    for k in range(4):
        keep_out[k] = held[k]
        send_out[k] = held[4 + k].astype(BF)


def turned_layout(matrix):
    count = matrix.shape[0]
    fill = -count % LANES
    if fill:
        matrix = jnp.concatenate([matrix, jnp.zeros((fill, LANES), F32)], axis=0)
    return matrix.T[:, :count]


def pieces_of(refs, idx):
    for at in range(4):
        for group in range(2):
            for k in range(2):
                yield refs[2 * at + group], k, (idx[1] * 2 + idx[0]) ^ at, (2 * k + group) ^ idx[2]


def unpack_layout(piece, k, lowest, table, quarter, place):
    for slot in range(3):
        first = pl.multiple_of(place * 48 + 16 * slot, 16)
        table[quarter, pl.ds(first, 16), :] = piece[
            k, lowest : lowest + 16, LANES * slot : LANES * (slot + 1)
        ].astype(F32)


def up_result_kernel(idx, *refs):
    pieces, (out_t, out_l), (table,) = refs[:8], refs[8:10], refs[10:]
    rows, columns = out_t.shape[0] // 4, out_t.shape[1] // 4
    for piece, k, quarter, place in pieces_of(pieces, idx):
        out_t[
            pl.ds(pl.multiple_of(place * rows, rows), rows),
            pl.ds(pl.multiple_of(quarter * columns, columns), columns),
        ] = piece[k, :rows, :].astype(F32)
        unpack_layout(piece, k, rows, table, quarter, place)
    thin = out_l.shape[1] // 4
    for q in range(4):
        out_l[:, thin * q : thin * (q + 1)] = table[q][:, :thin]


def down_result_kernel(idx, *refs):
    pieces, (out_t, out_l), (table,) = refs[:8], refs[8:10], refs[10:]
    rows, columns = out_t.shape[0] // 16, out_t.shape[1] // 2
    for piece, k, quarter, place in pieces_of(pieces, idx):
        first = pl.multiple_of((quarter * 4 + place) * rows, rows)
        for side in range(2):
            out_t[pl.ds(first, rows), columns * side : columns * (side + 1)] = piece[
                k, rows * side : rows * (side + 1), :
            ].astype(F32)
        unpack_layout(piece, k, 2 * rows, table, quarter, place)
    thin = out_l.shape[0] // 4
    for q in range(4):
        out_l[thin * q : thin * (q + 1), :] = turned_layout(table[q])[:thin]


def attention_result_kernel(idx, *refs):
    pieces, (qkv_t, out_t, qkv_l, out_l), (table,) = refs[:8], refs[8:12], refs[12:]
    side = qkv_t.shape[1] // 2
    thin, strip = side // 8, qkv_l.shape[1] // 8
    for piece, k, quarter, place in pieces_of(pieces, idx):
        x, y = quarter & 1, quarter >> 1
        eighth = y * 4 + place
        first = pl.multiple_of(x * side + eighth * thin, 16)
        for which in range(3):
            qkv_t[which, pl.ds(first, thin), :] = piece[
                k, thin * which : thin * (which + 1), :
            ].astype(F32)
        out_t[
            pl.ds(pl.multiple_of(eighth * thin, 16), thin), pl.ds(pl.multiple_of(x * side, side), side)
        ] = piece[k, 3 * thin : 4 * thin, :].astype(F32)
        both = jnp.concatenate(
            [
                piece[k, 4 * thin : 4 * thin + 16, LANES * slot : LANES * (slot + 1)].astype(F32)
                for slot in range(3)
            ],
            axis=0,
        )
        for member in range(2):
            table[2 * x + member, pl.ds(pl.multiple_of(eighth * strip, 8), strip), :] = both[
                strip * member : strip * (member + 1)
            ]
    heads_l = qkv_l.shape[2]
    for which in range(3):
        qkv_l[which] = table[which][:, :heads_l]
    out_l[...] = turned_layout(table[3])[:heads_l]


def gathered(own):
    even = jnp.stack([own, exchange(own, 8)])
    odd = exchange(even, 4)
    even_x, odd_y = exchange(even, 1), exchange(odd, 2)
    even_y, odd_x = exchange(even, 2), exchange(odd, 1)
    even_xy, odd_xy = exchange(even_x, 2), exchange(odd_y, 1)
    return even, odd, even_x, odd_x, even_y, odd_y, even_xy, odd_xy


def reduced(keep, send):
    total = keep + exchange(send, 4).astype(F32)
    own = total[0] + exchange(total[1].astype(BF), 8).astype(F32)
    mask = 16
    while mask < lax.axis_size("seq"):
        own = own + exchange(own, mask)
        mask *= 2
    return own.astype(BF)


def per_device(
    text_in,
    layout_in,
    text_cot,
    layout_cot,
    doc_ids,
    span_ids,
    intersection_flags,
    text_qkv,
    text_qv_bias,
    text_out,
    text_out_bias,
    text_gains,
    text_shifts,
    text_up,
    text_up_bias,
    text_down,
    layout_qkv,
    layout_qv_bias,
    layout_out,
    layout_out_bias,
    layout_gains,
    layout_shifts,
    layout_up,
    layout_up_bias,
    layout_down,
):
    rows, wide = text_in.shape
    thin = layout_in.shape[1]
    whole = wide + thin
    width, width_l = text_qkv.shape[2], layout_qkv.shape[2]
    padded = width + LANES
    units, units_l = text_up.shape[1], layout_up.shape[1]
    half = rows // 2
    place = lax.axis_index("seq")
    idx = jnp.stack(
        [place & 1, (place >> 1) & 1, (place >> 2) & 3, lax.axis_index("tensor")]
    ).astype(jnp.int32)
    quarter = place & 3
    quarter_l = units_l // 4

    own_key = (doc_ids * 65536 + span_ids).astype(F32)[None, :]
    text_other, layout_other = exchange(text_in, 1), exchange(layout_in, 1)
    keys = jnp.concatenate([own_key, exchange(own_key, 1)], axis=1)
    keep_rows = (1 - intersection_flags).astype(F32)[:, None]
    bias_up_t, bias_up_l = text_up_bias[None, :], layout_up_bias[None, :]
    quarter_up_l = lax.dynamic_slice_in_dim(layout_up, quarter * quarter_l, quarter_l, 1)
    quarter_ub_l = lax.dynamic_slice_in_dim(bias_up_l, quarter * quarter_l, quarter_l, 1)

    qkv_weights = (text_qkv, text_qv_bias, layout_qkv, layout_qv_bias)
    q_own, k_own, v_own = call(
        project_kernel, [shape((rows, padded), BF)] * 3, text_in, layout_in, *qkv_weights
    )
    attended, k_all, v_all = call(
        attend_kernel,
        [shape((rows, whole), F32)] + [shape((2 * rows, padded), BF)] * 2,
        q_own, k_own, v_own, text_other, layout_other, *qkv_weights, keys, text_out, layout_out,
        scratch=[pltpu.VMEM((rows, padded), BF)],
    )
    hidden, normed, inverse, low_mine, low, slope_t, slope_l, ffn = call(
        forward_kernel,
        [
            shape((rows, whole), F32),
            shape((rows, whole), F32),
            shape((rows, 2 * LANES), F32),
            shape((half, whole), BF),
            shape((rows, whole), BF),
            shape((rows, units), F32),
            shape((rows, units_l), F32),
            shape((rows, whole), F32),
        ],
        idx, text_in, layout_in, attended, over_cores(attended), text_out_bias, layout_out_bias,
        text_gains, layout_gains, text_shifts, layout_shifts, text_up, bias_up_t, text_down,
        layout_up, bias_up_l, layout_down, smem=1, flops=14 * 10**8,
    )
    ffn_back = over_cores(ffn)
    low_far = [exchange(low_mine, mask) for mask in (1, 2, 3)]
    text_result, layout_result, second, grad_low, grad_mine, sums_two = call(
        second_norm_kernel,
        [
            shape((rows, wide), BF),
            shape((rows, thin), BF),
            shape((rows, whole), F32),
            shape((rows, whole), BF),
            shape((half, whole), BF),
            shape((3, whole), F32),
        ],
        idx, hidden, ffn, ffn_back, text_cot, layout_cot, keep_rows, text_out_bias, layout_out_bias,
        text_gains, layout_gains, text_shifts, layout_shifts, smem=1,
    )
    grad_far = [exchange(grad_mine, mask) for mask in (1, 2, 3)]
    hidden_part, bias_t, bias_l = call(
        ffn_back_kernel,
        [shape((rows, whole), F32), shape((1, units), F32), shape((1, units_l), F32)],
        grad_low, slope_t, slope_l, text_up, text_down, layout_up, layout_down, flops=14 * 10**8,
    )
    first, attended_grad, sums_one = call(
        first_norm_kernel,
        [shape((rows, whole), F32), shape((rows, whole), BF), shape((3, whole), F32)],
        second, hidden_part, over_cores(hidden_part), normed, inverse, text_gains, layout_gains,
    )
    attended_grad_other = exchange(attended_grad, 1)

    low_parts, grad_parts = [low], [grad_low]
    for low_one, grad_one in zip(low_far, grad_far):
        low_parts += [low_one, over_cores(low_one)]
        grad_parts += [grad_one, over_cores(grad_one)]
    block = (2, wide // 4 + 16, width)
    up_keep, up_send, down_keep, down_send = call(
        unit_grads_kernel,
        [shape(block, F32), shape(block, BF)] * 2,
        idx, *low_parts, *grad_parts, text_up, text_down, layout_down, bias_up_t, quarter_up_l,
        quarter_ub_l,
        scratch=[
            pltpu.VMEM((4 * rows, whole), BF),
            pltpu.VMEM((4 * rows, whole), BF),
            pltpu.VMEM((wide, units // 4), BF),
            pltpu.VMEM((units // 4, wide), BF),
            pltpu.VMEM((quarter_l, thin), BF),
            pltpu.VMEM((4,) + block[1:], F32),
            pltpu.SemaphoreType.DMA((17,)),
        ],
        smem=1, anys=range(1, 18), flops=24 * 10**8,
    )
    up_own = reduced(up_keep, up_send)
    down_own = reduced(down_keep, down_send)

    keep, send, input_part, small = call(
        attention_back_kernel,
        [
            shape((4,) + block[1:], F32),
            shape((4,) + block[1:], BF),
            shape((rows, whole), F32),
            shape((16, 1024), F32),
        ],
        idx, q_own, k_all, v_all, text_in, layout_in, text_other, layout_other, *qkv_weights, keys,
        text_out, layout_out, attended_grad, attended_grad_other, sums_two, sums_one, bias_t, bias_l,
        scratch=[
            pltpu.VMEM((2 * rows, padded), BF),
            pltpu.VMEM((2 * rows, padded), BF),
            pltpu.VMEM((2 * rows, whole), BF),
            pltpu.VMEM((2 * rows, whole), BF),
            pltpu.VMEM((2 * rows, padded), BF),
            pltpu.VMEM((2 * rows, padded), BF),
            pltpu.VMEM((2 * rows, padded), BF),
            pltpu.VMEM((2 * rows, padded), BF),
            pltpu.VMEM((4, thin, LANES), F32),
            pltpu.VMEM((8,) + block[1:], F32),
        ],
        smem=1, flops=50 * 10**8,
    )
    input_total = input_part + over_cores(input_part)
    text_in_grad = (first[:, :wide] + input_total[:, :wide]).astype(BF)
    layout_in_grad = (first[:, wide:] + input_total[:, wide:]).astype(BF)
    plane = keep + exchange(send, 2).astype(F32)
    attention_own = reduced(
        jnp.stack([plane[0], plane[2]]), jnp.stack([plane[1], plane[3]]).astype(BF)
    )
    mask = 1
    while mask < lax.axis_size("seq"):
        small = small + exchange(small, mask)
        mask *= 2

    up_t, up_l = call(
        up_result_kernel,
        [shape(text_up.shape, F32), shape(layout_up.shape, F32)],
        idx, *gathered(up_own), scratch=[pltpu.VMEM((4, thin, LANES), F32)], smem=1,
    )
    down_t, down_l = call(
        down_result_kernel,
        [shape(text_down.shape, F32), shape(layout_down.shape, F32)],
        idx, *gathered(down_own), scratch=[pltpu.VMEM((4, thin, LANES), F32)], smem=1,
    )
    qkv_t, out_t, qkv_l, out_l = call(
        attention_result_kernel,
        [
            shape(text_qkv.shape, F32),
            shape(text_out.shape, F32),
            shape(layout_qkv.shape, F32),
            shape(layout_out.shape, F32),
        ],
        idx, *gathered(attention_own), scratch=[pltpu.VMEM((4, thin, LANES), F32)], smem=1,
    )
    room = small.shape[1]

    def rows_of(one, two):
        both = jnp.stack([small[one, :whole], small[two, :whole]])
        return both[:, :wide], both[:, wide:]

    gains_t, gains_l = rows_of(3, 0)
    shifts_t, shifts_l = rows_of(4, 1)
    out_bias_t, out_bias_l = rows_of(5, 2)
    up_bias_t = jnp.concatenate([small[6], small[7, : units - room]])
    up_bias_l = small[8, :units_l]
    qv_t, qv_l = small[9:11, :width], small[9:11, width : width + width_l]
    return (
        text_result,
        layout_result,
        text_in_grad,
        layout_in_grad,
        qkv_t,
        qv_t,
        out_t,
        out_bias_t,
        gains_t,
        shifts_t,
        up_t,
        up_bias_t,
        down_t,
        qkv_l,
        qv_l,
        out_l,
        out_bias_l,
        gains_l,
        shifts_l,
        up_l,
        up_bias_l,
        down_l,
    )


def solution(mesh):
    rows, both, halves = P("seq", None), P(), P("tensor", None)
    stack, columns, one = P(None, None, "tensor"), P(None, "tensor"), P("tensor")
    weights_in = (stack, columns, halves, both, both, both, columns, one, halves)
    return jax.shard_map(
        per_device,
        mesh=mesh,
        in_specs=(rows,) * 4 + (P("seq"),) * 3 + weights_in * 2,
        out_specs=(rows,) * 4 + weights_in * 2,
        check_vma=False,
    )
```

```python
from functools import partial

import jax
import jax.numpy as jnp
from jax import lax
from jax.experimental import pallas as pl
from jax.experimental.pallas import tpu as pltpu
from jax.sharding import PartitionSpec as P

HT = 64
HL = 16
EPS = 1e-06
NEG = -1e30
BF = jnp.bfloat16
F32 = jnp.float32
LANES = 128


def exchange(shard, mask, axis="seq"):
    return lax.ppermute(shard, axis, [(i, i ^ mask) for i in range(lax.axis_size(axis))])


def over_cores(shard):
    return exchange(shard, 1, "tensor")


def dot(left, right):
    return lax.dot_general(left, right, (((1,), (0,)), ((), ())), preferred_element_type=F32)


def dot_nt(left, right):
    return lax.dot_general(left, right, (((1,), (1,)), ((), ())), preferred_element_type=F32)


def dot_tn(left, right):
    return lax.dot_general(left, right, (((0,), (0,)), ((), ())), preferred_element_type=F32)


def tied(shard, token):
    return lax.optimization_barrier((shard, token))[0]


def call(kernel, outs, *args, scratch=(), smem=0, anys=(), far=(), pin=(), after=(), flops=10**8, room=16):
    far, pin = list(far), list(pin)
    n_in = len(args)
    args = (*args, *after)
    specs, given = [], []
    for at, arg in enumerate(args):
        if at < smem:
            specs.append(pl.BlockSpec(memory_space=pltpu.SMEM))
        elif at in far:
            specs.append(pl.BlockSpec(memory_space=pltpu.HBM))
            arg = pltpu.with_memory_space_constraint(arg, pltpu.HBM)
        elif at in anys or at >= n_in:
            specs.append(pl.BlockSpec(memory_space=pl.ANY))
        else:
            specs.append(pl.BlockSpec(memory_space=pltpu.VMEM))
        if isinstance(arg, Near):
            arg = pltpu.with_memory_space_constraint(arg.value, pltpu.VMEM)
        given.append(arg)
    moved = sum(a.size * a.dtype.itemsize for a in args) + sum(
        o.size * o.dtype.itemsize for o in outs
    )
    stage = [pltpu.VMEM(args[k].shape, args[k].dtype) for k in far]
    if stage:
        stage.append(pltpu.SemaphoreType.DMA((len(far),)))

    def body(*refs):
        refs = list(refs[:n_in] + refs[len(args) :])
        if not stage:
            return kernel(*refs)
        held, sems = refs[-len(stage) : -1], refs[-1]
        refs = refs[: -len(stage)]
        coming = [
            pltpu.make_async_copy(refs[k], held[at], sems.at[at]) for at, k in enumerate(far)
        ]
        for copy in coming:
            copy.start()
        for copy in coming:
            copy.wait()
        for at, k in enumerate(far):
            refs[k] = held[at]
        kernel(*refs)

    found = pl.pallas_call(
        body,
        out_shape=tuple(
            pltpu.VMEM(o.shape, o.dtype) if k in pin else o for k, o in enumerate(outs)
        ),
        in_specs=specs,
        out_specs=tuple(pl.BlockSpec(memory_space=pltpu.VMEM) for _ in outs),
        scratch_shapes=list(scratch) + stage,
        compiler_params=pltpu.CompilerParams(vmem_limit_bytes=room * 1024 * 1024),
        cost_estimate=pl.CostEstimate(flops=flops, bytes_accessed=moved, transcendentals=0),
    )(*given)
    return tuple(Near(a) if k in pin else a for k, a in enumerate(found))


class Near:
    def __init__(self, value):
        self.value = value
        self.shape, self.dtype, self.size = value.shape, value.dtype, value.size


def shape(dims, dtype):
    return jax.ShapeDtypeStruct(tuple(dims), dtype)


def project_rows(text_rows, layout_columns, weight_t, bias_t, weight_l, bias_l, which, write):
    text_part = dot(text_rows, weight_t[which])
    layout_part = dot_tn(layout_columns, weight_l[which])
    if which != 1:
        row = which // 2
        text_part = text_part + bias_t[row : row + 1, :].astype(F32)
        layout_part = layout_part + bias_l[row : row + 1, :].astype(F32)
    pad = jnp.zeros((layout_part.shape[0], LANES - layout_part.shape[1]), F32)
    write(text_part.astype(BF), jnp.concatenate([layout_part, pad], axis=1).astype(BF))


def turned(matrix):
    rows, columns = matrix.shape
    matrix = matrix.astype(F32)
    if columns % LANES:
        fill = jnp.zeros((rows, -columns % LANES), F32)
        matrix = jnp.concatenate([matrix, fill], axis=1)
    if rows % LANES:
        fill = jnp.zeros((-rows % LANES, matrix.shape[1]), F32)
        matrix = jnp.concatenate([matrix, fill], axis=0)
    return matrix.T[:columns, :rows]


OB, GAIN, SHIFT, UP_T, UP_L, UP_Q = 0, 2, 4, 6, 7, 8


def pack_kernel(
    idx, cl, flags, ob_t, g_t, s_t, ub_t, ob_l, g_l, s_l, ub_l, up_l, dn_l,
    cl_out, keep_out, pack_out, quarter_out,
):
    wide, thin = ob_t.shape[1], ob_l.shape[1]
    pack_out[...] = jnp.zeros_like(pack_out)
    for first, text, layout in ((OB, ob_t, ob_l), (GAIN, g_t, g_l), (SHIFT, s_t, s_l)):
        pack_out[first : first + 2, :wide] = text[...].astype(F32)
        pack_out[first : first + 2, wide : wide + thin] = layout[...].astype(F32)
    pack_out[UP_T : UP_T + 1, :] = ub_t[...].astype(F32)
    pack_out[UP_L : UP_L + 1, : ub_l.shape[1]] = ub_l[...].astype(F32)
    quarter = idx[1] * 2 + idx[0]
    count = up_l.shape[1] // 4

    def cut(ref):
        value = ref[:, :count].astype(F32)
        for q in range(1, 4):
            value = jnp.where(quarter == q, ref[:, count * q : count * (q + 1)].astype(F32), value)
        return value

    pack_out[UP_Q : UP_Q + 1, :count] = cut(ub_l)
    quarter_out[:, :count] = cut(up_l).astype(BF)
    quarter_out[:, LANES : LANES + count] = cut(dn_l).astype(BF)
    cl_out[...] = turned(cl[...]).astype(BF)
    keep_out[...] = jnp.broadcast_to((1 - flags[...]).astype(F32), (LANES, flags.shape[1])).T


def project_kernel(xt, xl, wt, bt, wl, bl, q_out, k_out, v_out, xl_out):
    xl_out[...] = turned(xl[...]).astype(BF)
    width = wt.shape[2]
    for which, out in enumerate((q_out, k_out, v_out)):

        def write(text_part, layout_part, out=out):
            out[:, :width] = text_part
            out[:, width:] = layout_part

        project_rows(xt[...], xl[...], wt, bt, wl, bl, which, write)


def hidden_bias(keys, columns):
    rows = keys.shape[1]
    down = jnp.broadcast_to(keys, (LANES, rows)).T
    parts = [
        jnp.where(down == keys[:, at : at + LANES], 0.0, NEG).astype(F32)
        for at in range(0, columns, LANES)
    ]
    return jnp.concatenate(parts, axis=1)


def head_mask(member, head, text_value, layout_value, axis):
    dims = (1, 2 * LANES) if axis == 1 else (2 * LANES, 1)
    at = lax.broadcasted_iota(jnp.int32, dims, axis)
    text = (at >= member * HT) & (at < (member + 1) * HT)
    layout = (at >= LANES + head * HL) & (at < LANES + (head + 1) * HL)
    return jnp.where(text, text_value, jnp.where(layout, layout_value, 0.0)).astype(F32)


def pair_of(ref, pair, width):
    return jnp.concatenate([ref[:, LANES * pair : LANES * (pair + 1)], ref[:, width:]], axis=1)


def probabilities(key_pair, query_head, bias):
    scores = dot_nt(key_pair, query_head) + bias
    weights = jnp.exp(scores - jnp.max(scores, axis=0, keepdims=True))
    return weights * (1.0 / jnp.sum(weights, axis=0, keepdims=True))


OB, GAIN, SHIFT, UP_T, UP_L, UP_Q = 0, 2, 4, 6, 7, 8
SCALE_T = HT ** (-0.5)
SCALE_L = HL ** (-0.5)


def attend_kernel(
    q_own, k_own, v_own, xt, xl, wt, bt, wl, bl, keys, out_t, out_l, part_out, k_all, v_all, context,
):
    rows, width = q_own.shape[0], wt.shape[2]
    for which, own, target in ((1, k_own, k_all), (2, v_own, v_all)):
        target[:rows, :] = own[...]

        def write(text_part, layout_part, target=target):
            target[rows:, :width] = text_part
            target[rows:, width:] = layout_part

        project_rows(xt[...], xl[...], wt, bt, wl, bl, which, write)
    bias = hidden_bias(keys[...], rows)
    layout_sum = jnp.zeros((LANES, rows), F32)
    for pair in range(width // LANES):
        query_pair, key_pair = pair_of(q_own, pair, width), pair_of(k_all, pair, width)
        value_turned = pair_of(v_all, pair, width).T
        text_sum = jnp.zeros((LANES, rows), F32)
        for member in range(2):
            head = 2 * pair + member
            mask = head_mask(member, head, SCALE_T, SCALE_L, 1).astype(BF)
            probs_low = probabilities(key_pair, query_pair * mask, bias).astype(BF)
            turned = dot(value_turned, probs_low) * head_mask(member, head, 1.0, 1.0, 0)
            text_sum += turned[:LANES]
            layout_sum += turned[LANES:]
        context[:, LANES * pair : LANES * (pair + 1)] = text_sum.T.astype(BF)
    context[:, width:] = layout_sum.T.astype(BF)
    text_width = out_t.shape[1]
    part_out[:, :text_width] = dot(context[:, :width], out_t[...])
    part_out[:, text_width : text_width + out_l.shape[1]] = dot(
        context[:, width : width + out_l.shape[0]], out_l[...]
    )


def norm_parts(total):
    center = total - jnp.mean(total, axis=1, keepdims=True)
    inverse = lax.rsqrt(jnp.mean(center * center, axis=1, keepdims=True) + EPS)
    return center * inverse, inverse


def norm_back(upstream, normed, inverse, gain):
    scaled = upstream * gain
    return inverse * (
        scaled
        - jnp.mean(scaled, axis=1, keepdims=True)
        - normed * jnp.mean(scaled * normed, axis=1, keepdims=True)
    )


def gelu_parts(before):
    share = 0.5 * (1.0 + lax.erf(before * (0.5**0.5)))
    slope = share + before * (jnp.exp(-0.5 * before * before) * 0.3989422804014327)
    return before * share, slope


def norm_kernel(
    idx, xt, xl, part, back, pack, hidden_out, normed_out, inverse_out, mine_out, low_out
):
    width, whole, half = xt.shape[1], hidden_out.shape[1], mine_out.shape[0]
    for at, (lo, hi, x) in enumerate(((0, width, xt), (width, whole, xl))):
        total = x[...].astype(F32) + (part[:, lo:hi] + back[:, lo:hi]) + pack[OB : OB + 1, lo:hi]
        normed, inverse = norm_parts(total)
        hidden = normed * pack[GAIN : GAIN + 1, lo:hi] + pack[SHIFT : SHIFT + 1, lo:hi]
        hidden_out[:, lo:hi] = hidden
        normed_out[:, lo:hi] = normed
        inverse_out[:, LANES * at : LANES * (at + 1)] = jnp.broadcast_to(
            inverse, (inverse.shape[0], LANES)
        )
        low_out[:, lo:hi] = hidden.astype(BF)
    mine_out[...] = low_out[pl.ds(pl.multiple_of(idx[3] * half, half), half), :]


def ffn_kernel(low, pack, up_t, dn_t, up_l, dn_l, slope_t, slope_l, ffn_out):
    width = up_t.shape[0]
    whole = width + up_l.shape[0]
    for lo, hi, up, ub, dn, slope_out in (
        (0, width, up_t, UP_T, dn_t, slope_t),
        (width, whole, up_l, UP_L, dn_l, slope_l),
    ):
        rows_low = low[:, lo:hi]
        units = up.shape[1]
        step = min(units, 384)
        total = None
        for cut in range(0, units, step):
            before = dot(rows_low, up[:, cut : cut + step]) + pack[ub : ub + 1, cut : cut + step]
            activated, slope = gelu_parts(before)
            slope_out[:, cut : cut + step] = slope
            if lo == 0:
                term = dot(activated.astype(BF), dn[cut : cut + step, :])
            else:
                term = dot_nt(activated.astype(BF), dn[:, cut : cut + step])
            total = term if total is None else total + term
        ffn_out[:, lo:hi] = total


def second_norm_kernel(
    idx, hidden, part, back, ct, cl, keep, pack,
    rt_out, rl_out, second_out, low_out, mine_out, sums_out,
):
    width, whole = ct.shape[1], hidden.shape[1]
    half = mine_out.shape[0]
    for lo, hi, cot, result in ((0, width, ct, rt_out), (width, whole, cl, rl_out)):
        total = (
            hidden[:, lo:hi] + (part[:, lo:hi] + back[:, lo:hi]) + pack[OB + 1 : OB + 2, lo:hi]
        )
        normed, inverse = norm_parts(total)
        gain = pack[GAIN + 1 : GAIN + 2, lo:hi]
        value = normed * gain + pack[SHIFT + 1 : SHIFT + 2, lo:hi]
        result[...] = (value if lo == 0 else turned(value)).astype(BF)
        upstream = cot[...].astype(F32) * keep[:, :1]
        grad = norm_back(upstream, normed, inverse, gain)
        second_out[:, lo:hi] = grad
        low = grad.astype(BF)
        low_out[:, lo:hi] = low
        sums_out[0:1, lo:hi] = jnp.sum(upstream * normed, axis=0, keepdims=True)
        sums_out[1:2, lo:hi] = jnp.sum(upstream, axis=0, keepdims=True)
        sums_out[2:3, lo:hi] = jnp.sum(low.astype(F32), axis=0, keepdims=True)
    mine_out[...] = low_out[pl.ds(pl.multiple_of(idx[3] * half, half), half), :]


def ffn_back_kernel(grad, slope_t, slope_l, up_t, dn_t, up_l, dn_l, part_out, bias_t, bias_l):
    width = up_t.shape[0]
    whole = width + up_l.shape[0]
    for lo, hi, slope, up, dn, bias in (
        (0, width, slope_t, up_t, dn_t, bias_t),
        (width, whole, slope_l, up_l, dn_l, bias_l),
    ):
        rows = grad[:, lo:hi]
        units = up.shape[1]
        step = min(units, 384)
        total = None
        for cut in range(0, units, step):
            if lo == 0:
                act_grad = dot_nt(rows, dn[cut : cut + step, :])
            else:
                act_grad = dot(rows, dn[:, cut : cut + step])
            before_grad = (act_grad * slope[:, cut : cut + step]).astype(BF)
            bias[:, cut : cut + step] = jnp.sum(before_grad.astype(F32), axis=0, keepdims=True)
            term = dot_nt(before_grad, up[:, cut : cut + step])
            total = term if total is None else total + term
        part_out[:, lo:hi] = total


def pieces(columns, piece):
    return [(at, min(at + piece, columns)) for at in range(0, columns, piece)]


def first_norm_kernel(
    second, part, back, normed_in, inverse_in, pack, sums_two, bias_t, bias_l,
    first_out, low_out, small_out,
):
    whole, piece = second.shape[1], small_out.shape[1]
    width = whole * 4 // 5
    small_out[...] = jnp.zeros_like(small_out)
    row = 0

    def put(value):
        nonlocal row
        for lo, hi in pieces(value.shape[1], piece):
            small_out[row : row + 1, : hi - lo] = value[:, lo:hi]
            row += 1

    sums = [[], [], []]
    for at, (lo, hi) in enumerate(((0, width), (width, whole))):
        upstream = second[:, lo:hi] + (part[:, lo:hi] + back[:, lo:hi])
        normed = normed_in[:, lo:hi]
        inverse = inverse_in[:, LANES * at : LANES * at + 1]
        grad = norm_back(upstream, normed, inverse, pack[GAIN : GAIN + 1, lo:hi])
        first_out[:, lo:hi] = grad
        low = grad.astype(BF)
        low_out[:, lo:hi] = low
        sums[0].append(jnp.sum(upstream * normed, axis=0, keepdims=True))
        sums[1].append(jnp.sum(upstream, axis=0, keepdims=True))
        sums[2].append(jnp.sum(low.astype(F32), axis=0, keepdims=True))
    for kind in range(3):
        put(jnp.concatenate(sums[kind], axis=1))
        put(sums_two[kind : kind + 1, :])
    put(bias_t[...])
    put(bias_l[...])


def unit_grads_kernel(idx, *refs):
    (
        low_parts, grad_parts, (up_t, dn_t, quarters, pack_in),
        (up_keep, up_send, dn_keep, dn_send),
        (low, grad, w_up, w_dn, w_l, pack, held, sems),
    ) = refs[:5], refs[5:10], refs[10:14], refs[14:18], refs[18:]
    quarter = idx[1] * 2 + idx[0]
    zz = idx[2]
    copies = []
    for parts, target in ((low_parts, low), (grad_parts, grad)):
        at = 0
        for part in parts:
            count = part.shape[0]
            copies.append((part, target.at[pl.ds(at, count), :]))
            at += count
    units = w_dn.shape[0]
    start = pl.multiple_of(quarter * units, units)
    copies.append((up_t.at[:, pl.ds(start, units)], w_up))
    copies.append((dn_t.at[pl.ds(start, units), :], w_dn))
    copies += [(quarters, w_l), (pack_in, pack)]
    copies = [pltpu.make_async_copy(s, d, sems.at[k]) for k, (s, d) in enumerate(copies)]
    for c in copies:
        c.start()
    for c in copies:
        c.wait()
    width = w_up.shape[0]
    piece = width // 4
    slot_rows = 16

    def grads(lo, hi, up, bias, down):
        before = dot(low[:, lo:hi], up) + bias
        activated, slope = gelu_parts(before)
        act_grad = dot_nt(grad[:, lo:hi], down) if lo == 0 else dot(grad[:, lo:hi], down)
        before_grad = (act_grad * slope).astype(BF)
        return activated.astype(BF), before_grad

    whole = width + w_l.shape[0]
    count = w_l.shape[0] // 2
    act_t, back_t = grads(
        0, width, w_up[...], pack[UP_T : UP_T + 1, pl.ds(start, units)], w_dn[...]
    )
    act_l, back_l = grads(
        width,
        whole,
        w_l[:, :count],
        pack[UP_Q : UP_Q + 1, :count],
        w_l[:, LANES : LANES + count],
    )

    def place_layout(matrix):
        pad = jnp.zeros((matrix.shape[0], LANES - matrix.shape[1]), F32)
        padded = jnp.concatenate([matrix, pad], axis=1)
        for k in range(4):
            for slot in range(3):
                first = slot_rows * (3 * k + slot)
                held[k ^ zz, piece : piece + slot_rows, LANES * slot : LANES * (slot + 1)] = padded[
                    first : first + slot_rows
                ]

    def hand_out(keep, send):
        for at in range(2):
            keep[at] = held[2 * at]
            send[at] = held[2 * at + 1].astype(BF)

    up_grad = dot_tn(low[:, :width], back_t)
    for k in range(4):
        held[k ^ zz, :piece, :] = up_grad[piece * k : piece * (k + 1)]
    place_layout(dot_tn(low[:, width:whole], back_l))
    hand_out(up_keep, up_send)
    down_grad = dot_tn(act_t, grad[:, :width])
    part = piece // 2
    for k in range(4):
        for side in range(2):
            held[k ^ zz, part * side : part * (side + 1), :] = down_grad[
                part * k : part * (k + 1), units * side : units * (side + 1)
            ]
    place_layout(dot_tn(grad[:, width:whole], act_l))
    hand_out(dn_keep, dn_send)


def attention_back_kernel(
    k_all, v_all, xt, xl, xt_p, xl_p, wt, bt, wl, bl, keys, out_t, out_l, ag_own, ag_p,
    dq, dk, dv, context, q_all, g_all,
):
    rows, width = xt.shape[0], wt.shape[2]
    wide = out_t.shape[1]
    for at, text_rows, layout_columns in ((0, xt, xl), (rows, xt_p, xl_p)):

        def write(text_part, layout_part, at=at):
            q_all[at : at + rows, :width] = text_part
            q_all[at : at + rows, width:] = layout_part

        project_rows(text_rows[...], layout_columns[...], wt, bt, wl, bl, 0, write)
    for at, grad in ((0, ag_own), (rows, ag_p)):
        g_all[at : at + rows, :width] = dot_nt(grad[:, :wide], out_t[...]).astype(BF)
        layout_grad = dot_nt(grad[:, wide:], out_l[...])
        pad = jnp.zeros((rows, LANES - layout_grad.shape[1]), F32)
        g_all[at : at + rows, width:] = jnp.concatenate([layout_grad, pad], axis=1).astype(BF)
    bias = hidden_bias(keys[...], 2 * rows)
    zero_turned, zero = jnp.zeros((LANES, 2 * rows), F32), jnp.zeros((2 * rows, LANES), F32)
    layout_context, layout_dq, layout_dk, layout_dv = zero_turned, zero_turned, zero, zero
    for pair in range(width // LANES):
        query_pair, key_pair = pair_of(q_all, pair, width), pair_of(k_all, pair, width)
        grad_pair, value_pair = pair_of(g_all, pair, width), pair_of(v_all, pair, width)
        key_turned, value_turned = key_pair.T, value_pair.T
        text_context, text_dq, text_dk, text_dv = zero_turned, zero_turned, zero, zero
        for member in range(2):
            head = 2 * pair + member
            query_head = query_pair * head_mask(member, head, SCALE_T, SCALE_L, 1).astype(BF)
            grad_head = grad_pair * head_mask(member, head, 1.0, 1.0, 1).astype(BF)
            probs = probabilities(key_pair, query_head, bias)
            probs_low = probs.astype(BF)
            prob_grads = dot_nt(value_pair, grad_head)
            delta = jnp.sum(probs * prob_grads, axis=0, keepdims=True)
            score_grads = (probs * (prob_grads - delta)).astype(BF)
            value_part = dot(probs_low, grad_head)
            text_dv += value_part[:, :LANES]
            layout_dv += value_part[:, LANES:]
            key_part = dot(score_grads, query_head)
            text_dk += key_part[:, :LANES]
            layout_dk += key_part[:, LANES:]
            query_part = dot(key_turned, score_grads) * head_mask(member, head, SCALE_T, SCALE_L, 0)
            text_dq += query_part[:LANES]
            layout_dq += query_part[LANES:]
            context_part = dot(value_turned, probs_low) * head_mask(member, head, 1.0, 1.0, 0)
            text_context += context_part[:LANES]
            layout_context += context_part[LANES:]
        columns = slice(LANES * pair, LANES * (pair + 1))
        context[:, columns] = text_context.T.astype(BF)
        dq[:, columns] = text_dq.T.astype(BF)
        dk[:, columns] = text_dk.astype(BF)
        dv[:, columns] = text_dv.astype(BF)
    context[:, width:] = layout_context.T.astype(BF)
    dq[:, width:] = layout_dq.T.astype(BF)
    dk[:, width:] = layout_dk.astype(BF)
    dv[:, width:] = layout_dv.astype(BF)


def input_part_kernel(dq, dk, dv, wt, wl, part_out):
    rows, width, heads_l = part_out.shape[0], wt.shape[2], wl.shape[2]
    wide = wt.shape[1]
    total_t = total_l = None
    for which, grad in enumerate((dq, dk, dv)):
        term_t = dot_nt(grad[:rows, :width], wt[which])
        term_l = dot_nt(grad[:rows, width : width + heads_l], wl[which])
        total_t = term_t if which == 0 else total_t + term_t
        total_l = term_l if which == 0 else total_l + term_l
    part_out[:, :wide] = total_t
    part_out[:, wide : wide + wl.shape[1]] = total_l


def input_grad_kernel(first, part, back, text_out, layout_out):
    wide, whole = text_out.shape[1], first.shape[1]
    text_out[...] = (first[:, :wide] + (part[:, :wide] + back[:, :wide])).astype(BF)
    layout_out[...] = turned(
        first[:, wide:] + (part[:, wide:whole] + back[:, wide:whole])
    ).astype(BF)


def attention_grads_kernel(
    row, idx, dq, dk, dv, context, xt, xl, xt_p, xl_p, ag_own, ag_p, small, small_p,
    keep_out, send_out, matrices, held, sums,
):
    wide, rows = xt.shape[1], xt.shape[0]
    width = keep_out.shape[2]
    bx, by, zz = idx[0], idx[1], idx[2]
    side = wide // 2
    start = pl.multiple_of(bx * side, side)
    thin = side // 8

    def over_rows(left_own, left_other, right):
        both = jnp.concatenate([left_own, left_other], axis=0)
        return dot_tn(both, right)

    def place(matrix, lowest):
        for y in range(2):
            for z in range(4):
                first = thin * (4 * y + z)
                held[(y ^ by) * 4 + (z ^ zz), lowest : lowest + thin, :] = matrix[
                    first : first + thin
                ]

    x_side = jnp.concatenate([xt[:, pl.ds(start, side)], xt_p[:, pl.ds(start, side)]], axis=0)
    for which, grad in enumerate((dq, dk, dv)):
        place(dot_tn(x_side, grad[:, :width]), thin * which)
        matrices[which] = dot(xl[...], grad[:rows, width:]) + dot(xl_p[...], grad[rows:, width:])
    ag_side = jnp.concatenate([ag_own[:, pl.ds(start, side)], ag_p[:, pl.ds(start, side)]], axis=0)
    place(dot_tn(context[:, :width], ag_side), 3 * thin)
    ag_l = jnp.concatenate([ag_own[:, wide:], ag_p[:, wide:]], axis=0)
    matrices[3] = dot_tn(ag_l, context[:, width:])
    sums[...] = small[...] + small_p[...]
    for grad in (dq, dv):
        total = jnp.sum(grad[...].astype(F32), axis=0, keepdims=True)
        for lo, hi in pieces(total.shape[1], width):
            sums[row : row + 1, : hi - lo] = total[:, lo:hi]
            row += 1
    left, right = matrices[2 * bx], matrices[2 * bx + 1]
    strip = left.shape[0] // 8
    for y in range(2):
        for z in range(4):
            eighth = 4 * y + z
            first = strip * eighth
            both = jnp.concatenate(
                [left[first : first + strip], right[first : first + strip]], axis=0
            )[:, : width // 4]
            count = 2 * strip // 4
            packed = jnp.concatenate(
                [both[count * slot : count * (slot + 1)] for slot in range(4)], axis=1
            )
            rest = 16 - count
            held[(y ^ by) * 4 + (z ^ zz), 4 * thin : 4 * thin + 16, :] = jnp.concatenate(
                [packed, sums[rest * eighth : rest * (eighth + 1), :]], axis=0
            )
    for k in range(4):
        keep_out[k] = held[k]
        send_out[k] = held[4 + k].astype(BF)


def pieces_of(refs, idx):
    for at in range(4):
        for group in range(2):
            for k in range(2):
                yield refs[2 * at + group], k, (idx[1] * 2 + idx[0]) ^ at, (2 * k + group) ^ idx[2]


def unpack_layout(piece, k, lowest, table, quarter, place):
    for slot in range(3):
        first = pl.multiple_of(place * 48 + 16 * slot, 16)
        table[quarter, pl.ds(first, 16), :] = piece[
            k, lowest : lowest + 16, LANES * slot : LANES * (slot + 1)
        ].astype(F32)


def units_result_kernel(idx, *refs):
    parts, (up_t, up_l, dn_t, dn_l), (up_table, dn_table) = refs[:16], refs[16:20], refs[20:]
    rows, columns = up_t.shape[0] // 4, up_t.shape[1] // 4
    thin = up_l.shape[1] // 4
    half = rows // 2
    for at, piece in enumerate(parts):
        quarter, place = (idx[1] * 2 + idx[0]) ^ (at & 3), (at >> 2) ^ idx[2]
        up_t[
            pl.ds(pl.multiple_of(place * rows, rows), rows),
            pl.ds(pl.multiple_of(quarter * columns, columns), columns),
        ] = piece[0, :rows, :].astype(F32)
        unpack_layout(piece, 0, rows, up_table, quarter, place)
        first = pl.multiple_of((quarter * 4 + place) * half, half)
        for side in range(2):
            dn_t[pl.ds(first, half), columns * side : columns * (side + 1)] = piece[
                1, half * side : half * (side + 1), :
            ].astype(F32)
        unpack_layout(piece, 1, rows, dn_table, quarter, place)
    for q in range(4):
        up_l[:, thin * q : thin * (q + 1)] = up_table[q][:, :thin]
        dn_l[:, thin * q : thin * (q + 1)] = dn_table[q][:, :thin]


def attention_result_kernel(idx, *refs):
    parts, (qkv_t, out_t, qkv_l, out_l), refs = refs[:8], refs[8:12], refs[12:]
    (bt, gt, st, ubt, qvt, bl, gl, sl, ubl, qvl), (table, sums) = refs[:10], refs[10:]
    side = qkv_t.shape[1] // 2
    thin, strip, heads_l = side // 8, qkv_l.shape[1] // 8, qkv_l.shape[2]
    count = 2 * strip // 4
    rest = 16 - count
    for piece, k, quarter, place in pieces_of(parts, idx):
        x, y = quarter & 1, quarter >> 1
        eighth = y * 4 + place
        first = pl.multiple_of(x * side + eighth * thin, 16)
        for which in range(3):
            qkv_t[which, pl.ds(first, thin), :] = piece[
                k, thin * which : thin * (which + 1), :
            ].astype(F32)
        out_t[
            pl.ds(pl.multiple_of(eighth * thin, 16), thin), pl.ds(pl.multiple_of(x * side, side), side)
        ] = piece[k, 3 * thin : 4 * thin, :].astype(F32)
        last = piece[k, 4 * thin : 4 * thin + 16, :].astype(F32)
        both = jnp.concatenate(
            [last[:count, heads_l * slot : heads_l * (slot + 1)] for slot in range(4)], axis=0
        )
        for member in range(2):
            table[
                2 * x + member, pl.ds(pl.multiple_of(eighth * strip, 8), strip), :heads_l
            ] = both[strip * member : strip * (member + 1)]
        sums[x, eighth, :rest, :] = last[count:, :]
    for which in range(3):
        qkv_l[which] = table[which][:, :heads_l]
    out_l[...] = turned(table[3])[:heads_l]

    at = 0

    def take(columns):
        nonlocal at
        found = []
        for lo, hi in pieces(columns, sums.shape[3]):
            found.append(sums[0, at // rest, at % rest : at % rest + 1, : hi - lo])
            at += 1
        return jnp.concatenate(found, axis=1) if len(found) > 1 else found[0]

    wide, whole = gt.shape[1], gt.shape[1] + gl.shape[1]
    for text_out, layout_out in ((gt, gl), (st, sl), (bt, bl)):
        for row in range(2):
            value = take(whole)
            text_out[row : row + 1, :] = value[:, :wide]
            layout_out[row : row + 1, :] = value[:, wide:]
    ubt[...] = take(ubt.shape[1])
    ubl[...] = take(ubl.shape[1])
    for row in range(2):
        value = take(qvt.shape[1] + LANES)
        qvt[row : row + 1, :] = value[:, : qvt.shape[1]]
        qvl[row : row + 1, :] = value[:, qvt.shape[1] : qvt.shape[1] + qvl.shape[1]]


def gathered(own):
    even = jnp.stack([own, exchange(own, 8)])
    odd = exchange(even, 4)
    even_x, odd_y = exchange(even, 1), exchange(odd, 2)
    even_y, odd_x = exchange(even, 2), exchange(odd, 1)
    even_xy, odd_xy = exchange(even_x, 2), exchange(odd_y, 1)
    return even, odd, even_x, odd_x, even_y, odd_y, even_xy, odd_xy


def gathered_singly(own):
    found = {0: own, 4: exchange(own, 4), 8: exchange(own, 8)}
    found[12] = exchange(found[8], 4)
    for z, first, second in ((0, 1, 2), (4, 2, 1), (8, 1, 2), (12, 2, 1)):
        found[z + first] = exchange(found[z], first)
        found[z + second] = exchange(found[z], second)
        found[z + 3] = exchange(found[z + first], second)
    return [found[at] for at in range(16)]


def reduced(keep, far):
    total = keep + far.astype(F32)
    own = total[0] + exchange(total[1].astype(BF), 8).astype(F32)
    mask = 16
    while mask < lax.axis_size("seq"):
        own = own + exchange(own, mask)
        mask *= 2
    return own.astype(BF)


def per_device(
    text_in,
    layout_in,
    text_cot,
    layout_cot,
    doc_ids,
    span_ids,
    intersection_flags,
    text_qkv,
    text_qv_bias,
    text_out,
    text_out_bias,
    text_gains,
    text_shifts,
    text_up,
    text_up_bias,
    text_down,
    layout_qkv,
    layout_qv_bias,
    layout_out,
    layout_out_bias,
    layout_gains,
    layout_shifts,
    layout_up,
    layout_up_bias,
    layout_down,
):
    rows, wide = text_in.shape
    thin = layout_in.shape[1]
    whole = wide + thin
    width, width_l = text_qkv.shape[2], layout_qkv.shape[2]
    padded = width + LANES
    units, units_l = text_up.shape[1], layout_up.shape[1]
    half = rows // 2
    place = lax.axis_index("seq")
    idx = jnp.stack(
        [place & 1, (place >> 1) & 1, (place >> 2) & 3, lax.axis_index("tensor")]
    ).astype(jnp.int32)

    layout_turned, cot_turned, down_turned = layout_in.T, layout_cot.T, layout_down.T
    own_key = (doc_ids * 65536 + span_ids).astype(F32)[None, :]
    text_other, layout_other = exchange(text_in, 1), exchange(layout_turned, 1)
    keys = jnp.concatenate([own_key, exchange(own_key, 1)], axis=1)
    sent = shape((rows, wide + 2 * LANES), F32)

    cot_rows, keep_rows, pack, quarters = call(
        pack_kernel,
        [
            shape((rows, thin), BF),
            shape((rows, LANES), F32),
            shape((16, units), F32),
            shape((thin, 2 * LANES), BF),
        ],
        idx, cot_turned, intersection_flags[None, :], text_out_bias, text_gains, text_shifts,
        text_up_bias[None, :], layout_out_bias, layout_gains, layout_shifts,
        layout_up_bias[None, :], layout_up, down_turned, smem=1, far=range(1, 13), pin=range(4),
    )
    qkv_weights = (text_qkv, text_qv_bias, layout_qkv, layout_qv_bias)
    q_own, k_own, v_own, layout_rows = call(
        project_kernel,
        [shape((rows, padded), BF)] * 3 + [shape((rows, thin), BF)],
        text_in, layout_turned, *qkv_weights, pin=range(4),
    )
    attended, k_all, v_all = call(
        attend_kernel,
        [sent] + [shape((2 * rows, padded), BF)] * 2,
        q_own, k_own, v_own, text_other, layout_other, *qkv_weights, keys, text_out, layout_out,
        scratch=[pltpu.VMEM((rows, padded), BF)], pin=[1, 2],
    )
    hidden, normed, inverse, low_mine, low = call(
        norm_kernel,
        [
            shape((rows, whole), F32),
            shape((rows, whole), F32),
            shape((rows, 2 * LANES), F32),
            shape((half, wide + 2 * LANES), BF),
            shape((rows, wide + 2 * LANES), BF),
        ],
        idx, text_in, layout_rows, attended, over_cores(attended), pack, smem=1, pin=[0, 1, 2, 4],
    )
    slope_t, slope_l, ffn = call(
        ffn_kernel,
        [shape((rows, units), F32), shape((rows, units_l), F32), sent],
        low, pack, text_up, text_down, layout_up, down_turned, flops=14 * 10**8, room=20, pin=[0, 1],
    )
    ffn_back = over_cores(ffn)
    low_far = [exchange(low_mine, mask) for mask in (1, 2, 3)]
    text_result, layout_result, second, grad_low, grad_mine, sums_two = call(
        second_norm_kernel,
        [
            shape((rows, wide), BF),
            shape((thin, rows), BF),
            shape((rows, whole), F32),
            shape((rows, wide + 2 * LANES), BF),
            shape((half, wide + 2 * LANES), BF),
            shape((3, whole), F32),
        ],
        idx, hidden, ffn, ffn_back, text_cot, cot_rows, keep_rows, pack, smem=1, pin=[2, 3, 5],
    )
    grad_far = [exchange(grad_mine, mask) for mask in (1, 2, 3)]
    low_back = Near(over_cores(jnp.concatenate(low_far, axis=0)))
    hidden_part, bias_t, bias_l = call(
        ffn_back_kernel,
        [sent, shape((1, units), F32), shape((1, units_l), F32)],
        grad_low, slope_t, slope_l, text_up, text_down, layout_up, down_turned, flops=14 * 10**8,
        room=20, pin=[1, 2], after=[low_back],
    )
    first, attended_grad, small = call(
        first_norm_kernel,
        [shape((rows, whole), F32), shape((rows, whole), BF), shape((32, width), F32)],
        second, hidden_part, over_cores(hidden_part), normed, inverse, pack, sums_two, bias_t, bias_l, pin=[0],
    )
    attended_grad_other = exchange(attended_grad, 1)

    grad_cat = jnp.concatenate(grad_far, axis=0)
    low_parts = [low, *low_far, low_back]
    grad_parts = [grad_low, *grad_far, over_cores(tied(grad_cat, small))]
    block = (2, wide // 4 + 16, width)
    up_keep, up_send, down_keep, down_send = call(
        unit_grads_kernel,
        [shape(block, F32), shape(block, BF)] * 2,
        idx, *low_parts, *grad_parts, text_up, text_down, quarters, pack,
        scratch=[
            pltpu.VMEM((4 * rows, wide + 2 * LANES), BF),
            pltpu.VMEM((4 * rows, wide + 2 * LANES), BF),
            pltpu.VMEM((wide, units // 4), BF),
            pltpu.VMEM((units // 4, wide), BF),
            pltpu.VMEM((thin, 2 * LANES), BF),
            pltpu.VMEM((16, units), F32),
            pltpu.VMEM((4,) + block[1:], F32),
            pltpu.SemaphoreType.DMA((14,)),
        ],
        smem=1, anys=range(1, 15), flops=24 * 10**8, room=24,
    )
    up_far, down_far = exchange(up_send, 4), exchange(down_send, 4)
    small_other = exchange(tied(small, up_send), 1)

    dq, dk, dv, context = call(
        attention_back_kernel,
        [shape((2 * rows, padded), BF)] * 4,
        k_all, v_all, text_in, layout_turned, text_other, layout_other, *qkv_weights, keys, text_out,
        layout_out, attended_grad, attended_grad_other,
        scratch=[pltpu.VMEM((2 * rows, padded), BF)] * 2, flops=50 * 10**8, room=24, pin=range(4),
    )
    used = 6 * len(pieces(whole, width)) + len(pieces(units, width)) + len(pieces(units_l, width))
    keep, send = call(
        partial(attention_grads_kernel, used),
        [shape((4,) + block[1:], F32), shape((4,) + block[1:], BF)],
        idx, dq, dk, dv, context, text_in, layout_turned, text_other, layout_other, attended_grad,
        attended_grad_other, small, small_other,
        scratch=[
            pltpu.VMEM((4, thin, LANES), F32),
            pltpu.VMEM((8,) + block[1:], F32),
            pltpu.VMEM(small.shape, F32),
        ],
        smem=1, flops=10**9, room=24,
    )
    send_far = exchange(send, 2)
    up_own = reduced(up_keep, tied(up_far, keep))
    down_own = reduced(down_keep, tied(down_far, keep))
    (input_part,) = call(
        input_part_kernel, [sent], dq, dk, dv, text_qkv, layout_qkv, flops=5 * 10**8
    )
    text_in_grad, layout_in_grad = call(
        input_grad_kernel,
        [shape((rows, wide), BF), shape((thin, rows), BF)],
        first, input_part, over_cores(input_part),
    )
    plane = keep + send_far.astype(F32)
    attention_own = reduced(
        jnp.stack([plane[0], plane[2]]),
        exchange(jnp.stack([plane[1], plane[3]]).astype(BF), 4),
    )

    up_t, up_l, down_t, down_l = call(
        units_result_kernel,
        [shape(a.shape, F32) for a in (text_up, layout_up, text_down, down_turned)],
        idx, *gathered_singly(jnp.stack([up_own, down_own])), scratch=[pltpu.VMEM((4, thin, LANES), F32)] * 2, smem=1,
        room=32,
    )
    one_row = (1, units), (1, units_l)
    kinds = [text_out_bias.shape] * 3 + [one_row[0], text_qv_bias.shape]
    kinds += [layout_out_bias.shape] * 3 + [one_row[1], layout_qv_bias.shape]
    (
        qkv_t, out_t, qkv_l, out_l,
        out_bias_t, gains_t, shifts_t, ub_t, qv_t, out_bias_l, gains_l, shifts_l, ub_l, qv_l,
    ) = call(
        attention_result_kernel,
        [shape(a.shape, F32) for a in (text_qkv, text_out, layout_qkv, layout_out)]
        + [shape(dims, F32) for dims in kinds],
        idx, *gathered(attention_own),
        scratch=[pltpu.VMEM((4, thin, LANES), F32), pltpu.VMEM((2, 8, 8, width), F32)], smem=1,
    )
    return (
        text_result,
        layout_result.T,
        text_in_grad,
        layout_in_grad.T,
        qkv_t,
        qv_t,
        out_t,
        out_bias_t,
        gains_t,
        shifts_t,
        up_t,
        ub_t[0],
        down_t,
        qkv_l,
        qv_l,
        out_l,
        out_bias_l,
        gains_l,
        shifts_l,
        up_l,
        ub_l[0],
        down_l.T,
    )


def solution(mesh):
    rows, both, halves = P("seq", None), P(), P("tensor", None)
    stack, columns, one = P(None, None, "tensor"), P(None, "tensor"), P("tensor")
    weights_in = (stack, columns, halves, both, both, both, columns, one, halves)
    return jax.shard_map(
        per_device,
        mesh=mesh,
        in_specs=(rows,) * 4 + (P("seq"),) * 3 + weights_in * 2,
        out_specs=(rows,) * 4 + weights_in * 2,
        check_vma=False,
    )
```

```python
from functools import partial

import jax
import jax.numpy as jnp
from jax import lax
from jax.experimental import pallas as pl
from jax.experimental.pallas import tpu as pltpu
from jax.sharding import PartitionSpec as P

HT = 64
HL = 16
EPS = 1e-06
NEG = -1e30
BF = jnp.bfloat16
F32 = jnp.float32
LANES = 128


def exchange(shard, mask, axis="seq"):
    return lax.ppermute(shard, axis, [(i, i ^ mask) for i in range(lax.axis_size(axis))])


def over_cores(shard):
    return exchange(shard, 1, "tensor")


def dot(left, right):
    return lax.dot_general(left, right, (((1,), (0,)), ((), ())), preferred_element_type=F32)


def dot_nt(left, right):
    return lax.dot_general(left, right, (((1,), (1,)), ((), ())), preferred_element_type=F32)


def dot_tn(left, right):
    return lax.dot_general(left, right, (((0,), (0,)), ((), ())), preferred_element_type=F32)


def tied(shard, token):
    return lax.optimization_barrier((shard, token))[0]


def call(kernel, outs, *args, scratch=(), smem=0, anys=(), far=(), pin=(), after=(), flops=10**8, room=16):
    far, pin = list(far), list(pin)
    n_in = len(args)
    args = (*args, *after)
    specs, given = [], []
    for at, arg in enumerate(args):
        if at < smem:
            specs.append(pl.BlockSpec(memory_space=pltpu.SMEM))
        elif at in far:
            specs.append(pl.BlockSpec(memory_space=pltpu.HBM))
            arg = pltpu.with_memory_space_constraint(arg, pltpu.HBM)
        elif at in anys or at >= n_in:
            specs.append(pl.BlockSpec(memory_space=pl.ANY))
        else:
            specs.append(pl.BlockSpec(memory_space=pltpu.VMEM))
        if isinstance(arg, Near):
            arg = pltpu.with_memory_space_constraint(arg.value, pltpu.VMEM)
        given.append(arg)
    moved = sum(a.size * a.dtype.itemsize for a in args) + sum(
        o.size * o.dtype.itemsize for o in outs
    )
    stage = [pltpu.VMEM(args[k].shape, args[k].dtype) for k in far]
    if stage:
        stage.append(pltpu.SemaphoreType.DMA((len(far),)))

    def body(*refs):
        refs = list(refs[:n_in] + refs[len(args) :])
        if not stage:
            return kernel(*refs)
        held, sems = refs[-len(stage) : -1], refs[-1]
        refs = refs[: -len(stage)]
        coming = [
            pltpu.make_async_copy(refs[k], held[at], sems.at[at]) for at, k in enumerate(far)
        ]
        for copy in coming:
            copy.start()
        for copy in coming:
            copy.wait()
        for at, k in enumerate(far):
            refs[k] = held[at]
        kernel(*refs)

    found = pl.pallas_call(
        body,
        out_shape=tuple(
            pltpu.VMEM(o.shape, o.dtype) if k in pin else o for k, o in enumerate(outs)
        ),
        in_specs=specs,
        out_specs=tuple(pl.BlockSpec(memory_space=pltpu.VMEM) for _ in outs),
        scratch_shapes=list(scratch) + stage,
        compiler_params=pltpu.CompilerParams(vmem_limit_bytes=room * 1024 * 1024),
        cost_estimate=pl.CostEstimate(flops=flops, bytes_accessed=moved, transcendentals=0),
    )(*given)
    return tuple(Near(a) if k in pin else a for k, a in enumerate(found))


class Near:
    def __init__(self, value):
        self.value = value
        self.shape, self.dtype, self.size = value.shape, value.dtype, value.size


def shape(dims, dtype):
    return jax.ShapeDtypeStruct(tuple(dims), dtype)


def project_rows(text_rows, layout_columns, weight_t, bias_t, weight_l, bias_l, which, write):
    text_part = dot(text_rows, weight_t[which])
    layout_part = dot_tn(layout_columns, weight_l[which])
    if which != 1:
        row = which // 2
        text_part = text_part + bias_t[row : row + 1, :].astype(F32)
        layout_part = layout_part + bias_l[row : row + 1, :].astype(F32)
    pad = jnp.zeros((layout_part.shape[0], LANES - layout_part.shape[1]), F32)
    write(text_part.astype(BF), jnp.concatenate([layout_part, pad], axis=1).astype(BF))


def turned(matrix):
    rows, columns = matrix.shape
    matrix = matrix.astype(F32)
    if columns % LANES:
        fill = jnp.zeros((rows, -columns % LANES), F32)
        matrix = jnp.concatenate([matrix, fill], axis=1)
    if rows % LANES:
        fill = jnp.zeros((-rows % LANES, matrix.shape[1]), F32)
        matrix = jnp.concatenate([matrix, fill], axis=0)
    return matrix.T[:columns, :rows]


OB, GAIN, SHIFT, UP_T, UP_L, UP_Q = 0, 2, 4, 6, 7, 8


def pack_kernel(
    idx, cl, flags, ob_t, g_t, s_t, ub_t, ob_l, g_l, s_l, ub_l, up_l, dn_l,
    cl_out, keep_out, pack_out, quarter_out,
):
    wide, thin = ob_t.shape[1], ob_l.shape[1]
    pack_out[...] = jnp.zeros_like(pack_out)
    for first, text, layout in ((OB, ob_t, ob_l), (GAIN, g_t, g_l), (SHIFT, s_t, s_l)):
        pack_out[first : first + 2, :wide] = text[...].astype(F32)
        pack_out[first : first + 2, wide : wide + thin] = layout[...].astype(F32)
    pack_out[UP_T : UP_T + 1, :] = ub_t[...].astype(F32)[None, :]
    bias_l = ub_l[...].astype(F32)[None, :]
    pack_out[UP_L : UP_L + 1, : bias_l.shape[1]] = bias_l
    quarter = idx[1] * 2 + idx[0]
    count = up_l.shape[1] // 4

    def cut(ref):
        value = ref[:, :count].astype(F32)
        for q in range(1, 4):
            value = jnp.where(quarter == q, ref[:, count * q : count * (q + 1)].astype(F32), value)
        return value

    pack_out[UP_Q : UP_Q + 1, :count] = cut(bias_l)
    quarter_out[:, :count] = cut(up_l).astype(BF)
    quarter_out[:, LANES : LANES + count] = cut(dn_l).astype(BF)
    cl_out[...] = turned(cl[...]).astype(BF)
    keep_out[...] = jnp.broadcast_to((1 - flags[...]).astype(F32), (LANES, flags.shape[1])).T


def project_kernel(xt, xl, wt, bt, wl, bl, q_out, k_out, v_out, xl_out):
    xl_out[...] = turned(xl[...]).astype(BF)
    width = wt.shape[2]
    for which, out in enumerate((q_out, k_out, v_out)):

        def write(text_part, layout_part, out=out):
            out[:, :width] = text_part
            out[:, width:] = layout_part

        project_rows(xt[...], xl[...], wt, bt, wl, bl, which, write)


def hidden_bias(keys, columns):
    rows = keys.shape[1]
    down = jnp.broadcast_to(keys, (LANES, rows)).T
    parts = [
        jnp.where(down == keys[:, at : at + LANES], 0.0, NEG).astype(F32)
        for at in range(0, columns, LANES)
    ]
    return jnp.concatenate(parts, axis=1)


def head_mask(member, head, text_value, layout_value, axis):
    dims = (1, 2 * LANES) if axis == 1 else (2 * LANES, 1)
    at = lax.broadcasted_iota(jnp.int32, dims, axis)
    text = (at >= member * HT) & (at < (member + 1) * HT)
    layout = (at >= LANES + head * HL) & (at < LANES + (head + 1) * HL)
    return jnp.where(text, text_value, jnp.where(layout, layout_value, 0.0)).astype(F32)


def pair_of(ref, pair, width):
    return jnp.concatenate([ref[:, LANES * pair : LANES * (pair + 1)], ref[:, width:]], axis=1)


def probabilities(key_pair, query_head, bias):
    scores = dot_nt(key_pair, query_head) + bias
    weights = jnp.exp(scores - jnp.max(scores, axis=0, keepdims=True))
    return weights * (1.0 / jnp.sum(weights, axis=0, keepdims=True))


OB, GAIN, SHIFT, UP_T, UP_L, UP_Q = 0, 2, 4, 6, 7, 8
SCALE_T = HT ** (-0.5)
SCALE_L = HL ** (-0.5)


def attend_kernel(
    q_own, k_own, v_own, xt, xl, wt, bt, wl, bl, keys, out_t, out_l, part_out, k_all, v_all, context,
):
    rows, width = q_own.shape[0], wt.shape[2]
    for which, own, target in ((1, k_own, k_all), (2, v_own, v_all)):
        target[:rows, :] = own[...]

        def write(text_part, layout_part, target=target):
            target[rows:, :width] = text_part
            target[rows:, width:] = layout_part

        project_rows(xt[...], xl[...], wt, bt, wl, bl, which, write)
    bias = hidden_bias(keys[...], rows)
    layout_sum = jnp.zeros((LANES, rows), F32)
    for pair in range(width // LANES):
        query_pair, key_pair = pair_of(q_own, pair, width), pair_of(k_all, pair, width)
        value_turned = pair_of(v_all, pair, width).T
        text_sum = jnp.zeros((LANES, rows), F32)
        for member in range(2):
            head = 2 * pair + member
            mask = head_mask(member, head, SCALE_T, SCALE_L, 1).astype(BF)
            probs_low = probabilities(key_pair, query_pair * mask, bias).astype(BF)
            turned = dot(value_turned, probs_low) * head_mask(member, head, 1.0, 1.0, 0)
            text_sum += turned[:LANES]
            layout_sum += turned[LANES:]
        context[:, LANES * pair : LANES * (pair + 1)] = text_sum.T.astype(BF)
    context[:, width:] = layout_sum.T.astype(BF)
    text_width = out_t.shape[1]
    part_out[:, :text_width] = dot(context[:, :width], out_t[...])
    part_out[:, text_width : text_width + out_l.shape[1]] = dot(
        context[:, width : width + out_l.shape[0]], out_l[...]
    )


def norm_parts(total):
    center = total - jnp.mean(total, axis=1, keepdims=True)
    inverse = lax.rsqrt(jnp.mean(center * center, axis=1, keepdims=True) + EPS)
    return center * inverse, inverse


def norm_back(upstream, normed, inverse, gain):
    scaled = upstream * gain
    return inverse * (
        scaled
        - jnp.mean(scaled, axis=1, keepdims=True)
        - normed * jnp.mean(scaled * normed, axis=1, keepdims=True)
    )


def gelu_parts(before):
    share = 0.5 * (1.0 + lax.erf(before * (0.5**0.5)))
    slope = share + before * (jnp.exp(-0.5 * before * before) * 0.3989422804014327)
    return before * share, slope


def norm_kernel(
    idx, xt, xl, part, back, pack, hidden_out, normed_out, inverse_out, mine_out, low_out
):
    width, whole, half = xt.shape[1], hidden_out.shape[1], mine_out.shape[0]
    for at, (lo, hi, x) in enumerate(((0, width, xt), (width, whole, xl))):
        total = x[...].astype(F32) + (part[:, lo:hi] + back[:, lo:hi]) + pack[OB : OB + 1, lo:hi]
        normed, inverse = norm_parts(total)
        hidden = normed * pack[GAIN : GAIN + 1, lo:hi] + pack[SHIFT : SHIFT + 1, lo:hi]
        hidden_out[:, lo:hi] = hidden
        normed_out[:, lo:hi] = normed
        inverse_out[:, LANES * at : LANES * (at + 1)] = jnp.broadcast_to(
            inverse, (inverse.shape[0], LANES)
        )
        low_out[:, lo:hi] = hidden.astype(BF)
    mine_out[...] = low_out[pl.ds(pl.multiple_of(idx[3] * half, half), half), :]


def ffn_kernel(low, pack, up_t, dn_t, up_l, dn_l, slope_t, slope_l, ffn_out):
    width = up_t.shape[0]
    whole = width + up_l.shape[0]
    for lo, hi, up, ub, dn, slope_out in (
        (0, width, up_t, UP_T, dn_t, slope_t),
        (width, whole, up_l, UP_L, dn_l, slope_l),
    ):
        rows_low = low[:, lo:hi]
        units = up.shape[1]
        step = min(units, 384)
        total = None
        for cut in range(0, units, step):
            before = dot(rows_low, up[:, cut : cut + step]) + pack[ub : ub + 1, cut : cut + step]
            activated, slope = gelu_parts(before)
            slope_out[:, cut : cut + step] = slope
            if lo == 0:
                term = dot(activated.astype(BF), dn[cut : cut + step, :])
            else:
                term = dot_nt(activated.astype(BF), dn[:, cut : cut + step])
            total = term if total is None else total + term
        ffn_out[:, lo:hi] = total


def second_norm_kernel(
    idx, hidden, part, back, ct, cl, keep, pack,
    rt_out, rl_out, second_out, low_out, mine_out, sums_out,
):
    width, whole = ct.shape[1], hidden.shape[1]
    half = mine_out.shape[0]
    for lo, hi, cot, result in ((0, width, ct, rt_out), (width, whole, cl, rl_out)):
        total = (
            hidden[:, lo:hi] + (part[:, lo:hi] + back[:, lo:hi]) + pack[OB + 1 : OB + 2, lo:hi]
        )
        normed, inverse = norm_parts(total)
        gain = pack[GAIN + 1 : GAIN + 2, lo:hi]
        value = normed * gain + pack[SHIFT + 1 : SHIFT + 2, lo:hi]
        result[...] = (value if lo == 0 else turned(value)).astype(BF)
        upstream = cot[...].astype(F32) * keep[:, :1]
        grad = norm_back(upstream, normed, inverse, gain)
        second_out[:, lo:hi] = grad
        low = grad.astype(BF)
        low_out[:, lo:hi] = low
        sums_out[0:1, lo:hi] = jnp.sum(upstream * normed, axis=0, keepdims=True)
        sums_out[1:2, lo:hi] = jnp.sum(upstream, axis=0, keepdims=True)
        sums_out[2:3, lo:hi] = jnp.sum(low.astype(F32), axis=0, keepdims=True)
    mine_out[...] = low_out[pl.ds(pl.multiple_of(idx[3] * half, half), half), :]


def ffn_back_kernel(grad, slope_t, slope_l, up_t, dn_t, up_l, dn_l, part_out, bias_t, bias_l):
    width = up_t.shape[0]
    whole = width + up_l.shape[0]
    for lo, hi, slope, up, dn, bias in (
        (0, width, slope_t, up_t, dn_t, bias_t),
        (width, whole, slope_l, up_l, dn_l, bias_l),
    ):
        rows = grad[:, lo:hi]
        units = up.shape[1]
        step = min(units, 384)
        total = None
        for cut in range(0, units, step):
            if lo == 0:
                act_grad = dot_nt(rows, dn[cut : cut + step, :])
            else:
                act_grad = dot(rows, dn[:, cut : cut + step])
            before_grad = (act_grad * slope[:, cut : cut + step]).astype(BF)
            bias[:, cut : cut + step] = jnp.sum(before_grad.astype(F32), axis=0, keepdims=True)
            term = dot_nt(before_grad, up[:, cut : cut + step])
            total = term if total is None else total + term
        part_out[:, lo:hi] = total


def turning_kernel(
    idx, hidden, part, back, ct, cl, keep, pack, slope_t, slope_l, up_t, dn_t, up_l, dn_l,
    rt_out, rl_out, second_out, low_out, mine_out, sums_out, part_out, bias_t, bias_l,
):
    second_norm_kernel(
        idx, hidden, part, back, ct, cl, keep, pack,
        rt_out, rl_out, second_out, low_out, mine_out, sums_out,
    )
    ffn_back_kernel(
        low_out, slope_t, slope_l, up_t, dn_t, up_l, dn_l, part_out, bias_t, bias_l
    )


def pieces(columns, piece):
    return [(at, min(at + piece, columns)) for at in range(0, columns, piece)]


def first_norm_kernel(
    idx, second, part, back, normed_in, inverse_in, pack, sums_two, bias_t, bias_l,
    first_out, low_out, mine_out, small_out,
):
    whole, piece = second.shape[1], small_out.shape[1]
    width = whole * 4 // 5
    small_out[...] = jnp.zeros_like(small_out)
    row = 0

    def put(value):
        nonlocal row
        for lo, hi in pieces(value.shape[1], piece):
            small_out[row : row + 1, : hi - lo] = value[:, lo:hi]
            row += 1

    sums = [[], [], []]
    for at, (lo, hi) in enumerate(((0, width), (width, whole))):
        upstream = second[:, lo:hi] + (part[:, lo:hi] + back[:, lo:hi])
        normed = normed_in[:, lo:hi]
        inverse = inverse_in[:, LANES * at : LANES * at + 1]
        grad = norm_back(upstream, normed, inverse, pack[GAIN : GAIN + 1, lo:hi])
        first_out[:, lo:hi] = grad
        low = grad.astype(BF)
        low_out[:, lo:hi] = low
        sums[0].append(jnp.sum(upstream * normed, axis=0, keepdims=True))
        sums[1].append(jnp.sum(upstream, axis=0, keepdims=True))
        sums[2].append(jnp.sum(low.astype(F32), axis=0, keepdims=True))
    half = mine_out.shape[0]
    mine_out[...] = low_out[pl.ds(pl.multiple_of(idx[3] * half, half), half), :]
    for kind in range(3):
        put(jnp.concatenate(sums[kind], axis=1))
        put(sums_two[kind : kind + 1, :])
    put(bias_t[...])
    put(bias_l[...])


def unit_grads_kernel(idx, *refs):
    (
        low_parts, grad_parts, (up_t, dn_t, quarters, pack_in),
        (keep, send, act_out, grad),
        (low, w_up, w_dn, w_l, pack, held, sems),
    ) = refs[:5], refs[5:10], refs[10:14], refs[14:18], refs[18:]
    quarter = idx[1] * 2 + idx[0]
    zz = idx[2]
    copies = []
    for parts, target in ((low_parts, low), (grad_parts, grad)):
        at = 0
        for part in parts:
            count = part.shape[0]
            copies.append((part, target.at[pl.ds(at, count), :]))
            at += count
    units = w_dn.shape[0]
    start = pl.multiple_of(quarter * units, units)
    copies.append((up_t.at[:, pl.ds(start, units)], w_up))
    copies.append((dn_t.at[pl.ds(start, units), :], w_dn))
    copies += [(quarters, w_l), (pack_in, pack)]
    copies = [pltpu.make_async_copy(s, d, sems.at[k]) for k, (s, d) in enumerate(copies)]
    for c in copies:
        c.start()
    for c in copies:
        c.wait()
    width = w_up.shape[0]
    piece = width // 4

    def grads(lo, hi, up, bias, down):
        before = dot(low[:, lo:hi], up) + bias
        activated, slope = gelu_parts(before)
        act_grad = dot_nt(grad[:, lo:hi], down) if lo == 0 else dot(grad[:, lo:hi], down)
        before_grad = (act_grad * slope).astype(BF)
        return activated.astype(BF), before_grad

    whole = width + w_l.shape[0]
    count = w_l.shape[0] // 2
    act_t, back_t = grads(
        0, width, w_up[...], pack[UP_T : UP_T + 1, pl.ds(start, units)], w_dn[...]
    )
    act_l, back_l = grads(
        width,
        whole,
        w_l[:, :count],
        pack[UP_Q : UP_Q + 1, :count],
        w_l[:, LANES : LANES + count],
    )

    act_out[:, :units] = act_t
    act_out[:, units:] = widened(act_l)
    up_grad = dot_tn(low[:, :width], back_t)
    for k in range(4):
        held[k ^ zz, :piece, :] = up_grad[piece * k : piece * (k + 1)]
    place_layout(held, zz, dot_tn(low[:, width:whole], widened(back_l)))
    hand_out(held, keep, send)


def widened(matrix):
    pad = jnp.zeros((matrix.shape[0], LANES - matrix.shape[1]), matrix.dtype)
    return jnp.concatenate([matrix, pad], axis=1)


def place_layout(held, zz, matrix):
    piece = held.shape[1] - 16
    for k in range(4):
        for slot in range(3):
            first = 16 * (3 * k + slot)
            held[k ^ zz, piece:, LANES * slot : LANES * (slot + 1)] = matrix[first : first + 16]


def hand_out(held, keep, send):
    for k in range(2):
        keep[k] = held[2 * k]
        send[k] = held[2 * k + 1].astype(BF)


def down_grads_kernel(idx, act, grad, keep, send, held):
    zz = idx[2]
    units, width = held.shape[2], 2 * held.shape[2]
    down_grad = dot_tn(act[:, :units], grad[:, :width])
    part = (held.shape[1] - 16) // 2
    for k in range(4):
        for side in range(2):
            held[k ^ zz, part * side : part * (side + 1), :] = down_grad[
                part * k : part * (k + 1), units * side : units * (side + 1)
            ]
    place_layout(held, zz, dot_tn(grad[:, width : width + width // 4], act[:, units:]))
    hand_out(held, keep, send)


def attention_back_kernel(
    idx, k_all, v_all, xt, xl, xt_p, xl_p, wt, bt, wl, bl, keys, out_t, out_l, ag_own, ag_far, ag_back,
    dq, dk, dv, context, ag_p, q_all, g_all,
):
    rows, width = xt.shape[0], wt.shape[2]
    wide = out_t.shape[1]
    half = ag_far.shape[0]
    core = idx[3]
    ag_p[pl.ds(pl.multiple_of(core * half, half), half), :] = ag_far[...]
    ag_p[pl.ds(pl.multiple_of((1 - core) * half, half), half), :] = ag_back[...]
    for at, text_rows, layout_columns in ((0, xt, xl), (rows, xt_p, xl_p)):

        def write(text_part, layout_part, at=at):
            q_all[at : at + rows, :width] = text_part
            q_all[at : at + rows, width:] = layout_part

        project_rows(text_rows[...], layout_columns[...], wt, bt, wl, bl, 0, write)
    for at, grad in ((0, ag_own), (rows, ag_p)):
        g_all[at : at + rows, :width] = dot_nt(grad[:, :wide], out_t[...]).astype(BF)
        layout_grad = dot_nt(grad[:, wide:], out_l[...])
        pad = jnp.zeros((rows, LANES - layout_grad.shape[1]), F32)
        g_all[at : at + rows, width:] = jnp.concatenate([layout_grad, pad], axis=1).astype(BF)
    bias = hidden_bias(keys[...], 2 * rows)
    zero_turned, zero = jnp.zeros((LANES, 2 * rows), F32), jnp.zeros((2 * rows, LANES), F32)
    layout_context, layout_dq, layout_dk, layout_dv = zero_turned, zero_turned, zero, zero
    for pair in range(width // LANES):
        query_pair, key_pair = pair_of(q_all, pair, width), pair_of(k_all, pair, width)
        grad_pair, value_pair = pair_of(g_all, pair, width), pair_of(v_all, pair, width)
        key_turned, value_turned = key_pair.T, value_pair.T
        text_context, text_dq, text_dk, text_dv = zero_turned, zero_turned, zero, zero
        for member in range(2):
            head = 2 * pair + member
            query_head = query_pair * head_mask(member, head, SCALE_T, SCALE_L, 1).astype(BF)
            grad_head = grad_pair * head_mask(member, head, 1.0, 1.0, 1).astype(BF)
            probs = probabilities(key_pair, query_head, bias)
            probs_low = probs.astype(BF)
            prob_grads = dot_nt(value_pair, grad_head)
            delta = jnp.sum(probs * prob_grads, axis=0, keepdims=True)
            score_grads = (probs * (prob_grads - delta)).astype(BF)
            value_part = dot(probs_low, grad_head)
            text_dv += value_part[:, :LANES]
            layout_dv += value_part[:, LANES:]
            key_part = dot(score_grads, query_head)
            text_dk += key_part[:, :LANES]
            layout_dk += key_part[:, LANES:]
            query_part = dot(key_turned, score_grads) * head_mask(member, head, SCALE_T, SCALE_L, 0)
            text_dq += query_part[:LANES]
            layout_dq += query_part[LANES:]
            context_part = dot(value_turned, probs_low) * head_mask(member, head, 1.0, 1.0, 0)
            text_context += context_part[:LANES]
            layout_context += context_part[LANES:]
        columns = slice(LANES * pair, LANES * (pair + 1))
        context[:, columns] = text_context.T.astype(BF)
        dq[:, columns] = text_dq.T.astype(BF)
        dk[:, columns] = text_dk.astype(BF)
        dv[:, columns] = text_dv.astype(BF)
    context[:, width:] = layout_context.T.astype(BF)
    dq[:, width:] = layout_dq.T.astype(BF)
    dk[:, width:] = layout_dk.astype(BF)
    dv[:, width:] = layout_dv.astype(BF)


def input_part_kernel(dq, dk, dv, wt, wl, part_out):
    rows, width, heads_l = part_out.shape[0], wt.shape[2], wl.shape[2]
    wide = wt.shape[1]
    total_t = total_l = None
    for which, grad in enumerate((dq, dk, dv)):
        term_t = dot_nt(grad[:rows, :width], wt[which])
        term_l = dot_nt(grad[:rows, width : width + heads_l], wl[which])
        total_t = term_t if which == 0 else total_t + term_t
        total_l = term_l if which == 0 else total_l + term_l
    part_out[:, :wide] = total_t
    part_out[:, wide : wide + wl.shape[1]] = total_l


def input_grad_kernel(first, part, back, text_out, layout_out):
    wide, whole = text_out.shape[1], first.shape[1]
    text_out[...] = (first[:, :wide] + (part[:, :wide] + back[:, :wide])).astype(BF)
    layout_out[...] = turned(
        first[:, wide:] + (part[:, wide:whole] + back[:, wide:whole])
    ).astype(BF)


def attention_grads_kernel(
    row, idx, dq, dk, dv, context, xt, xl, xt_p, xl_p, ag_own, ag_p, small, small_p,
    keep_out, send_out, matrices, held, sums,
):
    wide, rows = xt.shape[1], xt.shape[0]
    width = keep_out.shape[2]
    bx, by, zz = idx[0], idx[1], idx[2]
    side = wide // 2
    start = pl.multiple_of(bx * side, side)
    thin = side // 8

    def over_rows(left_own, left_other, right):
        both = jnp.concatenate([left_own, left_other], axis=0)
        return dot_tn(both, right)

    def place(matrix, lowest):
        for y in range(2):
            for z in range(4):
                first = thin * (4 * y + z)
                held[(y ^ by) * 4 + (z ^ zz), lowest : lowest + thin, :] = matrix[
                    first : first + thin
                ]

    x_side = jnp.concatenate([xt[:, pl.ds(start, side)], xt_p[:, pl.ds(start, side)]], axis=0)
    for which, grad in enumerate((dq, dk, dv)):
        place(dot_tn(x_side, grad[:, :width]), thin * which)
        matrices[which] = dot(xl[...], grad[:rows, width:]) + dot(xl_p[...], grad[rows:, width:])
    ag_side = jnp.concatenate([ag_own[:, pl.ds(start, side)], ag_p[:, pl.ds(start, side)]], axis=0)
    place(dot_tn(context[:, :width], ag_side), 3 * thin)
    ag_l = jnp.concatenate([ag_own[:, wide:], ag_p[:, wide:]], axis=0)
    matrices[3] = dot_tn(ag_l, context[:, width:])
    sums[...] = small[...] + small_p[...]
    for grad in (dq, dv):
        total = jnp.sum(grad[...].astype(F32), axis=0, keepdims=True)
        for lo, hi in pieces(total.shape[1], width):
            sums[row : row + 1, : hi - lo] = total[:, lo:hi]
            row += 1
    left, right = matrices[2 * bx], matrices[2 * bx + 1]
    strip = left.shape[0] // 8
    for y in range(2):
        for z in range(4):
            eighth = 4 * y + z
            first = strip * eighth
            both = jnp.concatenate(
                [left[first : first + strip], right[first : first + strip]], axis=0
            )[:, : width // 4]
            count = 2 * strip // 4
            packed = jnp.concatenate(
                [both[count * slot : count * (slot + 1)] for slot in range(4)], axis=1
            )
            rest = 16 - count
            held[(y ^ by) * 4 + (z ^ zz), 4 * thin : 4 * thin + 16, :] = jnp.concatenate(
                [packed, sums[rest * eighth : rest * (eighth + 1), :]], axis=0
            )
    for at, k in enumerate((0, 2, 1, 3)):
        keep_out[at] = held[k]
        send_out[at] = held[4 + k].astype(BF)


def pieces_of(refs, idx):
    for at in range(4):
        for group in range(2):
            for k in range(2):
                yield refs[2 * at + group], k, (idx[1] * 2 + idx[0]) ^ at, (2 * k + group) ^ idx[2]


def unpack_layout(piece, k, lowest, table, quarter, place):
    for slot in range(3):
        first = pl.multiple_of(place * 48 + 16 * slot, 16)
        table[quarter, pl.ds(first, 16), :] = piece[
            k, lowest : lowest + 16, LANES * slot : LANES * (slot + 1)
        ].astype(F32)


def units_result_kernel(idx, *refs):
    parts, (up_t, up_l, dn_t, dn_l), (up_table, dn_table) = refs[:16], refs[16:20], refs[20:]
    rows, columns = up_t.shape[0] // 4, up_t.shape[1] // 4
    thin = up_l.shape[1] // 4
    half = rows // 2
    for at, piece in enumerate(parts):
        quarter, place = (idx[1] * 2 + idx[0]) ^ (at & 3), (at >> 2) ^ idx[2]
        up_t[
            pl.ds(pl.multiple_of(place * rows, rows), rows),
            pl.ds(pl.multiple_of(quarter * columns, columns), columns),
        ] = piece[0, :rows, :].astype(F32)
        unpack_layout(piece, 0, rows, up_table, quarter, place)
        first = pl.multiple_of((quarter * 4 + place) * half, half)
        for side in range(2):
            dn_t[pl.ds(first, half), columns * side : columns * (side + 1)] = piece[
                1, half * side : half * (side + 1), :
            ].astype(F32)
        unpack_layout(piece, 1, rows, dn_table, quarter, place)
    for q in range(4):
        up_l[:, thin * q : thin * (q + 1)] = up_table[q][:, :thin]
        dn_l[:, thin * q : thin * (q + 1)] = dn_table[q][:, :thin]


def attention_result_kernel(idx, *refs):
    parts, (qkv_t, out_t, qkv_l, out_l), refs = refs[:8], refs[8:12], refs[12:]
    (bt, gt, st, ubt, qvt, bl, gl, sl, ubl, qvl), (table, sums) = refs[:10], refs[10:]
    side = qkv_t.shape[1] // 2
    thin, strip, heads_l = side // 8, qkv_l.shape[1] // 8, qkv_l.shape[2]
    count = 2 * strip // 4
    rest = 16 - count
    for piece, k, quarter, place in pieces_of(parts, idx):
        x, y = quarter & 1, quarter >> 1
        eighth = y * 4 + place
        first = pl.multiple_of(x * side + eighth * thin, 16)
        for which in range(3):
            qkv_t[which, pl.ds(first, thin), :] = piece[
                k, thin * which : thin * (which + 1), :
            ].astype(F32)
        out_t[
            pl.ds(pl.multiple_of(eighth * thin, 16), thin), pl.ds(pl.multiple_of(x * side, side), side)
        ] = piece[k, 3 * thin : 4 * thin, :].astype(F32)
        last = piece[k, 4 * thin : 4 * thin + 16, :].astype(F32)
        both = jnp.concatenate(
            [last[:count, heads_l * slot : heads_l * (slot + 1)] for slot in range(4)], axis=0
        )
        for member in range(2):
            table[
                2 * x + member, pl.ds(pl.multiple_of(eighth * strip, 8), strip), :heads_l
            ] = both[strip * member : strip * (member + 1)]
        sums[x, eighth, :rest, :] = last[count:, :]
    for which in range(3):
        qkv_l[which] = table[which][:, :heads_l]
    out_l[...] = turned(table[3])[:heads_l]

    at = 0

    def take(columns):
        nonlocal at
        found = []
        for lo, hi in pieces(columns, sums.shape[3]):
            found.append(sums[0, at // rest, at % rest : at % rest + 1, : hi - lo])
            at += 1
        return jnp.concatenate(found, axis=1) if len(found) > 1 else found[0]

    wide, whole = gt.shape[1], gt.shape[1] + gl.shape[1]
    for text_out, layout_out in ((gt, gl), (st, sl), (bt, bl)):
        for row in range(2):
            value = take(whole)
            text_out[row : row + 1, :] = value[:, :wide]
            layout_out[row : row + 1, :] = value[:, wide:]
    ubt[...] = take(ubt.shape[0])[0]
    ubl[...] = take(ubl.shape[0])[0]
    for row in range(2):
        value = take(qvt.shape[1] + LANES)
        qvt[row : row + 1, :] = value[:, : qvt.shape[1]]
        qvl[row : row + 1, :] = value[:, qvt.shape[1] : qvt.shape[1] + qvl.shape[1]]


ORDER = (
    "down4", "up8", "down8", "y", 4, 1, 8, "z4", 6, 5, 2, 10, "z8", 9, 3, 12, 7, "even", 11, 13, 14,
    "odd", "even1", "even2", "odd2", 15, "odd1", "even3", "odd3",
)


def reduced_and_gathered(token, up, up_far, down_keep, down_far, keep, far):
    last = token
    coming, found = {"up8": up_far, "down4": down_far, "y": far}, {}

    def send(shard, mask, name):
        coming[name] = exchange(shard, mask)

    def beyond(own):
        mask = 16
        while mask < lax.axis_size("seq"):
            own = own + exchange(own, mask)
            mask *= 2
        return own.astype(BF)

    for name in ORDER:
        last = found[name] = tied(coming[name], last)
        if name == "down4":
            down = down_keep + last.astype(F32)
            send(down[1].astype(BF), 8, "down8")
        elif name == "down8":
            up_own = beyond(up + found["up8"].astype(F32))
            found[0] = jnp.stack([up_own, beyond(down[0] + last.astype(F32))])
            for mask in (4, 1, 8, 2):
                send(found[0], mask, mask)
        elif name == "y":
            total = keep + last.astype(F32)
            send(total[2:].astype(BF), 4, "z4")
        elif name == "z4":
            total = total[:2] + last.astype(F32)
            send(total[1].astype(BF), 8, "z8")
        elif name == "z8":
            own = beyond(total[0] + last.astype(F32))
            send(own, 8, "even")
        elif name == "even":
            found["even"] = jnp.stack([own, last])
            for mask, to in ((4, "odd"), (1, "even1"), (2, "even2")):
                send(found["even"], mask, to)
        elif name == "odd":
            for mask in (1, 2):
                send(last, mask, f"odd{mask}")
        elif name == "even1":
            send(last, 2, "even3")
        elif name == "odd2":
            send(last, 1, "odd3")
        elif name in (4, 8, 12):
            for mask in (1, 2) if name != 8 else (4, 2, 1):
                send(last, mask, name + mask)
        elif name in (1, 9):
            send(last, 2, name + 2)
        elif name in (6, 14):
            send(last, 1, name + 1)
    names = ("even", "odd", "even1", "odd1", "even2", "odd2", "even3", "odd3")
    return [found[at] for at in range(16)], [found[name] for name in names]


def per_device(
    text_in,
    layout_in,
    text_cot,
    layout_cot,
    doc_ids,
    span_ids,
    intersection_flags,
    text_qkv,
    text_qv_bias,
    text_out,
    text_out_bias,
    text_gains,
    text_shifts,
    text_up,
    text_up_bias,
    text_down,
    layout_qkv,
    layout_qv_bias,
    layout_out,
    layout_out_bias,
    layout_gains,
    layout_shifts,
    layout_up,
    layout_up_bias,
    layout_down,
):
    rows, wide = text_in.shape
    thin = layout_in.shape[1]
    whole = wide + thin
    width, width_l = text_qkv.shape[2], layout_qkv.shape[2]
    padded = width + LANES
    units, units_l = text_up.shape[1], layout_up.shape[1]
    half = rows // 2
    place = lax.axis_index("seq")
    idx = jnp.stack(
        [place & 1, (place >> 1) & 1, (place >> 2) & 3, lax.axis_index("tensor")]
    ).astype(jnp.int32)

    layout_turned, cot_turned, down_turned = layout_in.T, layout_cot.T, layout_down.T
    own_key = (doc_ids * 65536 + span_ids).astype(F32)[None, :]
    text_other, layout_other = exchange(text_in, 1), exchange(layout_turned, 1)
    keys = jnp.concatenate([own_key, exchange(own_key, 1)], axis=1)
    sent = shape((rows, wide + 2 * LANES), F32)

    cot_rows, keep_rows, pack, quarters = call(
        pack_kernel,
        [
            shape((rows, thin), BF),
            shape((rows, LANES), F32),
            shape((16, units), F32),
            shape((thin, 2 * LANES), BF),
        ],
        idx, cot_turned, intersection_flags[None, :], text_out_bias, text_gains, text_shifts,
        text_up_bias, layout_out_bias, layout_gains, layout_shifts,
        layout_up_bias, layout_up, down_turned, smem=1, far=range(1, 13), pin=range(4),
    )
    qkv_weights = (text_qkv, text_qv_bias, layout_qkv, layout_qv_bias)
    q_own, k_own, v_own, layout_rows = call(
        project_kernel,
        [shape((rows, padded), BF)] * 3 + [shape((rows, thin), BF)],
        text_in, layout_turned, *qkv_weights, pin=range(4), after=[pack], far=range(6),
    )
    attended, k_all, v_all = call(
        attend_kernel,
        [sent] + [shape((2 * rows, padded), BF)] * 2,
        q_own, k_own, v_own, text_other, layout_other, *qkv_weights, keys, text_out, layout_out,
        scratch=[pltpu.VMEM((rows, padded), BF)], pin=[1, 2],
    )
    hidden, normed, inverse, low_mine, low = call(
        norm_kernel,
        [
            shape((rows, whole), F32),
            shape((rows, whole), F32),
            shape((rows, 2 * LANES), F32),
            shape((half, wide + 2 * LANES), BF),
            shape((rows, wide + 2 * LANES), BF),
        ],
        idx, text_in, layout_rows, attended, over_cores(attended), pack, smem=1, pin=[0, 1, 2, 4],
    )
    slope_t, slope_l, ffn = call(
        ffn_kernel,
        [shape((rows, units), F32), shape((rows, units_l), F32), sent],
        low, pack, text_up, text_down, layout_up, down_turned, flops=14 * 10**8, room=20, pin=[0, 1],
    )
    ffn_back = over_cores(ffn)
    low_x, low_y = exchange(low_mine, 1), exchange(low_mine, 2)
    (
        text_result, layout_result, second, grad_low, grad_mine, sums_two, hidden_part, bias_t, bias_l,
    ) = call(
        turning_kernel,
        [
            shape((rows, wide), BF),
            shape((thin, rows), BF),
            shape((rows, whole), F32),
            shape((rows, wide + 2 * LANES), BF),
            shape((half, wide + 2 * LANES), BF),
            shape((3, whole), F32),
            sent,
            shape((1, units), F32),
            shape((1, units_l), F32),
        ],
        idx, hidden, ffn, ffn_back, text_cot, cot_rows, keep_rows, pack, slope_t, slope_l, text_up,
        text_down, layout_up, down_turned, smem=1, pin=[2, 3, 5, 7, 8], flops=14 * 10**8, room=20,
    )
    grad_x, grad_y = exchange(grad_mine, 1), exchange(grad_mine, 2)
    low_x, low_y = tied(low_x, grad_mine), tied(low_y, grad_mine)
    low_xy = exchange(low_x, 2)
    hidden_back = over_cores(tied(tied(hidden_part, low_x), low_y))
    low_far = [low_x, low_y, tied(low_xy, hidden_part)]
    low_back = over_cores(jnp.concatenate(low_far, axis=0))
    grad_x = tied(grad_x, low_far[2])
    grad_xy = exchange(grad_x, 2)
    first, attended_grad, attended_mine, small = call(
        first_norm_kernel,
        [
            shape((rows, whole), F32),
            shape((rows, whole), BF),
            shape((half, whole), BF),
            shape((32, width), F32),
        ],
        idx, second, hidden_part, hidden_back, normed, inverse, pack, sums_two, bias_t, bias_l, smem=1, pin=[0, 1],
        after=[grad_x],
    )
    attended_far = exchange(attended_mine, 1)
    grad_y = tied(grad_y, small)
    attended_far = tied(attended_far, grad_y)
    attended_back = over_cores(attended_far)
    grad_far = [grad_x, grad_y, tied(grad_xy, attended_far)]
    low_parts = [low, *low_far, low_back]
    grad_parts = [grad_low, *grad_far, over_cores(jnp.concatenate(grad_far, axis=0))]
    block = (2, wide // 4 + 16, width)
    up_keep, up_send, activated, grad_rows = call(
        unit_grads_kernel,
        [
            shape(block, F32),
            shape(block, BF),
            shape((4 * rows, units // 4 + LANES), BF),
            shape((4 * rows, wide + 2 * LANES), BF),
        ],
        idx, *low_parts, *grad_parts, text_up, text_down, quarters, pack,
        scratch=[
            pltpu.VMEM((4 * rows, wide + 2 * LANES), BF),
            pltpu.VMEM((wide, units // 4), BF),
            pltpu.VMEM((units // 4, wide), BF),
            pltpu.VMEM((thin, 2 * LANES), BF),
            pltpu.VMEM((16, units), F32),
            pltpu.VMEM((4,) + block[1:], F32),
            pltpu.SemaphoreType.DMA((14,)),
        ],
        smem=1, anys=range(1, 15), flops=18 * 10**8, room=24, pin=[2, 3],
    )
    up_far = exchange(up_send, 4)
    down_keep, down_send = call(
        down_grads_kernel,
        [shape(block, F32), shape(block, BF)],
        idx, activated, grad_rows, scratch=[pltpu.VMEM((4,) + block[1:], F32)], smem=1,
        flops=7 * 10**8, after=[up_send],
    )
    down_far = exchange(down_send, 4)
    small_other = exchange(tied(small, up_send), 1)

    dq, dk, dv, context, attended_grad_other = call(
        attention_back_kernel,
        [shape((2 * rows, padded), BF)] * 4 + [shape((rows, whole), BF)],
        idx, k_all, v_all, text_in, layout_turned, text_other, layout_other, *qkv_weights, keys,
        text_out, layout_out, attended_grad, attended_far, attended_back,
        scratch=[pltpu.VMEM((2 * rows, padded), BF)] * 2, smem=1, flops=50 * 10**8, room=24,
        pin=[0, 1, 2, 4], after=[down_send],
    )
    up_total = up_keep + tied(up_far, context).astype(F32)
    up_part = up_total[1].astype(BF)
    used = 6 * len(pieces(whole, width)) + len(pieces(units, width)) + len(pieces(units_l, width))
    block = (4,) + block[1:]
    keep, send = call(
        partial(attention_grads_kernel, used),
        [shape(block, F32), shape(block, BF)],
        idx, dq, dk, dv, context, text_in, layout_turned, text_other, layout_other, attended_grad,
        attended_grad_other, small, small_other,
        scratch=[
            pltpu.VMEM((4, thin, LANES), F32),
            pltpu.VMEM((8,) + block[1:], F32),
            pltpu.VMEM(small.shape, F32),
        ],
        smem=1, flops=10**9, room=24, after=[up_part],
    )
    send_far = exchange(send, 2)
    (input_part,) = call(
        input_part_kernel, [sent], dq, dk, dv, text_qkv, layout_qkv, flops=5 * 10**8, after=[send],
    )
    text_in_grad, layout_in_grad = call(
        input_grad_kernel,
        [shape((rows, wide), BF), shape((thin, rows), BF)],
        first, input_part, over_cores(input_part),
    )
    units_pieces, attention_pieces = reduced_and_gathered(
        keep, up_total[0], exchange(up_part, 8), down_keep, down_far, keep, send_far
    )

    up_t, up_l, down_t, down_l = call(
        units_result_kernel,
        [shape(a.shape, F32) for a in (text_up, layout_up, text_down, down_turned)],
        idx, *units_pieces, scratch=[pltpu.VMEM((4, thin, LANES), F32)] * 2, smem=1,
        room=32,
    )
    one_row = (units,), (units_l,)
    kinds = [text_out_bias.shape] * 3 + [one_row[0], text_qv_bias.shape]
    kinds += [layout_out_bias.shape] * 3 + [one_row[1], layout_qv_bias.shape]
    (
        qkv_t, out_t, qkv_l, out_l,
        out_bias_t, gains_t, shifts_t, ub_t, qv_t, out_bias_l, gains_l, shifts_l, ub_l, qv_l,
    ) = call(
        attention_result_kernel,
        [shape(a.shape, F32) for a in (text_qkv, text_out, layout_qkv, layout_out)]
        + [shape(dims, F32) for dims in kinds],
        idx, *attention_pieces, after=[up_l],
        scratch=[pltpu.VMEM((4, thin, LANES), F32), pltpu.VMEM((2, 8, 8, width), F32)], smem=1,
    )
    return (
        text_result,
        layout_result.T,
        text_in_grad,
        layout_in_grad.T,
        qkv_t,
        qv_t,
        out_t,
        out_bias_t,
        gains_t,
        shifts_t,
        up_t,
        ub_t,
        down_t,
        qkv_l,
        qv_l,
        out_l,
        out_bias_l,
        gains_l,
        shifts_l,
        up_l,
        ub_l,
        down_l.T,
    )


def solution(mesh):
    rows, both, halves = P("seq", None), P(), P("tensor", None)
    stack, columns, one = P(None, None, "tensor"), P(None, "tensor"), P("tensor")
    weights_in = (stack, columns, halves, both, both, both, columns, one, halves)
    return jax.shard_map(
        per_device,
        mesh=mesh,
        in_specs=(rows,) * 4 + (P("seq"),) * 3 + weights_in * 2,
        out_specs=(rows,) * 4 + weights_in * 2,
        check_vma=False,
    )
```

```python
from functools import partial

import jax
import jax.numpy as jnp
from jax import lax
from jax.experimental import pallas as pl
from jax.experimental.pallas import tpu as pltpu
from jax.sharding import PartitionSpec as P

HT = 64
HL = 16
EPS = 1e-06
NEG = -1e30
BF = jnp.bfloat16
F32 = jnp.float32
LANES = 128


def exchange(shard, mask, axis="seq"):
    return lax.ppermute(shard, axis, [(i, i ^ mask) for i in range(lax.axis_size(axis))])


def over_cores(shard):
    return exchange(shard, 1, "tensor")


def dot(left, right):
    return lax.dot_general(left, right, (((1,), (0,)), ((), ())), preferred_element_type=F32)


def dot_nt(left, right):
    return lax.dot_general(left, right, (((1,), (1,)), ((), ())), preferred_element_type=F32)


def dot_tn(left, right):
    return lax.dot_general(left, right, (((0,), (0,)), ((), ())), preferred_element_type=F32)


def tied(shard, token):
    return lax.optimization_barrier((shard, token))[0]


def call(kernel, outs, *args, scratch=(), smem=0, anys=(), far=(), pin=(), after=(), flops=10**8, room=16):
    far, pin = list(far), list(pin)
    n_in = len(args)
    args = (*args, *after)
    specs, given = [], []
    for at, arg in enumerate(args):
        if at < smem:
            specs.append(pl.BlockSpec(memory_space=pltpu.SMEM))
        elif at in far:
            specs.append(pl.BlockSpec(memory_space=pltpu.HBM))
            arg = pltpu.with_memory_space_constraint(arg, pltpu.HBM)
        elif at in anys or at >= n_in:
            specs.append(pl.BlockSpec(memory_space=pl.ANY))
        else:
            specs.append(pl.BlockSpec(memory_space=pltpu.VMEM))
        if isinstance(arg, Near):
            arg = pltpu.with_memory_space_constraint(arg.value, pltpu.VMEM)
        given.append(arg)
    moved = sum(a.size * a.dtype.itemsize for a in args) + sum(
        o.size * o.dtype.itemsize for o in outs
    )
    stage = [pltpu.VMEM(args[k].shape, args[k].dtype) for k in far]
    if stage:
        stage.append(pltpu.SemaphoreType.DMA((len(far),)))

    def body(*refs):
        refs = list(refs[:n_in] + refs[len(args) :])
        if not stage:
            return kernel(*refs)
        held, sems = refs[-len(stage) : -1], refs[-1]
        refs = refs[: -len(stage)]
        coming = [
            pltpu.make_async_copy(refs[k], held[at], sems.at[at]) for at, k in enumerate(far)
        ]
        for copy in coming:
            copy.start()
        for copy in coming:
            copy.wait()
        for at, k in enumerate(far):
            refs[k] = held[at]
        kernel(*refs)

    found = pl.pallas_call(
        body,
        out_shape=tuple(
            pltpu.VMEM(o.shape, o.dtype) if k in pin else o for k, o in enumerate(outs)
        ),
        in_specs=specs,
        out_specs=tuple(pl.BlockSpec(memory_space=pltpu.VMEM) for _ in outs),
        scratch_shapes=list(scratch) + stage,
        compiler_params=pltpu.CompilerParams(vmem_limit_bytes=room * 1024 * 1024),
        cost_estimate=pl.CostEstimate(flops=flops, bytes_accessed=moved, transcendentals=0),
    )(*given)
    return tuple(Near(a) if k in pin else a for k, a in enumerate(found))


class Near:
    def __init__(self, value):
        self.value = value
        self.shape, self.dtype, self.size = value.shape, value.dtype, value.size


def shape(dims, dtype):
    return jax.ShapeDtypeStruct(tuple(dims), dtype)


def project_rows(text_rows, layout_columns, weight_t, bias_t, weight_l, bias_l, which, write):
    text_part = dot(text_rows, weight_t[which])
    layout_part = dot_tn(layout_columns, weight_l[which])
    if which != 1:
        row = which // 2
        text_part = text_part + bias_t[row : row + 1, :].astype(F32)
        layout_part = layout_part + bias_l[row : row + 1, :].astype(F32)
    pad = jnp.zeros((layout_part.shape[0], LANES - layout_part.shape[1]), F32)
    write(text_part.astype(BF), jnp.concatenate([layout_part, pad], axis=1).astype(BF))


def turned(matrix):
    rows, columns = matrix.shape
    matrix = matrix.astype(F32)
    if columns % LANES:
        fill = jnp.zeros((rows, -columns % LANES), F32)
        matrix = jnp.concatenate([matrix, fill], axis=1)
    if rows % LANES:
        fill = jnp.zeros((-rows % LANES, matrix.shape[1]), F32)
        matrix = jnp.concatenate([matrix, fill], axis=0)
    return matrix.T[:columns, :rows]


OB, GAIN, SHIFT, UP_T, UP_L, UP_Q = 0, 2, 4, 6, 7, 8


def pack_kernel(
    idx, cl, flags, ob_t, g_t, s_t, ub_t, ob_l, g_l, s_l, ub_l, up_l, dn_l,
    cl_out, keep_out, pack_out, quarter_out,
):
    wide, thin = ob_t.shape[1], ob_l.shape[1]
    pack_out[...] = jnp.zeros_like(pack_out)
    for first, text, layout in ((OB, ob_t, ob_l), (GAIN, g_t, g_l), (SHIFT, s_t, s_l)):
        pack_out[first : first + 2, :wide] = text[...].astype(F32)
        pack_out[first : first + 2, wide : wide + thin] = layout[...].astype(F32)
    pack_out[UP_T : UP_T + 1, :] = ub_t[...].astype(F32)[None, :]
    bias_l = ub_l[...].astype(F32)[None, :]
    pack_out[UP_L : UP_L + 1, : bias_l.shape[1]] = bias_l
    quarter = idx[1] * 2 + idx[0]
    count = up_l.shape[1] // 4

    def cut(ref):
        value = ref[:, :count].astype(F32)
        for q in range(1, 4):
            value = jnp.where(quarter == q, ref[:, count * q : count * (q + 1)].astype(F32), value)
        return value

    pack_out[UP_Q : UP_Q + 1, :count] = cut(bias_l)
    quarter_out[:, :count] = cut(up_l).astype(BF)
    quarter_out[:, LANES : LANES + count] = cut(dn_l).astype(BF)
    cl_out[...] = turned(cl[...]).astype(BF)
    keep_out[...] = jnp.broadcast_to((1 - flags[...]).astype(F32), (LANES, flags.shape[1])).T


def project_kernel(xt, xl, wt, bt, wl, bl, q_out, k_out, v_out, xl_out):
    xl_out[...] = turned(xl[...]).astype(BF)
    width = wt.shape[2]
    for which, out in enumerate((q_out, k_out, v_out)):

        def write(text_part, layout_part, out=out):
            out[:, :width] = text_part
            out[:, width:] = layout_part

        project_rows(xt[...], xl[...], wt, bt, wl, bl, which, write)


def hidden_bias(keys, columns):
    rows = keys.shape[1]
    down = jnp.broadcast_to(keys, (LANES, rows)).T
    parts = [
        jnp.where(down == keys[:, at : at + LANES], 0.0, NEG).astype(F32)
        for at in range(0, columns, LANES)
    ]
    return jnp.concatenate(parts, axis=1)


def head_mask(member, head, text_value, layout_value, axis):
    dims = (1, 2 * LANES) if axis == 1 else (2 * LANES, 1)
    at = lax.broadcasted_iota(jnp.int32, dims, axis)
    text = (at >= member * HT) & (at < (member + 1) * HT)
    layout = (at >= LANES + head * HL) & (at < LANES + (head + 1) * HL)
    return jnp.where(text, text_value, jnp.where(layout, layout_value, 0.0)).astype(F32)


def pair_of(ref, pair, width):
    return jnp.concatenate([ref[:, LANES * pair : LANES * (pair + 1)], ref[:, width:]], axis=1)


def probabilities(key_pair, query_head, bias):
    scores = dot_nt(key_pair, query_head) + bias
    weights = jnp.exp(scores - jnp.max(scores, axis=0, keepdims=True))
    return weights * (1.0 / jnp.sum(weights, axis=0, keepdims=True))


OB, GAIN, SHIFT, UP_T, UP_L, UP_Q = 0, 2, 4, 6, 7, 8
SCALE_T = HT ** (-0.5)
SCALE_L = HL ** (-0.5)


def attend_kernel(
    q_own, k_own, v_own, xt, xl, wt, bt, wl, bl, keys, out_t, out_l, part_out, k_all, v_all, context,
):
    rows, width = q_own.shape[0], wt.shape[2]
    for which, own, target in ((1, k_own, k_all), (2, v_own, v_all)):
        target[:rows, :] = own[...]

        def write(text_part, layout_part, target=target):
            target[rows:, :width] = text_part
            target[rows:, width:] = layout_part

        project_rows(xt[...], xl[...], wt, bt, wl, bl, which, write)
    bias = hidden_bias(keys[...], rows)
    layout_sum = jnp.zeros((LANES, rows), F32)
    for pair in range(width // LANES):
        query_pair, key_pair = pair_of(q_own, pair, width), pair_of(k_all, pair, width)
        value_turned = pair_of(v_all, pair, width).T
        text_sum = jnp.zeros((LANES, rows), F32)
        for member in range(2):
            head = 2 * pair + member
            mask = head_mask(member, head, SCALE_T, SCALE_L, 1).astype(BF)
            probs_low = probabilities(key_pair, query_pair * mask, bias).astype(BF)
            turned = dot(value_turned, probs_low) * head_mask(member, head, 1.0, 1.0, 0)
            text_sum += turned[:LANES]
            layout_sum += turned[LANES:]
        context[:, LANES * pair : LANES * (pair + 1)] = text_sum.T.astype(BF)
    context[:, width:] = layout_sum.T.astype(BF)
    text_width = out_t.shape[1]
    part_out[:, :text_width] = dot(context[:, :width], out_t[...])
    part_out[:, text_width : text_width + out_l.shape[1]] = dot(
        context[:, width : width + out_l.shape[0]], out_l[...]
    )


def norm_parts(total):
    center = total - jnp.mean(total, axis=1, keepdims=True)
    inverse = lax.rsqrt(jnp.mean(center * center, axis=1, keepdims=True) + EPS)
    return center * inverse, inverse


def norm_back(upstream, normed, inverse, gain):
    scaled = upstream * gain
    return inverse * (
        scaled
        - jnp.mean(scaled, axis=1, keepdims=True)
        - normed * jnp.mean(scaled * normed, axis=1, keepdims=True)
    )


def gelu_parts(before):
    share = 0.5 * (1.0 + lax.erf(before * (0.5**0.5)))
    slope = share + before * (jnp.exp(-0.5 * before * before) * 0.3989422804014327)
    return before * share, slope


def norm_kernel(
    idx, xt, xl, part, back, pack, hidden_out, normed_out, inverse_out, mine_out, low_out
):
    width, whole, half = xt.shape[1], hidden_out.shape[1], mine_out.shape[0]
    for at, (lo, hi, x) in enumerate(((0, width, xt), (width, whole, xl))):
        total = x[...].astype(F32) + (part[:, lo:hi] + back[:, lo:hi]) + pack[OB : OB + 1, lo:hi]
        normed, inverse = norm_parts(total)
        hidden = normed * pack[GAIN : GAIN + 1, lo:hi] + pack[SHIFT : SHIFT + 1, lo:hi]
        hidden_out[:, lo:hi] = hidden
        normed_out[:, lo:hi] = normed
        inverse_out[:, LANES * at : LANES * (at + 1)] = jnp.broadcast_to(
            inverse, (inverse.shape[0], LANES)
        )
        low_out[:, lo:hi] = hidden.astype(BF)
    mine_out[...] = low_out[pl.ds(pl.multiple_of(idx[3] * half, half), half), :]


def ffn_kernel(low, pack, up_t, dn_t, up_l, dn_l, slope_t, slope_l, ffn_out):
    width = up_t.shape[0]
    whole = width + up_l.shape[0]
    for lo, hi, up, ub, dn, slope_out in (
        (0, width, up_t, UP_T, dn_t, slope_t),
        (width, whole, up_l, UP_L, dn_l, slope_l),
    ):
        rows_low = low[:, lo:hi]
        units = up.shape[1]
        step = min(units, 384)
        total = None
        for cut in range(0, units, step):
            before = dot(rows_low, up[:, cut : cut + step]) + pack[ub : ub + 1, cut : cut + step]
            activated, slope = gelu_parts(before)
            slope_out[:, cut : cut + step] = slope
            if lo == 0:
                term = dot(activated.astype(BF), dn[cut : cut + step, :])
            else:
                term = dot_nt(activated.astype(BF), dn[:, cut : cut + step])
            total = term if total is None else total + term
        ffn_out[:, lo:hi] = total


def second_norm_kernel(
    idx, hidden, part, back, ct, cl, keep, pack,
    rt_out, rl_out, second_out, low_out, mine_out, sums_out,
):
    width, whole = ct.shape[1], hidden.shape[1]
    half = mine_out.shape[0]
    for lo, hi, cot, result in ((0, width, ct, rt_out), (width, whole, cl, rl_out)):
        total = (
            hidden[:, lo:hi] + (part[:, lo:hi] + back[:, lo:hi]) + pack[OB + 1 : OB + 2, lo:hi]
        )
        normed, inverse = norm_parts(total)
        gain = pack[GAIN + 1 : GAIN + 2, lo:hi]
        value = normed * gain + pack[SHIFT + 1 : SHIFT + 2, lo:hi]
        result[...] = (value if lo == 0 else turned(value)).astype(BF)
        upstream = cot[...].astype(F32) * keep[:, :1]
        grad = norm_back(upstream, normed, inverse, gain)
        second_out[:, lo:hi] = grad
        low = grad.astype(BF)
        low_out[:, lo:hi] = low
        sums_out[0:1, lo:hi] = jnp.sum(upstream * normed, axis=0, keepdims=True)
        sums_out[1:2, lo:hi] = jnp.sum(upstream, axis=0, keepdims=True)
        sums_out[2:3, lo:hi] = jnp.sum(low.astype(F32), axis=0, keepdims=True)
    mine_out[...] = low_out[pl.ds(pl.multiple_of(idx[3] * half, half), half), :]


def ffn_back_kernel(grad, slope_t, slope_l, up_t, dn_t, up_l, dn_l, part_out, bias_t, bias_l):
    width = up_t.shape[0]
    whole = width + up_l.shape[0]
    for lo, hi, slope, up, dn, bias in (
        (0, width, slope_t, up_t, dn_t, bias_t),
        (width, whole, slope_l, up_l, dn_l, bias_l),
    ):
        rows = grad[:, lo:hi]
        units = up.shape[1]
        step = min(units, 384)
        total = None
        for cut in range(0, units, step):
            if lo == 0:
                act_grad = dot_nt(rows, dn[cut : cut + step, :])
            else:
                act_grad = dot(rows, dn[:, cut : cut + step])
            before_grad = (act_grad * slope[:, cut : cut + step]).astype(BF)
            bias[:, cut : cut + step] = jnp.sum(before_grad.astype(F32), axis=0, keepdims=True)
            term = dot_nt(before_grad, up[:, cut : cut + step])
            total = term if total is None else total + term
        part_out[:, lo:hi] = total


def turning_kernel(
    idx, hidden, part, back, ct, cl, keep, pack, slope_t, slope_l, up_t, dn_t, up_l, dn_l,
    rt_out, rl_out, second_out, low_out, mine_out, sums_out, part_out, bias_t, bias_l,
):
    second_norm_kernel(
        idx, hidden, part, back, ct, cl, keep, pack,
        rt_out, rl_out, second_out, low_out, mine_out, sums_out,
    )
    ffn_back_kernel(
        low_out, slope_t, slope_l, up_t, dn_t, up_l, dn_l, part_out, bias_t, bias_l
    )


def pieces(columns, piece):
    return [(at, min(at + piece, columns)) for at in range(0, columns, piece)]


def first_norm_kernel(
    idx, second, part, back, normed_in, inverse_in, pack, sums_two, bias_t, bias_l,
    first_out, low_out, mine_out, small_out,
):
    whole, piece = second.shape[1], small_out.shape[1]
    width = whole * 4 // 5
    small_out[...] = jnp.zeros_like(small_out)
    row = 0

    def put(value):
        nonlocal row
        for lo, hi in pieces(value.shape[1], piece):
            small_out[row : row + 1, : hi - lo] = value[:, lo:hi]
            row += 1

    sums = [[], [], []]
    for at, (lo, hi) in enumerate(((0, width), (width, whole))):
        upstream = second[:, lo:hi] + (part[:, lo:hi] + back[:, lo:hi])
        normed = normed_in[:, lo:hi]
        inverse = inverse_in[:, LANES * at : LANES * at + 1]
        grad = norm_back(upstream, normed, inverse, pack[GAIN : GAIN + 1, lo:hi])
        first_out[:, lo:hi] = grad
        low = grad.astype(BF)
        low_out[:, lo:hi] = low
        sums[0].append(jnp.sum(upstream * normed, axis=0, keepdims=True))
        sums[1].append(jnp.sum(upstream, axis=0, keepdims=True))
        sums[2].append(jnp.sum(low.astype(F32), axis=0, keepdims=True))
    half = mine_out.shape[0]
    mine_out[...] = low_out[pl.ds(pl.multiple_of(idx[3] * half, half), half), :]
    for kind in range(3):
        put(jnp.concatenate(sums[kind], axis=1))
        put(sums_two[kind : kind + 1, :])
    put(bias_t[...])
    put(bias_l[...])


def unit_grads_kernel(idx, *refs):
    (
        low_parts, grad_parts, (up_t, dn_t, quarters, pack_in),
        (keep, send, act_out, grad),
        (low, w_up, w_dn, w_l, pack, held, sems),
    ) = refs[:5], refs[5:10], refs[10:14], refs[14:18], refs[18:]
    quarter = idx[1] * 2 + idx[0]
    zz = idx[2]
    copies = []
    for parts, target in ((low_parts, low), (grad_parts, grad)):
        at = 0
        for part in parts:
            count = part.shape[0]
            copies.append((part, target.at[pl.ds(at, count), :]))
            at += count
    units = w_dn.shape[0]
    start = pl.multiple_of(quarter * units, units)
    copies.append((up_t.at[:, pl.ds(start, units)], w_up))
    copies.append((dn_t.at[pl.ds(start, units), :], w_dn))
    copies += [(quarters, w_l), (pack_in, pack)]
    copies = [pltpu.make_async_copy(s, d, sems.at[k]) for k, (s, d) in enumerate(copies)]
    for c in copies:
        c.start()
    for c in copies:
        c.wait()
    width = w_up.shape[0]
    piece = width // 4

    def grads(lo, hi, up, bias, down):
        before = dot(low[:, lo:hi], up) + bias
        activated, slope = gelu_parts(before)
        act_grad = dot_nt(grad[:, lo:hi], down) if lo == 0 else dot(grad[:, lo:hi], down)
        before_grad = (act_grad * slope).astype(BF)
        return activated.astype(BF), before_grad

    whole = width + w_l.shape[0]
    count = w_l.shape[0] // 2
    act_t, back_t = grads(
        0, width, w_up[...], pack[UP_T : UP_T + 1, pl.ds(start, units)], w_dn[...]
    )
    act_l, back_l = grads(
        width,
        whole,
        w_l[:, :count],
        pack[UP_Q : UP_Q + 1, :count],
        w_l[:, LANES : LANES + count],
    )

    act_out[:, :units] = act_t
    act_out[:, units:] = widened(act_l)
    up_grad = dot_tn(low[:, :width], back_t)
    for k in range(4):
        held[k ^ zz, :piece, :] = up_grad[piece * k : piece * (k + 1)]
    place_layout(held, zz, dot_tn(low[:, width:whole], widened(back_l)))
    hand_out(held, keep, send)


def widened(matrix):
    pad = jnp.zeros((matrix.shape[0], LANES - matrix.shape[1]), matrix.dtype)
    return jnp.concatenate([matrix, pad], axis=1)


def place_layout(held, zz, matrix):
    piece = held.shape[1] - 16
    for k in range(4):
        for slot in range(3):
            first = 16 * (3 * k + slot)
            held[k ^ zz, piece:, LANES * slot : LANES * (slot + 1)] = matrix[first : first + 16]


def hand_out(held, keep, send):
    for k in range(2):
        keep[k] = held[2 * k]
        send[k] = held[2 * k + 1].astype(BF)


def down_grads_kernel(idx, act, grad, keep, send, held):
    zz = idx[2]
    units, width = held.shape[2], 2 * held.shape[2]
    down_grad = dot_tn(act[:, :units], grad[:, :width])
    part = (held.shape[1] - 16) // 2
    for k in range(4):
        for side in range(2):
            held[k ^ zz, part * side : part * (side + 1), :] = down_grad[
                part * k : part * (k + 1), units * side : units * (side + 1)
            ]
    place_layout(held, zz, dot_tn(grad[:, width : width + width // 4], act[:, units:]))
    hand_out(held, keep, send)


def attention_back_kernel(
    idx, k_all, v_all, xt, xl, xt_p, xl_p, wt, bt, wl, bl, keys, out_t, out_l, ag_own, ag_far, ag_back,
    dq, dk, dv, context, ag_p, q_all, g_all,
):
    rows, width = xt.shape[0], wt.shape[2]
    wide = out_t.shape[1]
    half = ag_far.shape[0]
    core = idx[3]
    ag_p[pl.ds(pl.multiple_of(core * half, half), half), :] = ag_far[...]
    ag_p[pl.ds(pl.multiple_of((1 - core) * half, half), half), :] = ag_back[...]
    for at, text_rows, layout_columns in ((0, xt, xl), (rows, xt_p, xl_p)):

        def write(text_part, layout_part, at=at):
            q_all[at : at + rows, :width] = text_part
            q_all[at : at + rows, width:] = layout_part

        project_rows(text_rows[...], layout_columns[...], wt, bt, wl, bl, 0, write)
    for at, grad in ((0, ag_own), (rows, ag_p)):
        g_all[at : at + rows, :width] = dot_nt(grad[:, :wide], out_t[...]).astype(BF)
        layout_grad = dot_nt(grad[:, wide:], out_l[...])
        pad = jnp.zeros((rows, LANES - layout_grad.shape[1]), F32)
        g_all[at : at + rows, width:] = jnp.concatenate([layout_grad, pad], axis=1).astype(BF)
    bias = hidden_bias(keys[...], 2 * rows)
    zero_turned, zero = jnp.zeros((LANES, 2 * rows), F32), jnp.zeros((2 * rows, LANES), F32)
    layout_context, layout_dq, layout_dk, layout_dv = zero_turned, zero_turned, zero, zero
    for pair in range(width // LANES):
        query_pair, key_pair = pair_of(q_all, pair, width), pair_of(k_all, pair, width)
        grad_pair, value_pair = pair_of(g_all, pair, width), pair_of(v_all, pair, width)
        key_turned, value_turned = key_pair.T, value_pair.T
        text_context, text_dq, text_dk, text_dv = zero_turned, zero_turned, zero, zero
        for member in range(2):
            head = 2 * pair + member
            query_head = query_pair * head_mask(member, head, SCALE_T, SCALE_L, 1).astype(BF)
            grad_head = grad_pair * head_mask(member, head, 1.0, 1.0, 1).astype(BF)
            probs = probabilities(key_pair, query_head, bias)
            probs_low = probs.astype(BF)
            prob_grads = dot_nt(value_pair, grad_head)
            delta = jnp.sum(probs * prob_grads, axis=0, keepdims=True)
            score_grads = (probs * (prob_grads - delta)).astype(BF)
            value_part = dot(probs_low, grad_head)
            text_dv += value_part[:, :LANES]
            layout_dv += value_part[:, LANES:]
            key_part = dot(score_grads, query_head)
            text_dk += key_part[:, :LANES]
            layout_dk += key_part[:, LANES:]
            query_part = dot(key_turned, score_grads) * head_mask(member, head, SCALE_T, SCALE_L, 0)
            text_dq += query_part[:LANES]
            layout_dq += query_part[LANES:]
            context_part = dot(value_turned, probs_low) * head_mask(member, head, 1.0, 1.0, 0)
            text_context += context_part[:LANES]
            layout_context += context_part[LANES:]
        columns = slice(LANES * pair, LANES * (pair + 1))
        context[:, columns] = text_context.T.astype(BF)
        dq[:, columns] = text_dq.T.astype(BF)
        dk[:, columns] = text_dk.astype(BF)
        dv[:, columns] = text_dv.astype(BF)
    context[:, width:] = layout_context.T.astype(BF)
    dq[:, width:] = layout_dq.T.astype(BF)
    dk[:, width:] = layout_dk.astype(BF)
    dv[:, width:] = layout_dv.astype(BF)


def input_part_kernel(dq, dk, dv, wt, wl, part_out):
    rows, width, heads_l = part_out.shape[0], wt.shape[2], wl.shape[2]
    wide = wt.shape[1]
    total_t = total_l = None
    for which, grad in enumerate((dq, dk, dv)):
        term_t = dot_nt(grad[:rows, :width], wt[which])
        term_l = dot_nt(grad[:rows, width : width + heads_l], wl[which])
        total_t = term_t if which == 0 else total_t + term_t
        total_l = term_l if which == 0 else total_l + term_l
    part_out[:, :wide] = total_t
    part_out[:, wide : wide + wl.shape[1]] = total_l


def input_grad_kernel(first, part, back, text_out, layout_out):
    wide, whole = text_out.shape[1], first.shape[1]
    text_out[...] = (first[:, :wide] + (part[:, :wide] + back[:, :wide])).astype(BF)
    layout_out[...] = turned(
        first[:, wide:] + (part[:, wide:whole] + back[:, wide:whole])
    ).astype(BF)


def attention_grads_kernel(
    row, idx, dq, dk, dv, context, xt, xl, xt_p, xl_p, ag_own, ag_p, small, small_p,
    keep_out, send_out, matrices, held, sums,
):
    wide, rows = xt.shape[1], xt.shape[0]
    width = keep_out.shape[2]
    bx, by, zz = idx[0], idx[1], idx[2]
    side = wide // 2
    start = pl.multiple_of(bx * side, side)
    thin = side // 8

    def over_rows(left_own, left_other, right):
        both = jnp.concatenate([left_own, left_other], axis=0)
        return dot_tn(both, right)

    def place(matrix, lowest):
        for y in range(2):
            for z in range(4):
                first = thin * (4 * y + z)
                held[(y ^ by) * 4 + (z ^ zz), lowest : lowest + thin, :] = matrix[
                    first : first + thin
                ]

    x_side = jnp.concatenate([xt[:, pl.ds(start, side)], xt_p[:, pl.ds(start, side)]], axis=0)
    for which, grad in enumerate((dq, dk, dv)):
        place(dot_tn(x_side, grad[:, :width]), thin * which)
        matrices[which] = dot(xl[...], grad[:rows, width:]) + dot(xl_p[...], grad[rows:, width:])
    ag_side = jnp.concatenate([ag_own[:, pl.ds(start, side)], ag_p[:, pl.ds(start, side)]], axis=0)
    place(dot_tn(context[:, :width], ag_side), 3 * thin)
    ag_l = jnp.concatenate([ag_own[:, wide:], ag_p[:, wide:]], axis=0)
    matrices[3] = dot_tn(ag_l, context[:, width:])
    sums[...] = small[...] + small_p[...]
    for grad in (dq, dv):
        total = jnp.sum(grad[...].astype(F32), axis=0, keepdims=True)
        for lo, hi in pieces(total.shape[1], width):
            sums[row : row + 1, : hi - lo] = total[:, lo:hi]
            row += 1
    left, right = matrices[2 * bx], matrices[2 * bx + 1]
    strip = left.shape[0] // 8
    for y in range(2):
        for z in range(4):
            eighth = 4 * y + z
            first = strip * eighth
            both = jnp.concatenate(
                [left[first : first + strip], right[first : first + strip]], axis=0
            )[:, : width // 4]
            count = 2 * strip // 4
            packed = jnp.concatenate(
                [both[count * slot : count * (slot + 1)] for slot in range(4)], axis=1
            )
            rest = 16 - count
            held[(y ^ by) * 4 + (z ^ zz), 4 * thin : 4 * thin + 16, :] = jnp.concatenate(
                [packed, sums[rest * eighth : rest * (eighth + 1), :]], axis=0
            )
    for at, k in enumerate((0, 2, 1, 3)):
        keep_out[at] = held[k]
        send_out[at] = held[4 + k].astype(BF)


def pieces_of(refs, idx):
    for at in range(4):
        for group in range(2):
            for k in range(2):
                yield refs[2 * at + group], k, (idx[1] * 2 + idx[0]) ^ at, (2 * k + group) ^ idx[2]


def unpack_layout(piece, k, lowest, table, quarter, place):
    for slot in range(3):
        first = pl.multiple_of(place * 48 + 16 * slot, 16)
        table[quarter, pl.ds(first, 16), :] = piece[
            k, lowest : lowest + 16, LANES * slot : LANES * (slot + 1)
        ].astype(F32)


def units_result_kernel(idx, *refs):
    parts, (up_t, up_l, dn_t, dn_l, token), (up_table, dn_table) = refs[:16], refs[16:21], refs[21:]
    token[...] = jnp.zeros_like(token)
    rows, columns = up_t.shape[0] // 4, up_t.shape[1] // 4
    thin = up_l.shape[1] // 4
    half = rows // 2
    for at, piece in enumerate(parts):
        quarter, place = (idx[1] * 2 + idx[0]) ^ (at & 3), (at >> 2) ^ idx[2]
        up_t[
            pl.ds(pl.multiple_of(place * rows, rows), rows),
            pl.ds(pl.multiple_of(quarter * columns, columns), columns),
        ] = piece[0, :rows, :].astype(F32)
        unpack_layout(piece, 0, rows, up_table, quarter, place)
        first = pl.multiple_of((quarter * 4 + place) * half, half)
        for side in range(2):
            dn_t[pl.ds(first, half), columns * side : columns * (side + 1)] = piece[
                1, half * side : half * (side + 1), :
            ].astype(F32)
        unpack_layout(piece, 1, rows, dn_table, quarter, place)
    for q in range(4):
        up_l[:, thin * q : thin * (q + 1)] = up_table[q][:, :thin]
        dn_l[:, thin * q : thin * (q + 1)] = dn_table[q][:, :thin]


def attention_result_kernel(idx, *refs):
    parts, (qkv_t, out_t, qkv_l, out_l), refs = refs[:8], refs[8:12], refs[12:]
    (bt, gt, st, ubt, qvt, bl, gl, sl, ubl, qvl), (table, sums) = refs[:10], refs[10:]
    side = qkv_t.shape[1] // 2
    thin, strip, heads_l = side // 8, qkv_l.shape[1] // 8, qkv_l.shape[2]
    count = 2 * strip // 4
    rest = 16 - count
    for piece, k, quarter, place in pieces_of(parts, idx):
        x, y = quarter & 1, quarter >> 1
        eighth = y * 4 + place
        first = pl.multiple_of(x * side + eighth * thin, 16)
        for which in range(3):
            qkv_t[which, pl.ds(first, thin), :] = piece[
                k, thin * which : thin * (which + 1), :
            ].astype(F32)
        out_t[
            pl.ds(pl.multiple_of(eighth * thin, 16), thin), pl.ds(pl.multiple_of(x * side, side), side)
        ] = piece[k, 3 * thin : 4 * thin, :].astype(F32)
        last = piece[k, 4 * thin : 4 * thin + 16, :].astype(F32)
        both = jnp.concatenate(
            [last[:count, heads_l * slot : heads_l * (slot + 1)] for slot in range(4)], axis=0
        )
        for member in range(2):
            table[
                2 * x + member, pl.ds(pl.multiple_of(eighth * strip, 8), strip), :heads_l
            ] = both[strip * member : strip * (member + 1)]
        sums[x, eighth, :rest, :] = last[count:, :]
    for which in range(3):
        qkv_l[which] = table[which][:, :heads_l]
    out_l[...] = turned(table[3])[:heads_l]

    at = 0

    def take(columns):
        nonlocal at
        found = []
        for lo, hi in pieces(columns, sums.shape[3]):
            found.append(sums[0, at // rest, at % rest : at % rest + 1, : hi - lo])
            at += 1
        return jnp.concatenate(found, axis=1) if len(found) > 1 else found[0]

    wide, whole = gt.shape[1], gt.shape[1] + gl.shape[1]
    for text_out, layout_out in ((gt, gl), (st, sl), (bt, bl)):
        for row in range(2):
            value = take(whole)
            text_out[row : row + 1, :] = value[:, :wide]
            layout_out[row : row + 1, :] = value[:, wide:]
    ubt[...] = take(ubt.shape[0])[0]
    ubl[...] = take(ubl.shape[0])[0]
    for row in range(2):
        value = take(qvt.shape[1] + LANES)
        qvt[row : row + 1, :] = value[:, : qvt.shape[1]]
        qvl[row : row + 1, :] = value[:, qvt.shape[1] : qvt.shape[1] + qvl.shape[1]]


ORDER = (
    ("down4", None, 0), ("up8", None, 0), ("down8", None, 0), (4, 0, 4), (1, 0, 1), (2, 0, 2), ("y", None, 0),
    (6, 4, 2), (8, 0, 8), ("z4", None, 0), (5, 4, 1), (3, 1, 2), (12, 8, 4), ("z8", None, 0), (10, 8, 2),
    (9, 8, 1), ("even", None, 0), (13, 9, 4), (11, 9, 2), (7, 6, 1), ("odd", "even", 4), (15, 11, 4),
    ("even2", "even", 2), ("even1", "even", 1), ("odd2", "odd", 2), ("odd1", "odd", 1), (14, 10, 4),
    ("even3", "even1", 2), ("odd3", "odd2", 1),
)


def reduced_and_gathered(token, up, up_far, down_keep, down_far, keep, far):
    last = token
    coming, found = {"up8": up_far, "down4": down_far, "y": far}, {}

    def beyond(own):
        mask = 16
        while mask < lax.axis_size("seq"):
            own = own + exchange(own, mask)
            mask *= 2
        return own.astype(BF)

    def have(name, value):
        found[name] = value
        for other, source, mask in ORDER:
            if source == name and source is not None:
                coming[other] = exchange(value, mask)

    for name, _, _ in ORDER:
        last = tied(coming[name], last)
        if name == "even":
            have("even", jnp.stack([own, last]))
        else:
            have(name, last)
        if name == "down4":
            down = down_keep + last.astype(F32)
            coming["down8"] = exchange(down[1].astype(BF), 8)
        elif name == "y":
            total = keep + last.astype(F32)
            coming["z4"] = exchange(total[2:].astype(BF), 4)
        elif name == "z4":
            total = total[:2] + last.astype(F32)
            coming["z8"] = exchange(total[1].astype(BF), 8)
        elif name == "z8":
            own = beyond(total[0] + last.astype(F32))
            coming["even"] = exchange(own, 8)
        if name in ("up8", "down8") and {"up8", "down8"} <= found.keys():
            sums = up + found["up8"].astype(F32), down[0] + found["down8"].astype(F32)
            have(0, jnp.stack([beyond(piece) for piece in sums]))
    names = ("even", "odd", "even1", "odd1", "even2", "odd2", "even3", "odd3")
    return [found[at] for at in range(16)], [found[name] for name in names]


def per_device(
    text_in,
    layout_in,
    text_cot,
    layout_cot,
    doc_ids,
    span_ids,
    intersection_flags,
    text_qkv,
    text_qv_bias,
    text_out,
    text_out_bias,
    text_gains,
    text_shifts,
    text_up,
    text_up_bias,
    text_down,
    layout_qkv,
    layout_qv_bias,
    layout_out,
    layout_out_bias,
    layout_gains,
    layout_shifts,
    layout_up,
    layout_up_bias,
    layout_down,
):
    rows, wide = text_in.shape
    thin = layout_in.shape[1]
    whole = wide + thin
    width, width_l = text_qkv.shape[2], layout_qkv.shape[2]
    padded = width + LANES
    units, units_l = text_up.shape[1], layout_up.shape[1]
    half = rows // 2
    place = lax.axis_index("seq")
    idx = jnp.stack(
        [place & 1, (place >> 1) & 1, (place >> 2) & 3, lax.axis_index("tensor")]
    ).astype(jnp.int32)

    layout_turned, cot_turned, down_turned = layout_in.T, layout_cot.T, layout_down.T
    own_key = (doc_ids * 65536 + span_ids).astype(F32)[None, :]
    text_other, layout_other = exchange(text_in, 1), exchange(layout_turned, 1)
    keys = jnp.concatenate([own_key, exchange(own_key, 1)], axis=1)
    sent = shape((rows, wide + 2 * LANES), F32)

    cot_rows, keep_rows, pack, quarters = call(
        pack_kernel,
        [
            shape((rows, thin), BF),
            shape((rows, LANES), F32),
            shape((16, units), F32),
            shape((thin, 2 * LANES), BF),
        ],
        idx, cot_turned, intersection_flags[None, :], text_out_bias, text_gains, text_shifts,
        text_up_bias, layout_out_bias, layout_gains, layout_shifts,
        layout_up_bias, layout_up, down_turned, smem=1, far=range(1, 13), pin=range(4),
    )
    qkv_weights = (text_qkv, text_qv_bias, layout_qkv, layout_qv_bias)
    q_own, k_own, v_own, layout_rows = call(
        project_kernel,
        [shape((rows, padded), BF)] * 3 + [shape((rows, thin), BF)],
        text_in, layout_turned, *qkv_weights, pin=range(4), after=[pack], far=range(6),
    )
    attended, k_all, v_all = call(
        attend_kernel,
        [sent] + [shape((2 * rows, padded), BF)] * 2,
        q_own, k_own, v_own, text_other, layout_other, *qkv_weights, keys, text_out, layout_out,
        scratch=[pltpu.VMEM((rows, padded), BF)], pin=[1, 2],
    )
    hidden, normed, inverse, low_mine, low = call(
        norm_kernel,
        [
            shape((rows, whole), F32),
            shape((rows, whole), F32),
            shape((rows, 2 * LANES), F32),
            shape((half, wide + 2 * LANES), BF),
            shape((rows, wide + 2 * LANES), BF),
        ],
        idx, text_in, layout_rows, attended, over_cores(attended), pack, smem=1, pin=[0, 1, 2, 4],
    )
    slope_t, slope_l, ffn = call(
        ffn_kernel,
        [shape((rows, units), F32), shape((rows, units_l), F32), sent],
        low, pack, text_up, text_down, layout_up, down_turned, flops=14 * 10**8, room=20, pin=[0, 1],
    )
    ffn_back = over_cores(ffn)
    low_x, low_y = exchange(low_mine, 1), exchange(low_mine, 2)
    (
        text_result, layout_result, second, grad_low, grad_mine, sums_two, hidden_part, bias_t, bias_l,
    ) = call(
        turning_kernel,
        [
            shape((rows, wide), BF),
            shape((thin, rows), BF),
            shape((rows, whole), F32),
            shape((rows, wide + 2 * LANES), BF),
            shape((half, wide + 2 * LANES), BF),
            shape((3, whole), F32),
            sent,
            shape((1, units), F32),
            shape((1, units_l), F32),
        ],
        idx, hidden, ffn, ffn_back, text_cot, cot_rows, keep_rows, pack, slope_t, slope_l, text_up,
        text_down, layout_up, down_turned, smem=1, pin=[2, 3, 5, 7, 8], flops=14 * 10**8, room=20,
    )
    grad_x, grad_y = exchange(grad_mine, 1), exchange(grad_mine, 2)
    low_x, low_y = tied(low_x, grad_mine), tied(low_y, grad_mine)
    low_xy = exchange(low_x, 2)
    hidden_back = over_cores(tied(tied(hidden_part, low_x), low_y))
    grad_y = tied(grad_y, hidden_part)
    grad_xy = exchange(grad_y, 1)
    first, attended_grad, attended_mine, small = call(
        first_norm_kernel,
        [
            shape((rows, whole), F32),
            shape((rows, whole), BF),
            shape((half, whole), BF),
            shape((32, width), F32),
        ],
        idx, second, hidden_part, hidden_back, normed, inverse, pack, sums_two, bias_t, bias_l, smem=1, pin=[0, 1],
        after=[grad_y],
    )
    attended_far, small_other = exchange(attended_mine, 1), exchange(small, 1)
    low_far = [low_x, low_y, tied(low_xy, small)]
    low_back = over_cores(jnp.concatenate(low_far, axis=0))
    small_other = tied(small_other, low_far[2])
    grad_x = tied(grad_x, small_other)
    grad_far = [grad_x, grad_y, tied(grad_xy, grad_x)]
    low_parts = [low, *low_far, low_back]
    grad_parts = [grad_low, *grad_far, over_cores(jnp.concatenate(grad_far, axis=0))]
    block = (2, wide // 4 + 16, width)
    up_keep, up_send, activated, grad_rows = call(
        unit_grads_kernel,
        [
            shape(block, F32),
            shape(block, BF),
            shape((4 * rows, units // 4 + LANES), BF),
            shape((4 * rows, wide + 2 * LANES), BF),
        ],
        idx, *low_parts, *grad_parts, text_up, text_down, quarters, pack,
        scratch=[
            pltpu.VMEM((4 * rows, wide + 2 * LANES), BF),
            pltpu.VMEM((wide, units // 4), BF),
            pltpu.VMEM((units // 4, wide), BF),
            pltpu.VMEM((thin, 2 * LANES), BF),
            pltpu.VMEM((16, units), F32),
            pltpu.VMEM((4,) + block[1:], F32),
            pltpu.SemaphoreType.DMA((14,)),
        ],
        smem=1, anys=range(1, 15), flops=18 * 10**8, room=24, pin=[2, 3],
    )
    up_far = exchange(up_send, 4)
    attended_far = tied(attended_far, up_send)
    attended_back = over_cores(attended_far)
    down_keep, down_send = call(
        down_grads_kernel,
        [shape(block, F32), shape(block, BF)],
        idx, activated, grad_rows, scratch=[pltpu.VMEM((4,) + block[1:], F32)], smem=1,
        flops=7 * 10**8, after=[attended_far],
    )
    down_far = exchange(down_send, 4)

    dq, dk, dv, context, attended_grad_other = call(
        attention_back_kernel,
        [shape((2 * rows, padded), BF)] * 4 + [shape((rows, whole), BF)],
        idx, k_all, v_all, text_in, layout_turned, text_other, layout_other, *qkv_weights, keys,
        text_out, layout_out, attended_grad, attended_far, attended_back,
        scratch=[pltpu.VMEM((2 * rows, padded), BF)] * 2, smem=1, flops=50 * 10**8, room=24,
        pin=[0, 1, 2, 4], after=[down_send],
    )
    up_total = up_keep + tied(up_far, context).astype(F32)
    up_part = up_total[1].astype(BF)
    used = 6 * len(pieces(whole, width)) + len(pieces(units, width)) + len(pieces(units_l, width))
    block = (4,) + block[1:]
    keep, send = call(
        partial(attention_grads_kernel, used),
        [shape(block, F32), shape(block, BF)],
        idx, dq, dk, dv, context, text_in, layout_turned, text_other, layout_other, attended_grad,
        attended_grad_other, small, small_other,
        scratch=[
            pltpu.VMEM((4, thin, LANES), F32),
            pltpu.VMEM((8,) + block[1:], F32),
            pltpu.VMEM(small.shape, F32),
        ],
        smem=1, flops=10**9, room=24, after=[up_part],
    )
    send_far = exchange(send, 2)
    (input_part,) = call(
        input_part_kernel, [sent], dq, dk, dv, text_qkv, layout_qkv, flops=5 * 10**8, after=[send],
    )
    text_in_grad, layout_in_grad = call(
        input_grad_kernel,
        [shape((rows, wide), BF), shape((thin, rows), BF)],
        first, input_part, over_cores(input_part),
    )
    units_pieces, attention_pieces = reduced_and_gathered(
        keep, up_total[0], exchange(up_part, 8), down_keep, down_far, keep, send_far
    )

    up_t, up_l, down_t, down_l, token = call(
        units_result_kernel,
        [shape(a.shape, F32) for a in (text_up, layout_up, text_down, down_turned)]
        + [shape((8, LANES), F32)],
        idx, *units_pieces, scratch=[pltpu.VMEM((4, thin, LANES), F32)] * 2, smem=1,
        pin=[4], room=32,
    )
    one_row = (units,), (units_l,)
    kinds = [text_out_bias.shape] * 3 + [one_row[0], text_qv_bias.shape]
    kinds += [layout_out_bias.shape] * 3 + [one_row[1], layout_qv_bias.shape]
    (
        qkv_t, out_t, qkv_l, out_l,
        out_bias_t, gains_t, shifts_t, ub_t, qv_t, out_bias_l, gains_l, shifts_l, ub_l, qv_l,
    ) = call(
        attention_result_kernel,
        [shape(a.shape, F32) for a in (text_qkv, text_out, layout_qkv, layout_out)]
        + [shape(dims, F32) for dims in kinds],
        idx, *attention_pieces, after=[token],
        scratch=[pltpu.VMEM((4, thin, LANES), F32), pltpu.VMEM((2, 8, 8, width), F32)], smem=1,
    )
    return (
        text_result,
        layout_result.T,
        text_in_grad,
        layout_in_grad.T,
        qkv_t,
        qv_t,
        out_t,
        out_bias_t,
        gains_t,
        shifts_t,
        up_t,
        ub_t,
        down_t,
        qkv_l,
        qv_l,
        out_l,
        out_bias_l,
        gains_l,
        shifts_l,
        up_l,
        ub_l,
        down_l.T,
    )


def solution(mesh):
    rows, both, halves = P("seq", None), P(), P("tensor", None)
    stack, columns, one = P(None, None, "tensor"), P(None, "tensor"), P("tensor")
    weights_in = (stack, columns, halves, both, both, both, columns, one, halves)
    return jax.shard_map(
        per_device,
        mesh=mesh,
        in_specs=(rows,) * 4 + (P("seq"),) * 3 + weights_in * 2,
        out_specs=(rows,) * 4 + weights_in * 2,
        check_vma=False,
    )
```

```python
from functools import partial

import jax
import jax.numpy as jnp
from jax import lax
from jax.experimental import pallas as pl
from jax.experimental.pallas import tpu as pltpu
from jax.sharding import PartitionSpec as P

HT = 64
HL = 16
EPS = 1e-06
NEG = -1e30
BF = jnp.bfloat16
F32 = jnp.float32
LANES = 128


def exchange(shard, mask, axis="seq"):
    return lax.ppermute(shard, axis, [(i, i ^ mask) for i in range(lax.axis_size(axis))])


def over_cores(shard):
    return exchange(shard, 1, "tensor")


def dot(left, right):
    return lax.dot_general(left, right, (((1,), (0,)), ((), ())), preferred_element_type=F32)


def dot_nt(left, right):
    return lax.dot_general(left, right, (((1,), (1,)), ((), ())), preferred_element_type=F32)


def dot_tn(left, right):
    return lax.dot_general(left, right, (((0,), (0,)), ((), ())), preferred_element_type=F32)


def tied(shard, token):
    return lax.optimization_barrier((shard, token))[0]


def call(kernel, outs, *args, scratch=(), smem=0, anys=(), far=(), pin=(), after=(), flops=10**8, room=16):
    far, pin = list(far), list(pin)
    n_in = len(args)
    args = (*args, *after)
    specs, given = [], []
    for at, arg in enumerate(args):
        if at < smem:
            specs.append(pl.BlockSpec(memory_space=pltpu.SMEM))
        elif at in far:
            specs.append(pl.BlockSpec(memory_space=pltpu.HBM))
            arg = pltpu.with_memory_space_constraint(arg, pltpu.HBM)
        elif at in anys or at >= n_in:
            specs.append(pl.BlockSpec(memory_space=pl.ANY))
        else:
            specs.append(pl.BlockSpec(memory_space=pltpu.VMEM))
        if isinstance(arg, Near):
            arg = pltpu.with_memory_space_constraint(arg.value, pltpu.VMEM)
        given.append(arg)
    moved = sum(a.size * a.dtype.itemsize for a in args) + sum(
        o.size * o.dtype.itemsize for o in outs
    )
    stage = [pltpu.VMEM(args[k].shape, args[k].dtype) for k in far]
    if stage:
        stage.append(pltpu.SemaphoreType.DMA((len(far),)))

    def body(*refs):
        refs = list(refs[:n_in] + refs[len(args) :])
        if not stage:
            return kernel(*refs)
        held, sems = refs[-len(stage) : -1], refs[-1]
        refs = refs[: -len(stage)]
        coming = [
            pltpu.make_async_copy(refs[k], held[at], sems.at[at]) for at, k in enumerate(far)
        ]
        for copy in coming:
            copy.start()
        for copy in coming:
            copy.wait()
        for at, k in enumerate(far):
            refs[k] = held[at]
        kernel(*refs)

    found = pl.pallas_call(
        body,
        out_shape=tuple(
            pltpu.VMEM(o.shape, o.dtype) if k in pin else o for k, o in enumerate(outs)
        ),
        in_specs=specs,
        out_specs=tuple(pl.BlockSpec(memory_space=pltpu.VMEM) for _ in outs),
        scratch_shapes=list(scratch) + stage,
        compiler_params=pltpu.CompilerParams(vmem_limit_bytes=room * 1024 * 1024),
        cost_estimate=pl.CostEstimate(flops=flops, bytes_accessed=moved, transcendentals=0),
    )(*given)
    return tuple(Near(a) if k in pin else a for k, a in enumerate(found))


class Near:
    def __init__(self, value):
        self.value = value
        self.shape, self.dtype, self.size = value.shape, value.dtype, value.size


def shape(dims, dtype):
    return jax.ShapeDtypeStruct(tuple(dims), dtype)


def project_rows(text_rows, layout_columns, weight_t, bias_t, weight_l, bias_l, which, write):
    text_part = dot(text_rows, weight_t[which])
    layout_part = dot_tn(layout_columns, weight_l[which])
    if which != 1:
        row = which // 2
        text_part = text_part + bias_t[row : row + 1, :].astype(F32)
        layout_part = layout_part + bias_l[row : row + 1, :].astype(F32)
    pad = jnp.zeros((layout_part.shape[0], LANES - layout_part.shape[1]), F32)
    write(text_part.astype(BF), jnp.concatenate([layout_part, pad], axis=1).astype(BF))


def turned(matrix):
    rows, columns = matrix.shape
    matrix = matrix.astype(F32)
    if columns % LANES:
        fill = jnp.zeros((rows, -columns % LANES), F32)
        matrix = jnp.concatenate([matrix, fill], axis=1)
    if rows % LANES:
        fill = jnp.zeros((-rows % LANES, matrix.shape[1]), F32)
        matrix = jnp.concatenate([matrix, fill], axis=0)
    return matrix.T[:columns, :rows]


OB, GAIN, SHIFT, UP_T, UP_L, UP_Q = 0, 2, 4, 6, 7, 8


def pack_kernel(
    idx, cl, flags, ob_t, g_t, s_t, ub_t, ob_l, g_l, s_l, ub_l, up_l, dn_l,
    cl_out, keep_out, pack_out, quarter_out,
):
    wide, thin = ob_t.shape[1], ob_l.shape[1]
    pack_out[...] = jnp.zeros_like(pack_out)
    for first, text, layout in ((OB, ob_t, ob_l), (GAIN, g_t, g_l), (SHIFT, s_t, s_l)):
        pack_out[first : first + 2, :wide] = text[...].astype(F32)
        pack_out[first : first + 2, wide : wide + thin] = layout[...].astype(F32)
    pack_out[UP_T : UP_T + 1, :] = ub_t[...].astype(F32)[None, :]
    bias_l = ub_l[...].astype(F32)[None, :]
    pack_out[UP_L : UP_L + 1, : bias_l.shape[1]] = bias_l
    quarter = idx[1] * 2 + idx[0]
    count = up_l.shape[1] // 4

    def cut(ref):
        value = ref[:, :count].astype(F32)
        for q in range(1, 4):
            value = jnp.where(quarter == q, ref[:, count * q : count * (q + 1)].astype(F32), value)
        return value

    pack_out[UP_Q : UP_Q + 1, :count] = cut(bias_l)
    quarter_out[:, :count] = cut(up_l).astype(BF)
    quarter_out[:, LANES : LANES + count] = cut(dn_l).astype(BF)
    cl_out[...] = turned(cl[...]).astype(BF)
    keep_out[...] = jnp.broadcast_to((1 - flags[...]).astype(F32), (LANES, flags.shape[1])).T


def project_kernel(xt, xl, wt, bt, wl, bl, q_out, k_out, v_out, xl_out):
    xl_out[...] = turned(xl[...]).astype(BF)
    width = wt.shape[2]
    for which, out in enumerate((q_out, k_out, v_out)):

        def write(text_part, layout_part, out=out):
            out[:, :width] = text_part
            out[:, width:] = layout_part

        project_rows(xt[...], xl[...], wt, bt, wl, bl, which, write)


def hidden_bias(keys, columns):
    rows = keys.shape[1]
    down = jnp.broadcast_to(keys, (LANES, rows)).T
    parts = [
        jnp.where(down == keys[:, at : at + LANES], 0.0, NEG).astype(F32)
        for at in range(0, columns, LANES)
    ]
    return jnp.concatenate(parts, axis=1)


def head_mask(member, head, text_value, layout_value, axis):
    dims = (1, 2 * LANES) if axis == 1 else (2 * LANES, 1)
    at = lax.broadcasted_iota(jnp.int32, dims, axis)
    text = (at >= member * HT) & (at < (member + 1) * HT)
    layout = (at >= LANES + head * HL) & (at < LANES + (head + 1) * HL)
    return jnp.where(text, text_value, jnp.where(layout, layout_value, 0.0)).astype(F32)


def pair_of(ref, pair, width):
    return jnp.concatenate([ref[:, LANES * pair : LANES * (pair + 1)], ref[:, width:]], axis=1)


def probabilities(key_pair, query_head, bias):
    scores = dot_nt(key_pair, query_head) + bias
    weights = jnp.exp(scores - jnp.max(scores, axis=0, keepdims=True))
    return weights * (1.0 / jnp.sum(weights, axis=0, keepdims=True))


OB, GAIN, SHIFT, UP_T, UP_L, UP_Q = 0, 2, 4, 6, 7, 8
SCALE_T = HT ** (-0.5)
SCALE_L = HL ** (-0.5)


def attend_kernel(
    q_own, k_own, v_own, xt, xl, wt, bt, wl, bl, keys, out_t, out_l, part_out, k_all, v_all, context,
):
    rows, width = q_own.shape[0], wt.shape[2]
    for which, own, target in ((1, k_own, k_all), (2, v_own, v_all)):
        target[:rows, :] = own[...]

        def write(text_part, layout_part, target=target):
            target[rows:, :width] = text_part
            target[rows:, width:] = layout_part

        project_rows(xt[...], xl[...], wt, bt, wl, bl, which, write)
    bias = hidden_bias(keys[...], rows)
    layout_sum = jnp.zeros((LANES, rows), F32)
    for pair in range(width // LANES):
        query_pair, key_pair = pair_of(q_own, pair, width), pair_of(k_all, pair, width)
        value_turned = pair_of(v_all, pair, width).T
        text_sum = jnp.zeros((LANES, rows), F32)
        for member in range(2):
            head = 2 * pair + member
            mask = head_mask(member, head, SCALE_T, SCALE_L, 1).astype(BF)
            probs_low = probabilities(key_pair, query_pair * mask, bias).astype(BF)
            turned = dot(value_turned, probs_low) * head_mask(member, head, 1.0, 1.0, 0)
            text_sum += turned[:LANES]
            layout_sum += turned[LANES:]
        context[:, LANES * pair : LANES * (pair + 1)] = text_sum.T.astype(BF)
    context[:, width:] = layout_sum.T.astype(BF)
    text_width = out_t.shape[1]
    part_out[:, :text_width] = dot(context[:, :width], out_t[...])
    part_out[:, text_width : text_width + out_l.shape[1]] = dot(
        context[:, width : width + out_l.shape[0]], out_l[...]
    )


def norm_parts(total):
    center = total - jnp.mean(total, axis=1, keepdims=True)
    inverse = lax.rsqrt(jnp.mean(center * center, axis=1, keepdims=True) + EPS)
    return center * inverse, inverse


def norm_back(upstream, normed, inverse, gain):
    scaled = upstream * gain
    return inverse * (
        scaled
        - jnp.mean(scaled, axis=1, keepdims=True)
        - normed * jnp.mean(scaled * normed, axis=1, keepdims=True)
    )


def gelu_parts(before):
    share = 0.5 * (1.0 + lax.erf(before * (0.5**0.5)))
    slope = share + before * (jnp.exp(-0.5 * before * before) * 0.3989422804014327)
    return before * share, slope


def norm_kernel(
    idx, xt, xl, part, back, pack, hidden_out, normed_out, inverse_out, mine_out, low_out
):
    width, whole, half = xt.shape[1], hidden_out.shape[1], mine_out.shape[0]
    for at, (lo, hi, x) in enumerate(((0, width, xt), (width, whole, xl))):
        total = x[...].astype(F32) + (part[:, lo:hi] + back[:, lo:hi]) + pack[OB : OB + 1, lo:hi]
        normed, inverse = norm_parts(total)
        hidden = normed * pack[GAIN : GAIN + 1, lo:hi] + pack[SHIFT : SHIFT + 1, lo:hi]
        hidden_out[:, lo:hi] = hidden
        normed_out[:, lo:hi] = normed
        inverse_out[:, LANES * at : LANES * (at + 1)] = jnp.broadcast_to(
            inverse, (inverse.shape[0], LANES)
        )
        low_out[:, lo:hi] = hidden.astype(BF)
    mine_out[...] = low_out[pl.ds(pl.multiple_of(idx[3] * half, half), half), :]


def ffn_kernel(low, pack, up_t, dn_t, up_l, dn_l, slope_t, slope_l, ffn_out):
    width = up_t.shape[0]
    whole = width + up_l.shape[0]
    for lo, hi, up, ub, dn, slope_out in (
        (0, width, up_t, UP_T, dn_t, slope_t),
        (width, whole, up_l, UP_L, dn_l, slope_l),
    ):
        rows_low = low[:, lo:hi]
        units = up.shape[1]
        step = min(units, 384)
        total = None
        for cut in range(0, units, step):
            before = dot(rows_low, up[:, cut : cut + step]) + pack[ub : ub + 1, cut : cut + step]
            activated, slope = gelu_parts(before)
            slope_out[:, cut : cut + step] = slope
            if lo == 0:
                term = dot(activated.astype(BF), dn[cut : cut + step, :])
            else:
                term = dot_nt(activated.astype(BF), dn[:, cut : cut + step])
            total = term if total is None else total + term
        ffn_out[:, lo:hi] = total


def second_norm_kernel(
    idx, hidden, part, back, ct, cl, keep, pack,
    rt_out, rl_out, second_out, low_out, mine_out, sums_out,
):
    width, whole = ct.shape[1], hidden.shape[1]
    half = mine_out.shape[0]
    for lo, hi, cot, result in ((0, width, ct, rt_out), (width, whole, cl, rl_out)):
        total = (
            hidden[:, lo:hi] + (part[:, lo:hi] + back[:, lo:hi]) + pack[OB + 1 : OB + 2, lo:hi]
        )
        normed, inverse = norm_parts(total)
        gain = pack[GAIN + 1 : GAIN + 2, lo:hi]
        value = normed * gain + pack[SHIFT + 1 : SHIFT + 2, lo:hi]
        result[...] = (value if lo == 0 else turned(value)).astype(BF)
        upstream = cot[...].astype(F32) * keep[:, :1]
        grad = norm_back(upstream, normed, inverse, gain)
        second_out[:, lo:hi] = grad
        low = grad.astype(BF)
        low_out[:, lo:hi] = low
        sums_out[0:1, lo:hi] = jnp.sum(upstream * normed, axis=0, keepdims=True)
        sums_out[1:2, lo:hi] = jnp.sum(upstream, axis=0, keepdims=True)
        sums_out[2:3, lo:hi] = jnp.sum(low.astype(F32), axis=0, keepdims=True)
    mine_out[...] = low_out[pl.ds(pl.multiple_of(idx[3] * half, half), half), :]


def ffn_back_kernel(grad, slope_t, slope_l, up_t, dn_t, up_l, dn_l, part_out, bias_t, bias_l):
    width = up_t.shape[0]
    whole = width + up_l.shape[0]
    for lo, hi, slope, up, dn, bias in (
        (0, width, slope_t, up_t, dn_t, bias_t),
        (width, whole, slope_l, up_l, dn_l, bias_l),
    ):
        rows = grad[:, lo:hi]
        units = up.shape[1]
        step = min(units, 384)
        total = None
        for cut in range(0, units, step):
            if lo == 0:
                act_grad = dot_nt(rows, dn[cut : cut + step, :])
            else:
                act_grad = dot(rows, dn[:, cut : cut + step])
            before_grad = (act_grad * slope[:, cut : cut + step]).astype(BF)
            bias[:, cut : cut + step] = jnp.sum(before_grad.astype(F32), axis=0, keepdims=True)
            term = dot_nt(before_grad, up[:, cut : cut + step])
            total = term if total is None else total + term
        part_out[:, lo:hi] = total


def turning_kernel(
    idx, hidden, part, back, ct, cl, keep, pack, slope_t, slope_l, up_t, dn_t, up_l, dn_l,
    rt_out, rl_out, second_out, low_out, mine_out, sums_out, part_out, bias_t, bias_l,
):
    second_norm_kernel(
        idx, hidden, part, back, ct, cl, keep, pack,
        rt_out, rl_out, second_out, low_out, mine_out, sums_out,
    )
    ffn_back_kernel(
        low_out, slope_t, slope_l, up_t, dn_t, up_l, dn_l, part_out, bias_t, bias_l
    )


def pieces(columns, piece):
    return [(at, min(at + piece, columns)) for at in range(0, columns, piece)]


def first_norm_kernel(
    idx, second, part, back, normed_in, inverse_in, pack, sums_two, bias_t, bias_l,
    first_out, low_out, mine_out, small_out,
):
    whole, piece = second.shape[1], small_out.shape[1]
    width = whole * 4 // 5
    small_out[...] = jnp.zeros_like(small_out)
    row = 0

    def put(value):
        nonlocal row
        for lo, hi in pieces(value.shape[1], piece):
            small_out[row : row + 1, : hi - lo] = value[:, lo:hi]
            row += 1

    sums = [[], [], []]
    for at, (lo, hi) in enumerate(((0, width), (width, whole))):
        upstream = second[:, lo:hi] + (part[:, lo:hi] + back[:, lo:hi])
        normed = normed_in[:, lo:hi]
        inverse = inverse_in[:, LANES * at : LANES * at + 1]
        grad = norm_back(upstream, normed, inverse, pack[GAIN : GAIN + 1, lo:hi])
        first_out[:, lo:hi] = grad
        low = grad.astype(BF)
        low_out[:, lo:hi] = low
        sums[0].append(jnp.sum(upstream * normed, axis=0, keepdims=True))
        sums[1].append(jnp.sum(upstream, axis=0, keepdims=True))
        sums[2].append(jnp.sum(low.astype(F32), axis=0, keepdims=True))
    half = mine_out.shape[0]
    mine_out[...] = low_out[pl.ds(pl.multiple_of(idx[3] * half, half), half), :]
    for kind in range(3):
        put(jnp.concatenate(sums[kind], axis=1))
        put(sums_two[kind : kind + 1, :])
    put(bias_t[...])
    put(bias_l[...])


def unit_grads_kernel(idx, *refs):
    (
        low_parts, grad_parts, (up_t, dn_t, quarters, pack_in),
        (keep, send, act_out, grad),
        (low, w_up, w_dn, w_l, pack, held, sems),
    ) = refs[:5], refs[5:10], refs[10:14], refs[14:18], refs[18:]
    quarter = idx[1] * 2 + idx[0]
    zz = idx[2]
    copies = []
    for parts, target in ((low_parts, low), (grad_parts, grad)):
        at = 0
        for part in parts:
            count = part.shape[0]
            copies.append((part, target.at[pl.ds(at, count), :]))
            at += count
    units = w_dn.shape[0]
    start = pl.multiple_of(quarter * units, units)
    copies.append((up_t.at[:, pl.ds(start, units)], w_up))
    copies.append((dn_t.at[pl.ds(start, units), :], w_dn))
    copies += [(quarters, w_l), (pack_in, pack)]
    copies = [pltpu.make_async_copy(s, d, sems.at[k]) for k, (s, d) in enumerate(copies)]
    for c in copies:
        c.start()
    for c in copies:
        c.wait()
    width = w_up.shape[0]
    piece = width // 4

    def grads(lo, hi, up, bias, down):
        before = dot(low[:, lo:hi], up) + bias
        activated, slope = gelu_parts(before)
        act_grad = dot_nt(grad[:, lo:hi], down) if lo == 0 else dot(grad[:, lo:hi], down)
        before_grad = (act_grad * slope).astype(BF)
        return activated.astype(BF), before_grad

    whole = width + w_l.shape[0]
    count = w_l.shape[0] // 2
    act_t, back_t = grads(
        0, width, w_up[...], pack[UP_T : UP_T + 1, pl.ds(start, units)], w_dn[...]
    )
    act_l, back_l = grads(
        width,
        whole,
        w_l[:, :count],
        pack[UP_Q : UP_Q + 1, :count],
        w_l[:, LANES : LANES + count],
    )

    act_out[:, :units] = act_t
    act_out[:, units:] = widened(act_l)
    up_grad = dot_tn(low[:, :width], back_t)
    for k in range(4):
        held[k ^ zz, :piece, :] = up_grad[piece * k : piece * (k + 1)]
    place_layout(held, zz, dot_tn(low[:, width:whole], widened(back_l)))
    hand_out(held, keep, send)


def widened(matrix):
    pad = jnp.zeros((matrix.shape[0], LANES - matrix.shape[1]), matrix.dtype)
    return jnp.concatenate([matrix, pad], axis=1)


def place_layout(held, zz, matrix):
    piece = held.shape[1] - 16
    for k in range(4):
        for slot in range(3):
            first = 16 * (3 * k + slot)
            held[k ^ zz, piece:, LANES * slot : LANES * (slot + 1)] = matrix[first : first + 16]


def hand_out(held, keep, send):
    for k in range(2):
        keep[k] = held[3 * k]
        send[k] = held[1 + k].astype(BF)


def down_grads_kernel(idx, act, grad, keep, send, held):
    zz = idx[2]
    units, width = held.shape[2], 2 * held.shape[2]
    down_grad = dot_tn(act[:, :units], grad[:, :width])
    part = (held.shape[1] - 16) // 2
    for k in range(4):
        for side in range(2):
            held[k ^ zz, part * side : part * (side + 1), :] = down_grad[
                part * k : part * (k + 1), units * side : units * (side + 1)
            ]
    place_layout(held, zz, dot_tn(grad[:, width : width + width // 4], act[:, units:]))
    hand_out(held, keep, send)


def attention_back_kernel(
    idx, k_all, v_all, xt, xl, xt_p, xl_p, wt, bt, wl, bl, keys, out_t, out_l, ag_own, ag_far, ag_back,
    dq, dk, dv, context, ag_p, q_all, g_all,
):
    rows, width = xt.shape[0], wt.shape[2]
    wide = out_t.shape[1]
    half = ag_far.shape[0]
    core = idx[3]
    ag_p[pl.ds(pl.multiple_of(core * half, half), half), :] = ag_far[...]
    ag_p[pl.ds(pl.multiple_of((1 - core) * half, half), half), :] = ag_back[...]
    for at, text_rows, layout_columns in ((0, xt, xl), (rows, xt_p, xl_p)):

        def write(text_part, layout_part, at=at):
            q_all[at : at + rows, :width] = text_part
            q_all[at : at + rows, width:] = layout_part

        project_rows(text_rows[...], layout_columns[...], wt, bt, wl, bl, 0, write)
    for at, grad in ((0, ag_own), (rows, ag_p)):
        g_all[at : at + rows, :width] = dot_nt(grad[:, :wide], out_t[...]).astype(BF)
        layout_grad = dot_nt(grad[:, wide:], out_l[...])
        pad = jnp.zeros((rows, LANES - layout_grad.shape[1]), F32)
        g_all[at : at + rows, width:] = jnp.concatenate([layout_grad, pad], axis=1).astype(BF)
    bias = hidden_bias(keys[...], 2 * rows)
    zero_turned, zero = jnp.zeros((LANES, 2 * rows), F32), jnp.zeros((2 * rows, LANES), F32)
    layout_context, layout_dq, layout_dk, layout_dv = zero_turned, zero_turned, zero, zero
    for pair in range(width // LANES):
        query_pair, key_pair = pair_of(q_all, pair, width), pair_of(k_all, pair, width)
        grad_pair, value_pair = pair_of(g_all, pair, width), pair_of(v_all, pair, width)
        key_turned, value_turned = key_pair.T, value_pair.T
        text_context, text_dq, text_dk, text_dv = zero_turned, zero_turned, zero, zero
        for member in range(2):
            head = 2 * pair + member
            query_head = query_pair * head_mask(member, head, SCALE_T, SCALE_L, 1).astype(BF)
            grad_head = grad_pair * head_mask(member, head, 1.0, 1.0, 1).astype(BF)
            probs = probabilities(key_pair, query_head, bias)
            probs_low = probs.astype(BF)
            prob_grads = dot_nt(value_pair, grad_head)
            delta = jnp.sum(probs * prob_grads, axis=0, keepdims=True)
            score_grads = (probs * (prob_grads - delta)).astype(BF)
            value_part = dot(probs_low, grad_head)
            text_dv += value_part[:, :LANES]
            layout_dv += value_part[:, LANES:]
            key_part = dot(score_grads, query_head)
            text_dk += key_part[:, :LANES]
            layout_dk += key_part[:, LANES:]
            query_part = dot(key_turned, score_grads) * head_mask(member, head, SCALE_T, SCALE_L, 0)
            text_dq += query_part[:LANES]
            layout_dq += query_part[LANES:]
            context_part = dot(value_turned, probs_low) * head_mask(member, head, 1.0, 1.0, 0)
            text_context += context_part[:LANES]
            layout_context += context_part[LANES:]
        columns = slice(LANES * pair, LANES * (pair + 1))
        context[:, columns] = text_context.T.astype(BF)
        dq[:, columns] = text_dq.T.astype(BF)
        dk[:, columns] = text_dk.astype(BF)
        dv[:, columns] = text_dv.astype(BF)
    context[:, width:] = layout_context.T.astype(BF)
    dq[:, width:] = layout_dq.T.astype(BF)
    dk[:, width:] = layout_dk.astype(BF)
    dv[:, width:] = layout_dv.astype(BF)


def input_part_kernel(dq, dk, dv, wt, wl, part_out):
    rows, width, heads_l = part_out.shape[0], wt.shape[2], wl.shape[2]
    wide = wt.shape[1]
    total_t = total_l = None
    for which, grad in enumerate((dq, dk, dv)):
        term_t = dot_nt(grad[:rows, :width], wt[which])
        term_l = dot_nt(grad[:rows, width : width + heads_l], wl[which])
        total_t = term_t if which == 0 else total_t + term_t
        total_l = term_l if which == 0 else total_l + term_l
    part_out[:, :wide] = total_t
    part_out[:, wide : wide + wl.shape[1]] = total_l


def input_grad_kernel(first, part, back, text_out, layout_out):
    wide, whole = text_out.shape[1], first.shape[1]
    text_out[...] = (first[:, :wide] + (part[:, :wide] + back[:, :wide])).astype(BF)
    layout_out[...] = turned(
        first[:, wide:] + (part[:, wide:whole] + back[:, wide:whole])
    ).astype(BF)


def attention_grads_kernel(
    row, idx, dq, dk, dv, context, xt, xl, xt_p, xl_p, ag_own, ag_p, small, small_p,
    keep_out, send_out, matrices, held, sums,
):
    wide, rows = xt.shape[1], xt.shape[0]
    width = keep_out.shape[2]
    bx, by, zz = idx[0], idx[1], idx[2]
    side = wide // 2
    start = pl.multiple_of(bx * side, side)
    thin = side // 8

    def over_rows(left_own, left_other, right):
        both = jnp.concatenate([left_own, left_other], axis=0)
        return dot_tn(both, right)

    def place(matrix, lowest):
        for y in range(2):
            for z in range(4):
                first = thin * (4 * y + z)
                held[(y ^ by) * 4 + (z ^ zz), lowest : lowest + thin, :] = matrix[
                    first : first + thin
                ]

    x_side = jnp.concatenate([xt[:, pl.ds(start, side)], xt_p[:, pl.ds(start, side)]], axis=0)
    for which, grad in enumerate((dq, dk, dv)):
        place(dot_tn(x_side, grad[:, :width]), thin * which)
        matrices[which] = dot(xl[...], grad[:rows, width:]) + dot(xl_p[...], grad[rows:, width:])
    ag_side = jnp.concatenate([ag_own[:, pl.ds(start, side)], ag_p[:, pl.ds(start, side)]], axis=0)
    place(dot_tn(context[:, :width], ag_side), 3 * thin)
    ag_l = jnp.concatenate([ag_own[:, wide:], ag_p[:, wide:]], axis=0)
    matrices[3] = dot_tn(ag_l, context[:, width:])
    sums[...] = small[...] + small_p[...]
    for grad in (dq, dv):
        total = jnp.sum(grad[...].astype(F32), axis=0, keepdims=True)
        for lo, hi in pieces(total.shape[1], width):
            sums[row : row + 1, : hi - lo] = total[:, lo:hi]
            row += 1
    left, right = matrices[2 * bx], matrices[2 * bx + 1]
    strip = left.shape[0] // 8
    for y in range(2):
        for z in range(4):
            eighth = 4 * y + z
            first = strip * eighth
            both = jnp.concatenate(
                [left[first : first + strip], right[first : first + strip]], axis=0
            )[:, : width // 4]
            count = 2 * strip // 4
            packed = jnp.concatenate(
                [both[count * slot : count * (slot + 1)] for slot in range(4)], axis=1
            )
            rest = 16 - count
            held[(y ^ by) * 4 + (z ^ zz), 4 * thin : 4 * thin + 16, :] = jnp.concatenate(
                [packed, sums[rest * eighth : rest * (eighth + 1), :]], axis=0
            )
    for at, k in enumerate((0, 3, 1, 2)):
        keep_out[at] = held[k]
        send_out[at] = held[4 + k].astype(BF)


def pieces_of(refs, idx):
    for at in range(4):
        for group in range(2):
            for k in range(2):
                yield refs[2 * at + group], k, (idx[1] * 2 + idx[0]) ^ at, (3 * k) ^ group ^ idx[2]


def unpack_layout(piece, k, lowest, table, quarter, place):
    for slot in range(3):
        first = pl.multiple_of(place * 48 + 16 * slot, 16)
        table[quarter, pl.ds(first, 16), :] = piece[
            k, lowest : lowest + 16, LANES * slot : LANES * (slot + 1)
        ].astype(F32)


def units_result_kernel(idx, *refs):
    parts, (up_t, up_l, dn_t, dn_l, token), (up_table, dn_table) = refs[:16], refs[16:21], refs[21:]
    token[...] = jnp.zeros_like(token)
    rows, columns = up_t.shape[0] // 4, up_t.shape[1] // 4
    thin = up_l.shape[1] // 4
    half = rows // 2
    for at, piece in enumerate(parts):
        quarter, place = (idx[1] * 2 + idx[0]) ^ (at & 3), (at >> 2) ^ idx[2]
        up_t[
            pl.ds(pl.multiple_of(place * rows, rows), rows),
            pl.ds(pl.multiple_of(quarter * columns, columns), columns),
        ] = piece[0, :rows, :].astype(F32)
        unpack_layout(piece, 0, rows, up_table, quarter, place)
        first = pl.multiple_of((quarter * 4 + place) * half, half)
        for side in range(2):
            dn_t[pl.ds(first, half), columns * side : columns * (side + 1)] = piece[
                1, half * side : half * (side + 1), :
            ].astype(F32)
        unpack_layout(piece, 1, rows, dn_table, quarter, place)
    for q in range(4):
        up_l[:, thin * q : thin * (q + 1)] = up_table[q][:, :thin]
        dn_l[:, thin * q : thin * (q + 1)] = dn_table[q][:, :thin]


def attention_result_kernel(idx, *refs):
    parts, (qkv_t, out_t, qkv_l, out_l), refs = refs[:8], refs[8:12], refs[12:]
    (bt, gt, st, ubt, qvt, bl, gl, sl, ubl, qvl), (table, sums) = refs[:10], refs[10:]
    side = qkv_t.shape[1] // 2
    thin, strip, heads_l = side // 8, qkv_l.shape[1] // 8, qkv_l.shape[2]
    count = 2 * strip // 4
    rest = 16 - count
    for piece, k, quarter, place in pieces_of(parts, idx):
        x, y = quarter & 1, quarter >> 1
        eighth = y * 4 + place
        first = pl.multiple_of(x * side + eighth * thin, 16)
        for which in range(3):
            qkv_t[which, pl.ds(first, thin), :] = piece[
                k, thin * which : thin * (which + 1), :
            ].astype(F32)
        out_t[
            pl.ds(pl.multiple_of(eighth * thin, 16), thin), pl.ds(pl.multiple_of(x * side, side), side)
        ] = piece[k, 3 * thin : 4 * thin, :].astype(F32)
        last = piece[k, 4 * thin : 4 * thin + 16, :].astype(F32)
        both = jnp.concatenate(
            [last[:count, heads_l * slot : heads_l * (slot + 1)] for slot in range(4)], axis=0
        )
        for member in range(2):
            table[
                2 * x + member, pl.ds(pl.multiple_of(eighth * strip, 8), strip), :heads_l
            ] = both[strip * member : strip * (member + 1)]
        sums[x, eighth, :rest, :] = last[count:, :]
    for which in range(3):
        qkv_l[which] = table[which][:, :heads_l]
    out_l[...] = turned(table[3])[:heads_l]

    at = 0

    def take(columns):
        nonlocal at
        found = []
        for lo, hi in pieces(columns, sums.shape[3]):
            found.append(sums[0, at // rest, at % rest : at % rest + 1, : hi - lo])
            at += 1
        return jnp.concatenate(found, axis=1) if len(found) > 1 else found[0]

    wide, whole = gt.shape[1], gt.shape[1] + gl.shape[1]
    for text_out, layout_out in ((gt, gl), (st, sl), (bt, bl)):
        for row in range(2):
            value = take(whole)
            text_out[row : row + 1, :] = value[:, :wide]
            layout_out[row : row + 1, :] = value[:, wide:]
    ubt[...] = take(ubt.shape[0])[0]
    ubl[...] = take(ubl.shape[0])[0]
    for row in range(2):
        value = take(qvt.shape[1] + LANES)
        qvt[row : row + 1, :] = value[:, : qvt.shape[1]]
        qvl[row : row + 1, :] = value[:, qvt.shape[1] : qvt.shape[1] + qvl.shape[1]]


ORDER = (
    ("down4", None, 0), ("up8", None, 0), ("down8", None, 0), (4, 0, 4), (1, 0, 1), (2, 0, 2),
    ("y", None, 0), (6, 4, 2), (12, 0, 12), ("z4", None, 0), (5, 4, 1), (3, 1, 2), (8, 12, 4),
    ("z8", None, 0), (14, 12, 2), (13, 12, 1), ("even", None, 0), (9, 13, 4), (15, 13, 2), (7, 6, 1),
    ("odd", "even", 4), (11, 15, 4), ("even2", "even", 2), ("even1", "even", 1), ("odd2", "odd", 2),
    ("odd1", "odd", 1), (10, 14, 4), ("even3", "even1", 2), ("odd3", "odd2", 1),
)


def reduced_and_gathered(token, up, up_far, down_keep, down_far, keep, far):
    last = token
    coming, found = {"up8": up_far, "down4": down_far, "y": far}, {}

    def beyond(own):
        mask = 16
        while mask < lax.axis_size("seq"):
            own = own + exchange(own, mask)
            mask *= 2
        return own.astype(BF)

    def have(name, value):
        found[name] = value
        for other, source, mask in ORDER:
            if source == name and source is not None:
                coming[other] = exchange(value, mask)

    for name, _, _ in ORDER:
        last = tied(coming[name], last)
        if name == "even":
            have("even", jnp.stack([own, last]))
        else:
            have(name, last)
        if name == "down4":
            down = down_keep + last.astype(F32)
            coming["down8"] = exchange(down[1].astype(BF), 12)
        elif name == "y":
            total = keep + last.astype(F32)
            coming["z4"] = exchange(total[2:].astype(BF), 4)
        elif name == "z4":
            total = total[:2] + last.astype(F32)
            coming["z8"] = exchange(total[1].astype(BF), 12)
        elif name == "z8":
            own = beyond(total[0] + last.astype(F32))
            coming["even"] = exchange(own, 12)
        if name in ("up8", "down8") and {"up8", "down8"} <= found.keys():
            sums = up + found["up8"].astype(F32), down[0] + found["down8"].astype(F32)
            have(0, jnp.stack([beyond(piece) for piece in sums]))
    names = ("even", "odd", "even1", "odd1", "even2", "odd2", "even3", "odd3")
    return [found[at] for at in range(16)], [found[name] for name in names]


def per_device(
    text_in,
    layout_in,
    text_cot,
    layout_cot,
    doc_ids,
    span_ids,
    intersection_flags,
    text_qkv,
    text_qv_bias,
    text_out,
    text_out_bias,
    text_gains,
    text_shifts,
    text_up,
    text_up_bias,
    text_down,
    layout_qkv,
    layout_qv_bias,
    layout_out,
    layout_out_bias,
    layout_gains,
    layout_shifts,
    layout_up,
    layout_up_bias,
    layout_down,
):
    rows, wide = text_in.shape
    thin = layout_in.shape[1]
    whole = wide + thin
    width, width_l = text_qkv.shape[2], layout_qkv.shape[2]
    padded = width + LANES
    units, units_l = text_up.shape[1], layout_up.shape[1]
    half = rows // 2
    place = lax.axis_index("seq")
    idx = jnp.stack(
        [place & 1, (place >> 1) & 1, (place >> 2) & 3, lax.axis_index("tensor")]
    ).astype(jnp.int32)

    layout_turned, cot_turned, down_turned = layout_in.T, layout_cot.T, layout_down.T
    own_key = (doc_ids * 65536 + span_ids).astype(F32)[None, :]
    text_other, layout_other = exchange(text_in, 1), exchange(layout_turned, 1)
    keys = jnp.concatenate([own_key, exchange(own_key, 1)], axis=1)
    sent = shape((rows, wide + 2 * LANES), F32)

    cot_rows, keep_rows, pack, quarters = call(
        pack_kernel,
        [
            shape((rows, thin), BF),
            shape((rows, LANES), F32),
            shape((16, units), F32),
            shape((thin, 2 * LANES), BF),
        ],
        idx, cot_turned, intersection_flags[None, :], text_out_bias, text_gains, text_shifts,
        text_up_bias, layout_out_bias, layout_gains, layout_shifts,
        layout_up_bias, layout_up, down_turned, smem=1, far=range(1, 13), pin=range(4),
    )
    qkv_weights = (text_qkv, text_qv_bias, layout_qkv, layout_qv_bias)
    q_own, k_own, v_own, layout_rows = call(
        project_kernel,
        [shape((rows, padded), BF)] * 3 + [shape((rows, thin), BF)],
        text_in, layout_turned, *qkv_weights, pin=range(4), after=[pack], far=range(6),
    )
    attended, k_all, v_all = call(
        attend_kernel,
        [sent] + [shape((2 * rows, padded), BF)] * 2,
        q_own, k_own, v_own, text_other, layout_other, *qkv_weights, keys, text_out, layout_out,
        scratch=[pltpu.VMEM((rows, padded), BF)], pin=[1, 2],
    )
    hidden, normed, inverse, low_mine, low = call(
        norm_kernel,
        [
            shape((rows, whole), F32),
            shape((rows, whole), F32),
            shape((rows, 2 * LANES), F32),
            shape((half, wide + 2 * LANES), BF),
            shape((rows, wide + 2 * LANES), BF),
        ],
        idx, text_in, layout_rows, attended, over_cores(attended), pack, smem=1, pin=[0, 1, 2, 4],
    )
    slope_t, slope_l, ffn = call(
        ffn_kernel,
        [shape((rows, units), F32), shape((rows, units_l), F32), sent],
        low, pack, text_up, text_down, layout_up, down_turned, flops=14 * 10**8, room=20, pin=[0, 1],
    )
    ffn_back = over_cores(ffn)
    low_x, low_y = exchange(low_mine, 1), exchange(low_mine, 2)
    (
        text_result, layout_result, second, grad_low, grad_mine, sums_two, hidden_part, bias_t, bias_l,
    ) = call(
        turning_kernel,
        [
            shape((rows, wide), BF),
            shape((thin, rows), BF),
            shape((rows, whole), F32),
            shape((rows, wide + 2 * LANES), BF),
            shape((half, wide + 2 * LANES), BF),
            shape((3, whole), F32),
            sent,
            shape((1, units), F32),
            shape((1, units_l), F32),
        ],
        idx, hidden, ffn, ffn_back, text_cot, cot_rows, keep_rows, pack, slope_t, slope_l, text_up,
        text_down, layout_up, down_turned, smem=1, pin=[2, 3, 5, 7, 8], flops=14 * 10**8, room=20,
    )
    grad_x, grad_y = exchange(grad_mine, 1), exchange(grad_mine, 2)
    low_x, low_y = tied(low_x, grad_mine), tied(low_y, grad_mine)
    low_xy = exchange(low_x, 2)
    hidden_back = over_cores(tied(tied(hidden_part, low_x), low_y))
    grad_y = tied(grad_y, hidden_part)
    grad_xy = exchange(grad_y, 1)
    first, attended_grad, attended_mine, small = call(
        first_norm_kernel,
        [
            shape((rows, whole), F32),
            shape((rows, whole), BF),
            shape((half, whole), BF),
            shape((32, width), F32),
        ],
        idx, second, hidden_part, hidden_back, normed, inverse, pack, sums_two, bias_t, bias_l, smem=1, pin=[0, 1],
        after=[grad_y],
    )
    attended_far, small_other = exchange(attended_mine, 1), exchange(small, 1)
    low_far = [low_x, low_y, tied(low_xy, small)]
    low_back = over_cores(jnp.concatenate(low_far, axis=0))
    small_other = tied(small_other, low_far[2])
    grad_x = tied(grad_x, small_other)
    grad_far = [grad_x, grad_y, tied(grad_xy, grad_x)]
    low_parts = [low, *low_far, low_back]
    grad_parts = [grad_low, *grad_far, over_cores(jnp.concatenate(grad_far, axis=0))]
    block = (2, wide // 4 + 16, width)
    up_keep, up_send, activated, grad_rows = call(
        unit_grads_kernel,
        [
            shape(block, F32),
            shape(block, BF),
            shape((4 * rows, units // 4 + LANES), BF),
            shape((4 * rows, wide + 2 * LANES), BF),
        ],
        idx, *low_parts, *grad_parts, text_up, text_down, quarters, pack,
        scratch=[
            pltpu.VMEM((4 * rows, wide + 2 * LANES), BF),
            pltpu.VMEM((wide, units // 4), BF),
            pltpu.VMEM((units // 4, wide), BF),
            pltpu.VMEM((thin, 2 * LANES), BF),
            pltpu.VMEM((16, units), F32),
            pltpu.VMEM((4,) + block[1:], F32),
            pltpu.SemaphoreType.DMA((14,)),
        ],
        smem=1, anys=range(1, 15), flops=18 * 10**8, room=24, pin=[2, 3],
    )
    up_far = exchange(up_send, 4)
    attended_far = tied(attended_far, up_send)
    attended_back = over_cores(attended_far)
    down_keep, down_send = call(
        down_grads_kernel,
        [shape(block, F32), shape(block, BF)],
        idx, activated, grad_rows, scratch=[pltpu.VMEM((4,) + block[1:], F32)], smem=1,
        flops=7 * 10**8, after=[attended_far],
    )
    down_far = exchange(down_send, 4)

    dq, dk, dv, context, attended_grad_other = call(
        attention_back_kernel,
        [shape((2 * rows, padded), BF)] * 4 + [shape((rows, whole), BF)],
        idx, k_all, v_all, text_in, layout_turned, text_other, layout_other, *qkv_weights, keys,
        text_out, layout_out, attended_grad, attended_far, attended_back,
        scratch=[pltpu.VMEM((2 * rows, padded), BF)] * 2, smem=1, flops=50 * 10**8, room=24,
        pin=[0, 1, 2, 4], after=[down_send],
    )
    up_total = up_keep + tied(up_far, context).astype(F32)
    up_part = up_total[1].astype(BF)
    used = 6 * len(pieces(whole, width)) + len(pieces(units, width)) + len(pieces(units_l, width))
    block = (4,) + block[1:]
    keep, send = call(
        partial(attention_grads_kernel, used),
        [shape(block, F32), shape(block, BF)],
        idx, dq, dk, dv, context, text_in, layout_turned, text_other, layout_other, attended_grad,
        attended_grad_other, small, small_other,
        scratch=[
            pltpu.VMEM((4, thin, LANES), F32),
            pltpu.VMEM((8,) + block[1:], F32),
            pltpu.VMEM(small.shape, F32),
        ],
        smem=1, flops=10**9, room=24, after=[up_part],
    )
    send_far = exchange(send, 2)
    (input_part,) = call(
        input_part_kernel, [sent], dq, dk, dv, text_qkv, layout_qkv, flops=5 * 10**8, after=[send],
    )
    text_in_grad, layout_in_grad = call(
        input_grad_kernel,
        [shape((rows, wide), BF), shape((thin, rows), BF)],
        first, input_part, over_cores(input_part),
    )
    units_pieces, attention_pieces = reduced_and_gathered(
        keep, up_total[0], exchange(up_part, 12), down_keep, down_far, keep, send_far
    )

    up_t, up_l, down_t, down_l, token = call(
        units_result_kernel,
        [shape(a.shape, F32) for a in (text_up, layout_up, text_down, down_turned)]
        + [shape((8, LANES), F32)],
        idx, *units_pieces, scratch=[pltpu.VMEM((4, thin, LANES), F32)] * 2, smem=1,
        pin=[4], room=32,
    )
    one_row = (units,), (units_l,)
    kinds = [text_out_bias.shape] * 3 + [one_row[0], text_qv_bias.shape]
    kinds += [layout_out_bias.shape] * 3 + [one_row[1], layout_qv_bias.shape]
    (
        qkv_t, out_t, qkv_l, out_l,
        out_bias_t, gains_t, shifts_t, ub_t, qv_t, out_bias_l, gains_l, shifts_l, ub_l, qv_l,
    ) = call(
        attention_result_kernel,
        [shape(a.shape, F32) for a in (text_qkv, text_out, layout_qkv, layout_out)]
        + [shape(dims, F32) for dims in kinds],
        idx, *attention_pieces, after=[token],
        scratch=[pltpu.VMEM((4, thin, LANES), F32), pltpu.VMEM((2, 8, 8, width), F32)], smem=1,
    )
    return (
        text_result,
        layout_result.T,
        text_in_grad,
        layout_in_grad.T,
        qkv_t,
        qv_t,
        out_t,
        out_bias_t,
        gains_t,
        shifts_t,
        up_t,
        ub_t,
        down_t,
        qkv_l,
        qv_l,
        out_l,
        out_bias_l,
        gains_l,
        shifts_l,
        up_l,
        ub_l,
        down_l.T,
    )


def solution(mesh):
    rows, both, halves = P("seq", None), P(), P("tensor", None)
    stack, columns, one = P(None, None, "tensor"), P(None, "tensor"), P("tensor")
    weights_in = (stack, columns, halves, both, both, both, columns, one, halves)
    return jax.shard_map(
        per_device,
        mesh=mesh,
        in_specs=(rows,) * 4 + (P("seq"),) * 3 + weights_in * 2,
        out_specs=(rows,) * 4 + weights_in * 2,
        check_vma=False,
    )
```

```python
from functools import partial

import jax
import jax.numpy as jnp
from jax import lax
from jax.experimental import pallas as pl
from jax.experimental.pallas import tpu as pltpu
from jax.sharding import PartitionSpec as P

HT = 64
HL = 16
EPS = 1e-06
NEG = -1e30
BF = jnp.bfloat16
F32 = jnp.float32
LANES = 128


def exchange(shard, mask, axis="seq"):
    return lax.ppermute(shard, axis, [(i, i ^ mask) for i in range(lax.axis_size(axis))])


def over_cores(shard):
    return exchange(shard, 1, "tensor")


def dot(left, right):
    return lax.dot_general(left, right, (((1,), (0,)), ((), ())), preferred_element_type=F32)


def dot_nt(left, right):
    return lax.dot_general(left, right, (((1,), (1,)), ((), ())), preferred_element_type=F32)


def dot_tn(left, right):
    return lax.dot_general(left, right, (((0,), (0,)), ((), ())), preferred_element_type=F32)


def tied(shard, token):
    return lax.optimization_barrier((shard, token))[0]


def call(kernel, outs, *args, scratch=(), smem=0, anys=(), far=(), pin=(), after=(), flops=10**8, room=16):
    far, pin = list(far), list(pin)
    n_in = len(args)
    args = (*args, *after)
    specs, given = [], []
    for at, arg in enumerate(args):
        if at < smem:
            specs.append(pl.BlockSpec(memory_space=pltpu.SMEM))
        elif at in far:
            specs.append(pl.BlockSpec(memory_space=pltpu.HBM))
            arg = pltpu.with_memory_space_constraint(arg, pltpu.HBM)
        elif at in anys or at >= n_in:
            specs.append(pl.BlockSpec(memory_space=pl.ANY))
        else:
            specs.append(pl.BlockSpec(memory_space=pltpu.VMEM))
        if isinstance(arg, Near):
            arg = pltpu.with_memory_space_constraint(arg.value, pltpu.VMEM)
        given.append(arg)
    moved = sum(a.size * a.dtype.itemsize for a in args) + sum(
        o.size * o.dtype.itemsize for o in outs
    )
    stage = [pltpu.VMEM(args[k].shape, args[k].dtype) for k in far]
    if stage:
        stage.append(pltpu.SemaphoreType.DMA((len(far),)))

    def body(*refs):
        refs = list(refs[:n_in] + refs[len(args) :])
        if not stage:
            return kernel(*refs)
        held, sems = refs[-len(stage) : -1], refs[-1]
        refs = refs[: -len(stage)]
        coming = [
            pltpu.make_async_copy(refs[k], held[at], sems.at[at]) for at, k in enumerate(far)
        ]
        for copy in coming:
            copy.start()
        for copy in coming:
            copy.wait()
        for at, k in enumerate(far):
            refs[k] = held[at]
        kernel(*refs)

    found = pl.pallas_call(
        body,
        out_shape=tuple(
            pltpu.VMEM(o.shape, o.dtype) if k in pin else o for k, o in enumerate(outs)
        ),
        in_specs=specs,
        out_specs=tuple(pl.BlockSpec(memory_space=pltpu.VMEM) for _ in outs),
        scratch_shapes=list(scratch) + stage,
        compiler_params=pltpu.CompilerParams(vmem_limit_bytes=room * 1024 * 1024),
        cost_estimate=pl.CostEstimate(flops=flops, bytes_accessed=moved, transcendentals=0),
    )(*given)
    return tuple(Near(a) if k in pin else a for k, a in enumerate(found))


class Near:
    def __init__(self, value):
        self.value = value
        self.shape, self.dtype, self.size = value.shape, value.dtype, value.size


def shape(dims, dtype):
    return jax.ShapeDtypeStruct(tuple(dims), dtype)


def project_rows(text_rows, layout_columns, weight_t, bias_t, weight_l, bias_l, which, write):
    text_part = dot(text_rows, weight_t[which])
    layout_part = dot_tn(layout_columns, weight_l[which])
    if which != 1:
        row = which // 2
        text_part = text_part + bias_t[row : row + 1, :].astype(F32)
        layout_part = layout_part + bias_l[row : row + 1, :].astype(F32)
    pad = jnp.zeros((layout_part.shape[0], LANES - layout_part.shape[1]), F32)
    write(text_part.astype(BF), jnp.concatenate([layout_part, pad], axis=1).astype(BF))


def turned(matrix):
    rows, columns = matrix.shape
    matrix = matrix.astype(F32)
    if columns % LANES:
        fill = jnp.zeros((rows, -columns % LANES), F32)
        matrix = jnp.concatenate([matrix, fill], axis=1)
    if rows % LANES:
        fill = jnp.zeros((-rows % LANES, matrix.shape[1]), F32)
        matrix = jnp.concatenate([matrix, fill], axis=0)
    return matrix.T[:columns, :rows]


OB, GAIN, SHIFT, UP_T, UP_L, UP_Q = 0, 2, 4, 6, 7, 8


def pack_kernel(
    idx, cl, flags, ob_t, g_t, s_t, ub_t, ob_l, g_l, s_l, ub_l, up_l, dn_l,
    cl_out, keep_out, pack_out, quarter_out,
):
    wide, thin = ob_t.shape[1], ob_l.shape[1]
    pack_out[...] = jnp.zeros_like(pack_out)
    for first, text, layout in ((OB, ob_t, ob_l), (GAIN, g_t, g_l), (SHIFT, s_t, s_l)):
        pack_out[first : first + 2, :wide] = text[...].astype(F32)
        pack_out[first : first + 2, wide : wide + thin] = layout[...].astype(F32)
    pack_out[UP_T : UP_T + 1, :] = ub_t[...].astype(F32)[None, :]
    bias_l = ub_l[...].astype(F32)[None, :]
    pack_out[UP_L : UP_L + 1, : bias_l.shape[1]] = bias_l
    quarter = idx[1] * 2 + idx[0]
    count = up_l.shape[1] // 4

    def cut(ref):
        value = ref[:, :count].astype(F32)
        for q in range(1, 4):
            value = jnp.where(quarter == q, ref[:, count * q : count * (q + 1)].astype(F32), value)
        return value

    pack_out[UP_Q : UP_Q + 1, :count] = cut(bias_l)
    quarter_out[:, :count] = cut(up_l).astype(BF)
    quarter_out[:, LANES : LANES + count] = cut(dn_l).astype(BF)
    cl_out[...] = turned(cl[...]).astype(BF)
    keep_out[...] = jnp.broadcast_to((1 - flags[...]).astype(F32), (LANES, flags.shape[1])).T


def project_kernel(xt, xl, wt, bt, wl, bl, q_out, k_out, v_out, xl_out):
    xl_out[...] = turned(xl[...]).astype(BF)
    width = wt.shape[2]
    for which, out in enumerate((q_out, k_out, v_out)):

        def write(text_part, layout_part, out=out):
            out[:, :width] = text_part
            out[:, width:] = layout_part

        project_rows(xt[...], xl[...], wt, bt, wl, bl, which, write)


def hidden_bias(keys, columns):
    rows = keys.shape[1]
    down = jnp.broadcast_to(keys, (LANES, rows)).T
    parts = [
        jnp.where(down == keys[:, at : at + LANES], 0.0, NEG).astype(F32)
        for at in range(0, columns, LANES)
    ]
    return jnp.concatenate(parts, axis=1)


def head_mask(member, head, text_value, layout_value, axis):
    dims = (1, 2 * LANES) if axis == 1 else (2 * LANES, 1)
    at = lax.broadcasted_iota(jnp.int32, dims, axis)
    text = (at >= member * HT) & (at < (member + 1) * HT)
    layout = (at >= LANES + head * HL) & (at < LANES + (head + 1) * HL)
    return jnp.where(text, text_value, jnp.where(layout, layout_value, 0.0)).astype(F32)


def pair_of(ref, pair, width):
    return jnp.concatenate([ref[:, LANES * pair : LANES * (pair + 1)], ref[:, width:]], axis=1)


def probabilities(key_pair, query_head, bias):
    scores = dot_nt(key_pair, query_head) + bias
    weights = jnp.exp(scores - jnp.max(scores, axis=0, keepdims=True))
    return weights * (1.0 / jnp.sum(weights, axis=0, keepdims=True))


OB, GAIN, SHIFT, UP_T, UP_L, UP_Q = 0, 2, 4, 6, 7, 8
SCALE_T = HT ** (-0.5)
SCALE_L = HL ** (-0.5)


def attend_kernel(
    q_own, k_own, v_own, xt, xl, wt, bt, wl, bl, keys, out_t, out_l, part_out, k_all, v_all, context,
):
    rows, width = q_own.shape[0], wt.shape[2]
    for which, own, target in ((1, k_own, k_all), (2, v_own, v_all)):
        target[:rows, :] = own[...]

        def write(text_part, layout_part, target=target):
            target[rows:, :width] = text_part
            target[rows:, width:] = layout_part

        project_rows(xt[...], xl[...], wt, bt, wl, bl, which, write)
    bias = hidden_bias(keys[...], rows)
    layout_sum = jnp.zeros((LANES, rows), F32)
    for pair in range(width // LANES):
        query_pair, key_pair = pair_of(q_own, pair, width), pair_of(k_all, pair, width)
        value_turned = pair_of(v_all, pair, width).T
        text_sum = jnp.zeros((LANES, rows), F32)
        for member in range(2):
            head = 2 * pair + member
            mask = head_mask(member, head, SCALE_T, SCALE_L, 1).astype(BF)
            probs_low = probabilities(key_pair, query_pair * mask, bias).astype(BF)
            turned = dot(value_turned, probs_low) * head_mask(member, head, 1.0, 1.0, 0)
            text_sum += turned[:LANES]
            layout_sum += turned[LANES:]
        context[:, LANES * pair : LANES * (pair + 1)] = text_sum.T.astype(BF)
    context[:, width:] = layout_sum.T.astype(BF)
    text_width = out_t.shape[1]
    part_out[:, :text_width] = dot(context[:, :width], out_t[...])
    part_out[:, text_width : text_width + out_l.shape[1]] = dot(
        context[:, width : width + out_l.shape[0]], out_l[...]
    )


def norm_parts(total):
    center = total - jnp.mean(total, axis=1, keepdims=True)
    inverse = lax.rsqrt(jnp.mean(center * center, axis=1, keepdims=True) + EPS)
    return center * inverse, inverse


def norm_back(upstream, normed, inverse, gain):
    scaled = upstream * gain
    return inverse * (
        scaled
        - jnp.mean(scaled, axis=1, keepdims=True)
        - normed * jnp.mean(scaled * normed, axis=1, keepdims=True)
    )


def gelu_parts(before):
    share = 0.5 * (1.0 + lax.erf(before * (0.5**0.5)))
    slope = share + before * (jnp.exp(-0.5 * before * before) * 0.3989422804014327)
    return before * share, slope


def norm_kernel(
    idx, xt, xl, part, back, pack, hidden_out, normed_out, inverse_out, mine_out, low_out
):
    width, whole, half = xt.shape[1], hidden_out.shape[1], mine_out.shape[0]
    for at, (lo, hi, x) in enumerate(((0, width, xt), (width, whole, xl))):
        total = x[...].astype(F32) + (part[:, lo:hi] + back[:, lo:hi]) + pack[OB : OB + 1, lo:hi]
        normed, inverse = norm_parts(total)
        hidden = normed * pack[GAIN : GAIN + 1, lo:hi] + pack[SHIFT : SHIFT + 1, lo:hi]
        hidden_out[:, lo:hi] = hidden
        normed_out[:, lo:hi] = normed
        inverse_out[:, LANES * at : LANES * (at + 1)] = jnp.broadcast_to(
            inverse, (inverse.shape[0], LANES)
        )
        low_out[:, lo:hi] = hidden.astype(BF)
    mine_out[...] = low_out[pl.ds(pl.multiple_of(idx[3] * half, half), half), :]


def ffn_kernel(low, pack, up_t, dn_t, up_l, dn_l, slope_t, slope_l, ffn_out):
    width = up_t.shape[0]
    whole = width + up_l.shape[0]
    for lo, hi, up, ub, dn, slope_out in (
        (0, width, up_t, UP_T, dn_t, slope_t),
        (width, whole, up_l, UP_L, dn_l, slope_l),
    ):
        rows_low = low[:, lo:hi]
        units = up.shape[1]
        step = min(units, 384)
        total = None
        for cut in range(0, units, step):
            before = dot(rows_low, up[:, cut : cut + step]) + pack[ub : ub + 1, cut : cut + step]
            activated, slope = gelu_parts(before)
            slope_out[:, cut : cut + step] = slope
            if lo == 0:
                term = dot(activated.astype(BF), dn[cut : cut + step, :])
            else:
                term = dot_nt(activated.astype(BF), dn[:, cut : cut + step])
            total = term if total is None else total + term
        ffn_out[:, lo:hi] = total


def second_norm_kernel(
    idx, hidden, part, back, ct, cl, keep, pack,
    rt_out, rl_out, second_out, low_out, mine_out, sums_out,
):
    width, whole = ct.shape[1], hidden.shape[1]
    half = mine_out.shape[0]
    for lo, hi, cot, result in ((0, width, ct, rt_out), (width, whole, cl, rl_out)):
        total = (
            hidden[:, lo:hi] + (part[:, lo:hi] + back[:, lo:hi]) + pack[OB + 1 : OB + 2, lo:hi]
        )
        normed, inverse = norm_parts(total)
        gain = pack[GAIN + 1 : GAIN + 2, lo:hi]
        value = normed * gain + pack[SHIFT + 1 : SHIFT + 2, lo:hi]
        result[...] = (value if lo == 0 else turned(value)).astype(BF)
        upstream = cot[...].astype(F32) * keep[:, :1]
        grad = norm_back(upstream, normed, inverse, gain)
        second_out[:, lo:hi] = grad
        low = grad.astype(BF)
        low_out[:, lo:hi] = low
        sums_out[0:1, lo:hi] = jnp.sum(upstream * normed, axis=0, keepdims=True)
        sums_out[1:2, lo:hi] = jnp.sum(upstream, axis=0, keepdims=True)
        sums_out[2:3, lo:hi] = jnp.sum(low.astype(F32), axis=0, keepdims=True)
    mine_out[...] = low_out[pl.ds(pl.multiple_of(idx[3] * half, half), half), :]


def ffn_back_kernel(grad, slope_t, slope_l, up_t, dn_t, up_l, dn_l, part_out, bias_t, bias_l):
    width = up_t.shape[0]
    whole = width + up_l.shape[0]
    for lo, hi, slope, up, dn, bias in (
        (0, width, slope_t, up_t, dn_t, bias_t),
        (width, whole, slope_l, up_l, dn_l, bias_l),
    ):
        rows = grad[:, lo:hi]
        units = up.shape[1]
        step = min(units, 384)
        total = None
        for cut in range(0, units, step):
            if lo == 0:
                act_grad = dot_nt(rows, dn[cut : cut + step, :])
            else:
                act_grad = dot(rows, dn[:, cut : cut + step])
            before_grad = (act_grad * slope[:, cut : cut + step]).astype(BF)
            bias[:, cut : cut + step] = jnp.sum(before_grad.astype(F32), axis=0, keepdims=True)
            term = dot_nt(before_grad, up[:, cut : cut + step])
            total = term if total is None else total + term
        part_out[:, lo:hi] = total


def turning_kernel(
    idx, hidden, part, back, ct, cl, keep, pack, slope_t, slope_l, up_t, dn_t, up_l, dn_l,
    rt_out, rl_out, second_out, low_out, mine_out, sums_out, part_out, bias_t, bias_l,
):
    second_norm_kernel(
        idx, hidden, part, back, ct, cl, keep, pack,
        rt_out, rl_out, second_out, low_out, mine_out, sums_out,
    )
    ffn_back_kernel(
        low_out, slope_t, slope_l, up_t, dn_t, up_l, dn_l, part_out, bias_t, bias_l
    )


def pieces(columns, piece):
    return [(at, min(at + piece, columns)) for at in range(0, columns, piece)]


def first_norm_kernel(
    idx, second, part, back, normed_in, inverse_in, pack, sums_two, bias_t, bias_l,
    first_out, low_out, mine_out, small_out,
):
    whole, piece = second.shape[1], small_out.shape[1]
    width = whole * 4 // 5
    small_out[...] = jnp.zeros_like(small_out)
    row = 0

    def put(value):
        nonlocal row
        for lo, hi in pieces(value.shape[1], piece):
            small_out[row : row + 1, : hi - lo] = value[:, lo:hi]
            row += 1

    sums = [[], [], []]
    for at, (lo, hi) in enumerate(((0, width), (width, whole))):
        upstream = second[:, lo:hi] + (part[:, lo:hi] + back[:, lo:hi])
        normed = normed_in[:, lo:hi]
        inverse = inverse_in[:, LANES * at : LANES * at + 1]
        grad = norm_back(upstream, normed, inverse, pack[GAIN : GAIN + 1, lo:hi])
        first_out[:, lo:hi] = grad
        low = grad.astype(BF)
        low_out[:, lo:hi] = low
        sums[0].append(jnp.sum(upstream * normed, axis=0, keepdims=True))
        sums[1].append(jnp.sum(upstream, axis=0, keepdims=True))
        sums[2].append(jnp.sum(low.astype(F32), axis=0, keepdims=True))
    half = mine_out.shape[0]
    mine_out[...] = low_out[pl.ds(pl.multiple_of(idx[3] * half, half), half), :]
    for kind in range(3):
        put(jnp.concatenate(sums[kind], axis=1))
        put(sums_two[kind : kind + 1, :])
    put(bias_t[...])
    put(bias_l[...])


def unit_grads_kernel(idx, *refs):
    (
        low_parts, grad_parts, (up_t, dn_t, quarters, pack_in),
        (keep, send, act_out, grad),
        (low, w_up, w_dn, w_l, pack, held, sems),
    ) = refs[:5], refs[5:10], refs[10:14], refs[14:18], refs[18:]
    quarter = idx[1] * 2 + idx[0]
    zz = idx[2]
    copies = []
    for parts, target in ((low_parts, low), (grad_parts, grad)):
        at = 0
        for part in parts:
            count = part.shape[0]
            copies.append((part, target.at[pl.ds(at, count), :]))
            at += count
    units = w_dn.shape[0]
    start = pl.multiple_of(quarter * units, units)
    copies.append((up_t.at[:, pl.ds(start, units)], w_up))
    copies.append((dn_t.at[pl.ds(start, units), :], w_dn))
    copies += [(quarters, w_l), (pack_in, pack)]
    copies = [pltpu.make_async_copy(s, d, sems.at[k]) for k, (s, d) in enumerate(copies)]
    for c in copies:
        c.start()
    for c in copies:
        c.wait()
    width = w_up.shape[0]
    piece = width // 4

    def grads(lo, hi, up, bias, down):
        before = dot(low[:, lo:hi], up) + bias
        activated, slope = gelu_parts(before)
        act_grad = dot_nt(grad[:, lo:hi], down) if lo == 0 else dot(grad[:, lo:hi], down)
        before_grad = (act_grad * slope).astype(BF)
        return activated.astype(BF), before_grad

    whole = width + w_l.shape[0]
    count = w_l.shape[0] // 2
    act_t, back_t = grads(
        0, width, w_up[...], pack[UP_T : UP_T + 1, pl.ds(start, units)], w_dn[...]
    )
    act_l, back_l = grads(
        width,
        whole,
        w_l[:, :count],
        pack[UP_Q : UP_Q + 1, :count],
        w_l[:, LANES : LANES + count],
    )

    act_out[:, :units] = act_t
    act_out[:, units:] = widened(act_l)
    up_grad = dot_tn(low[:, :width], back_t)
    for k in range(4):
        held[k ^ zz, :piece, :] = up_grad[piece * k : piece * (k + 1)]
    place_layout(held, zz, dot_tn(low[:, width:whole], widened(back_l)))
    hand_out(held, keep, send)


def widened(matrix):
    pad = jnp.zeros((matrix.shape[0], LANES - matrix.shape[1]), matrix.dtype)
    return jnp.concatenate([matrix, pad], axis=1)


def place_layout(held, zz, matrix):
    piece = held.shape[1] - 16
    for k in range(4):
        for slot in range(3):
            first = 16 * (3 * k + slot)
            held[k ^ zz, piece:, LANES * slot : LANES * (slot + 1)] = matrix[first : first + 16]


def hand_out(held, keep, send):
    for k in range(2):
        keep[k] = held[3 * k]
        send[k] = held[1 + k].astype(BF)


def down_grads_kernel(idx, act, grad, keep, send, held):
    zz = idx[2]
    units, width = held.shape[2], 2 * held.shape[2]
    down_grad = dot_tn(act[:, :units], grad[:, :width])
    part = (held.shape[1] - 16) // 2
    for k in range(4):
        for side in range(2):
            held[k ^ zz, part * side : part * (side + 1), :] = down_grad[
                part * k : part * (k + 1), units * side : units * (side + 1)
            ]
    place_layout(held, zz, dot_tn(grad[:, width : width + width // 4], act[:, units:]))
    hand_out(held, keep, send)


def attention_back_kernel(
    idx, k_all, v_all, xt, xl, xt_p, xl_p, wt, bt, wl, bl, keys, out_t, out_l, ag_own, ag_far, ag_back,
    dq, dk, dv, context, ag_p, q_all, g_all,
):
    rows, width = xt.shape[0], wt.shape[2]
    wide = out_t.shape[1]
    half = ag_far.shape[0]
    core = idx[3]
    ag_p[pl.ds(pl.multiple_of(core * half, half), half), :] = ag_far[...]
    ag_p[pl.ds(pl.multiple_of((1 - core) * half, half), half), :] = ag_back[...]
    for at, text_rows, layout_columns in ((0, xt, xl), (rows, xt_p, xl_p)):

        def write(text_part, layout_part, at=at):
            q_all[at : at + rows, :width] = text_part
            q_all[at : at + rows, width:] = layout_part

        project_rows(text_rows[...], layout_columns[...], wt, bt, wl, bl, 0, write)
    for at, grad in ((0, ag_own), (rows, ag_p)):
        g_all[at : at + rows, :width] = dot_nt(grad[:, :wide], out_t[...]).astype(BF)
        layout_grad = dot_nt(grad[:, wide:], out_l[...])
        pad = jnp.zeros((rows, LANES - layout_grad.shape[1]), F32)
        g_all[at : at + rows, width:] = jnp.concatenate([layout_grad, pad], axis=1).astype(BF)
    bias = hidden_bias(keys[...], 2 * rows)
    zero_turned, zero = jnp.zeros((LANES, 2 * rows), F32), jnp.zeros((2 * rows, LANES), F32)
    layout_context, layout_dq, layout_dk, layout_dv = zero_turned, zero_turned, zero, zero
    for pair in range(width // LANES):
        query_pair, key_pair = pair_of(q_all, pair, width), pair_of(k_all, pair, width)
        grad_pair, value_pair = pair_of(g_all, pair, width), pair_of(v_all, pair, width)
        key_turned, value_turned = key_pair.T, value_pair.T
        text_context, text_dq, text_dk, text_dv = zero_turned, zero_turned, zero, zero
        for member in range(2):
            head = 2 * pair + member
            query_head = query_pair * head_mask(member, head, SCALE_T, SCALE_L, 1).astype(BF)
            grad_head = grad_pair * head_mask(member, head, 1.0, 1.0, 1).astype(BF)
            probs = probabilities(key_pair, query_head, bias)
            probs_low = probs.astype(BF)
            prob_grads = dot_nt(value_pair, grad_head)
            delta = jnp.sum(probs * prob_grads, axis=0, keepdims=True)
            score_grads = (probs * (prob_grads - delta)).astype(BF)
            value_part = dot(probs_low, grad_head)
            text_dv += value_part[:, :LANES]
            layout_dv += value_part[:, LANES:]
            key_part = dot(score_grads, query_head)
            text_dk += key_part[:, :LANES]
            layout_dk += key_part[:, LANES:]
            query_part = dot(key_turned, score_grads) * head_mask(member, head, SCALE_T, SCALE_L, 0)
            text_dq += query_part[:LANES]
            layout_dq += query_part[LANES:]
            context_part = dot(value_turned, probs_low) * head_mask(member, head, 1.0, 1.0, 0)
            text_context += context_part[:LANES]
            layout_context += context_part[LANES:]
        columns = slice(LANES * pair, LANES * (pair + 1))
        context[:, columns] = text_context.T.astype(BF)
        dq[:, columns] = text_dq.T.astype(BF)
        dk[:, columns] = text_dk.astype(BF)
        dv[:, columns] = text_dv.astype(BF)
    context[:, width:] = layout_context.T.astype(BF)
    dq[:, width:] = layout_dq.T.astype(BF)
    dk[:, width:] = layout_dk.astype(BF)
    dv[:, width:] = layout_dv.astype(BF)


def input_part_kernel(dq, dk, dv, wt, wl, part_out):
    rows, width, heads_l = part_out.shape[0], wt.shape[2], wl.shape[2]
    wide = wt.shape[1]
    total_t = total_l = None
    for which, grad in enumerate((dq, dk, dv)):
        term_t = dot_nt(grad[:rows, :width], wt[which])
        term_l = dot_nt(grad[:rows, width : width + heads_l], wl[which])
        total_t = term_t if which == 0 else total_t + term_t
        total_l = term_l if which == 0 else total_l + term_l
    part_out[:, :wide] = total_t
    part_out[:, wide : wide + wl.shape[1]] = total_l


def input_grad_kernel(first, part, back, text_out, layout_out):
    wide, whole = text_out.shape[1], first.shape[1]
    text_out[...] = (first[:, :wide] + (part[:, :wide] + back[:, :wide])).astype(BF)
    layout_out[...] = turned(
        first[:, wide:] + (part[:, wide:whole] + back[:, wide:whole])
    ).astype(BF)


def attention_grads_kernel(
    row, idx, dq, dk, dv, context, xt, xl, xt_p, xl_p, ag_own, ag_p, small, small_p,
    keep_out, send_out, matrices, held, sums,
):
    wide, rows = xt.shape[1], xt.shape[0]
    width = keep_out.shape[2]
    bx, by, zz = idx[0], idx[1], idx[2]
    side = wide // 2
    start = pl.multiple_of(bx * side, side)
    thin = side // 8

    def over_rows(left_own, left_other, right):
        both = jnp.concatenate([left_own, left_other], axis=0)
        return dot_tn(both, right)

    def place(matrix, lowest):
        for y in range(2):
            for z in range(4):
                first = thin * (4 * y + z)
                held[(y ^ by) * 4 + (z ^ zz), lowest : lowest + thin, :] = matrix[
                    first : first + thin
                ]

    x_side = jnp.concatenate([xt[:, pl.ds(start, side)], xt_p[:, pl.ds(start, side)]], axis=0)
    for which, grad in enumerate((dq, dk, dv)):
        place(dot_tn(x_side, grad[:, :width]), thin * which)
        matrices[which] = dot(xl[...], grad[:rows, width:]) + dot(xl_p[...], grad[rows:, width:])
    ag_side = jnp.concatenate([ag_own[:, pl.ds(start, side)], ag_p[:, pl.ds(start, side)]], axis=0)
    place(dot_tn(context[:, :width], ag_side), 3 * thin)
    ag_l = jnp.concatenate([ag_own[:, wide:], ag_p[:, wide:]], axis=0)
    matrices[3] = dot_tn(ag_l, context[:, width:])
    sums[...] = small[...] + small_p[...]
    for grad in (dq, dv):
        total = jnp.sum(grad[...].astype(F32), axis=0, keepdims=True)
        for lo, hi in pieces(total.shape[1], width):
            sums[row : row + 1, : hi - lo] = total[:, lo:hi]
            row += 1
    left, right = matrices[2 * bx], matrices[2 * bx + 1]
    strip = left.shape[0] // 8
    for y in range(2):
        for z in range(4):
            eighth = 4 * y + z
            first = strip * eighth
            both = jnp.concatenate(
                [left[first : first + strip], right[first : first + strip]], axis=0
            )[:, : width // 4]
            count = 2 * strip // 4
            packed = jnp.concatenate(
                [both[count * slot : count * (slot + 1)] for slot in range(4)], axis=1
            )
            rest = 16 - count
            held[(y ^ by) * 4 + (z ^ zz), 4 * thin : 4 * thin + 16, :] = jnp.concatenate(
                [packed, sums[rest * eighth : rest * (eighth + 1), :]], axis=0
            )
    for at, k in enumerate((0, 3, 1, 2)):
        keep_out[at] = held[k]
        send_out[at] = held[4 + k].astype(BF)


def pieces_of(refs, idx):
    for at in range(4):
        for group in range(2):
            for k in range(2):
                yield refs[2 * at + group], k, (idx[1] * 2 + idx[0]) ^ at, (3 * k) ^ group ^ idx[2]


def unpack_layout(piece, k, lowest, table, quarter, place):
    for slot in range(3):
        first = pl.multiple_of(place * 48 + 16 * slot, 16)
        table[quarter, pl.ds(first, 16), :] = piece[
            k, lowest : lowest + 16, LANES * slot : LANES * (slot + 1)
        ].astype(F32)


def units_result_kernel(idx, *refs):
    parts, (up_t, up_l, dn_t, dn_l, token), (up_table, dn_table) = refs[:16], refs[16:21], refs[21:]
    token[...] = jnp.zeros_like(token)
    rows, columns = up_t.shape[0] // 4, up_t.shape[1] // 4
    thin = up_l.shape[1] // 4
    half = rows // 2
    for at, piece in enumerate(parts):
        quarter, place = (idx[1] * 2 + idx[0]) ^ (at & 3), (at >> 2) ^ idx[2]
        up_t[
            pl.ds(pl.multiple_of(place * rows, rows), rows),
            pl.ds(pl.multiple_of(quarter * columns, columns), columns),
        ] = piece[0, :rows, :].astype(F32)
        unpack_layout(piece, 0, rows, up_table, quarter, place)
        first = pl.multiple_of((quarter * 4 + place) * half, half)
        for side in range(2):
            dn_t[pl.ds(first, half), columns * side : columns * (side + 1)] = piece[
                1, half * side : half * (side + 1), :
            ].astype(F32)
        unpack_layout(piece, 1, rows, dn_table, quarter, place)
    for q in range(4):
        up_l[:, thin * q : thin * (q + 1)] = up_table[q][:, :thin]
        dn_l[:, thin * q : thin * (q + 1)] = dn_table[q][:, :thin]


def attention_result_kernel(idx, *refs):
    parts, (qkv_t, out_t, qkv_l, out_l), refs = refs[:8], refs[8:12], refs[12:]
    (bt, gt, st, ubt, qvt, bl, gl, sl, ubl, qvl), (table, sums) = refs[:10], refs[10:]
    side = qkv_t.shape[1] // 2
    thin, strip, heads_l = side // 8, qkv_l.shape[1] // 8, qkv_l.shape[2]
    count = 2 * strip // 4
    rest = 16 - count
    for piece, k, quarter, place in pieces_of(parts, idx):
        x, y = quarter & 1, quarter >> 1
        eighth = y * 4 + place
        first = pl.multiple_of(x * side + eighth * thin, 16)
        for which in range(3):
            qkv_t[which, pl.ds(first, thin), :] = piece[
                k, thin * which : thin * (which + 1), :
            ].astype(F32)
        out_t[
            pl.ds(pl.multiple_of(eighth * thin, 16), thin), pl.ds(pl.multiple_of(x * side, side), side)
        ] = piece[k, 3 * thin : 4 * thin, :].astype(F32)
        last = piece[k, 4 * thin : 4 * thin + 16, :].astype(F32)
        both = jnp.concatenate(
            [last[:count, heads_l * slot : heads_l * (slot + 1)] for slot in range(4)], axis=0
        )
        for member in range(2):
            table[
                2 * x + member, pl.ds(pl.multiple_of(eighth * strip, 8), strip), :heads_l
            ] = both[strip * member : strip * (member + 1)]
        sums[x, eighth, :rest, :] = last[count:, :]
    for which in range(3):
        qkv_l[which] = table[which][:, :heads_l]
    out_l[...] = turned(table[3])[:heads_l]

    at = 0

    def take(columns):
        nonlocal at
        found = []
        for lo, hi in pieces(columns, sums.shape[3]):
            found.append(sums[0, at // rest, at % rest : at % rest + 1, : hi - lo])
            at += 1
        return jnp.concatenate(found, axis=1) if len(found) > 1 else found[0]

    wide, whole = gt.shape[1], gt.shape[1] + gl.shape[1]
    for text_out, layout_out in ((gt, gl), (st, sl), (bt, bl)):
        for row in range(2):
            value = take(whole)
            text_out[row : row + 1, :] = value[:, :wide]
            layout_out[row : row + 1, :] = value[:, wide:]
    ubt[...] = take(ubt.shape[0])[0]
    ubl[...] = take(ubl.shape[0])[0]
    for row in range(2):
        value = take(qvt.shape[1] + LANES)
        qvt[row : row + 1, :] = value[:, : qvt.shape[1]]
        qvl[row : row + 1, :] = value[:, qvt.shape[1] : qvt.shape[1] + qvl.shape[1]]


ORDER = (
    ("down4", None, 0), ("up8", None, 0), ("down8", None, 0), (4, 0, 4), ("y", None, 0), (1, 0, 1),
    (12, 0, 12), (2, 0, 2), ("z4", None, 0), (5, 4, 1), (6, 4, 2), (13, 12, 1), (8, 12, 4), (7, 6, 1),
    (14, 12, 2), ("z8", None, 0), (3, 2, 1), (9, 8, 1), ("even", None, 0), (15, 13, 2), (10, 14, 4),
    ("odd", "even", 4), (11, 15, 4), ("even2", "even", 2), ("even1", "even", 1), ("odd2", "odd", 2),
    ("odd1", "even1", 4), ("even3", "even1", 2), ("odd3", "odd2", 1),
)


def reduced_and_gathered(token, up, up_far, down_keep, down_far, keep, far):
    last = token
    coming, found = {"up8": up_far, "down4": down_far, "y": far}, {}

    def beyond(own):
        mask = 16
        while mask < lax.axis_size("seq"):
            own = own + exchange(own, mask)
            mask *= 2
        return own.astype(BF)

    def have(name, value):
        found[name] = value
        for other, source, mask in ORDER:
            if source == name and source is not None:
                coming[other] = exchange(value, mask)

    for name, _, _ in ORDER:
        last = tied(coming[name], last)
        if name == "even":
            have("even", jnp.stack([own, last]))
        else:
            have(name, last)
        if name == "down4":
            down = down_keep + last.astype(F32)
            coming["down8"] = exchange(down[1].astype(BF), 12)
        elif name == "y":
            total = keep + last.astype(F32)
            coming["z4"] = exchange(total[2:].astype(BF), 4)
        elif name == "z4":
            total = total[:2] + last.astype(F32)
            coming["z8"] = exchange(total[1].astype(BF), 12)
        elif name == "z8":
            own = beyond(total[0] + last.astype(F32))
            coming["even"] = exchange(own, 12)
        if name in ("up8", "down8") and {"up8", "down8"} <= found.keys():
            sums = up + found["up8"].astype(F32), down[0] + found["down8"].astype(F32)
            have(0, jnp.stack([beyond(piece) for piece in sums]))
    names = ("even", "odd", "even1", "odd1", "even2", "odd2", "even3", "odd3")
    return [found[at] for at in range(16)], [found[name] for name in names]


def per_device(
    text_in,
    layout_in,
    text_cot,
    layout_cot,
    doc_ids,
    span_ids,
    intersection_flags,
    text_qkv,
    text_qv_bias,
    text_out,
    text_out_bias,
    text_gains,
    text_shifts,
    text_up,
    text_up_bias,
    text_down,
    layout_qkv,
    layout_qv_bias,
    layout_out,
    layout_out_bias,
    layout_gains,
    layout_shifts,
    layout_up,
    layout_up_bias,
    layout_down,
):
    rows, wide = text_in.shape
    thin = layout_in.shape[1]
    whole = wide + thin
    width, width_l = text_qkv.shape[2], layout_qkv.shape[2]
    padded = width + LANES
    units, units_l = text_up.shape[1], layout_up.shape[1]
    half = rows // 2
    place = lax.axis_index("seq")
    idx = jnp.stack(
        [place & 1, (place >> 1) & 1, (place >> 2) & 3, lax.axis_index("tensor")]
    ).astype(jnp.int32)

    layout_turned, cot_turned, down_turned = layout_in.T, layout_cot.T, layout_down.T
    own_key = (doc_ids * 65536 + span_ids).astype(F32)[None, :]
    text_other, layout_other = exchange(text_in, 1), exchange(layout_turned, 1)
    keys = jnp.concatenate([own_key, exchange(own_key, 1)], axis=1)
    sent = shape((rows, wide + 2 * LANES), F32)

    cot_rows, keep_rows, pack, quarters = call(
        pack_kernel,
        [
            shape((rows, thin), BF),
            shape((rows, LANES), F32),
            shape((16, units), F32),
            shape((thin, 2 * LANES), BF),
        ],
        idx, cot_turned, intersection_flags[None, :], text_out_bias, text_gains, text_shifts,
        text_up_bias, layout_out_bias, layout_gains, layout_shifts,
        layout_up_bias, layout_up, down_turned, smem=1, far=range(1, 13), pin=range(4),
    )
    qkv_weights = (text_qkv, text_qv_bias, layout_qkv, layout_qv_bias)
    q_own, k_own, v_own, layout_rows = call(
        project_kernel,
        [shape((rows, padded), BF)] * 3 + [shape((rows, thin), BF)],
        text_in, layout_turned, *qkv_weights, pin=range(4), after=[pack], far=range(6),
    )
    attended, k_all, v_all = call(
        attend_kernel,
        [sent] + [shape((2 * rows, padded), BF)] * 2,
        q_own, k_own, v_own, text_other, layout_other, *qkv_weights, keys, text_out, layout_out,
        scratch=[pltpu.VMEM((rows, padded), BF)], pin=[1, 2],
    )
    hidden, normed, inverse, low_mine, low = call(
        norm_kernel,
        [
            shape((rows, whole), F32),
            shape((rows, whole), F32),
            shape((rows, 2 * LANES), F32),
            shape((half, wide + 2 * LANES), BF),
            shape((rows, wide + 2 * LANES), BF),
        ],
        idx, text_in, layout_rows, attended, over_cores(attended), pack, smem=1, pin=[0, 1, 2, 4],
    )
    slope_t, slope_l, ffn = call(
        ffn_kernel,
        [shape((rows, units), F32), shape((rows, units_l), F32), sent],
        low, pack, text_up, text_down, layout_up, down_turned, flops=14 * 10**8, room=20, pin=[0, 1],
    )
    ffn_back = over_cores(ffn)
    low_x, low_y = exchange(low_mine, 1), exchange(low_mine, 2)
    (
        text_result, layout_result, second, grad_low, grad_mine, sums_two, hidden_part, bias_t, bias_l,
    ) = call(
        turning_kernel,
        [
            shape((rows, wide), BF),
            shape((thin, rows), BF),
            shape((rows, whole), F32),
            shape((rows, wide + 2 * LANES), BF),
            shape((half, wide + 2 * LANES), BF),
            shape((3, whole), F32),
            sent,
            shape((1, units), F32),
            shape((1, units_l), F32),
        ],
        idx, hidden, ffn, ffn_back, text_cot, cot_rows, keep_rows, pack, slope_t, slope_l, text_up,
        text_down, layout_up, down_turned, smem=1, pin=[2, 3, 5, 7, 8], flops=14 * 10**8, room=20,
    )
    grad_x, grad_y = exchange(grad_mine, 1), exchange(grad_mine, 2)
    low_x, low_y = tied(low_x, grad_mine), tied(low_y, grad_mine)
    low_xy = exchange(low_x, 2)
    hidden_back = over_cores(tied(tied(hidden_part, low_x), low_y))
    grad_y = tied(grad_y, hidden_part)
    grad_xy = exchange(grad_y, 1)
    first, attended_grad, attended_mine, small = call(
        first_norm_kernel,
        [
            shape((rows, whole), F32),
            shape((rows, whole), BF),
            shape((half, whole), BF),
            shape((32, width), F32),
        ],
        idx, second, hidden_part, hidden_back, normed, inverse, pack, sums_two, bias_t, bias_l, smem=1, pin=[0, 1],
        after=[grad_y],
    )
    attended_far, small_other = exchange(attended_mine, 1), exchange(small, 1)
    low_far = [low_x, low_y, tied(low_xy, small)]
    low_back = over_cores(jnp.concatenate(low_far, axis=0))
    small_other = tied(small_other, low_far[2])
    grad_x = tied(grad_x, small_other)
    grad_far = [grad_x, grad_y, tied(grad_xy, grad_x)]
    low_parts = [low, *low_far, low_back]
    grad_parts = [grad_low, *grad_far, over_cores(jnp.concatenate(grad_far, axis=0))]
    block = (2, wide // 4 + 16, width)
    up_keep, up_send, activated, grad_rows = call(
        unit_grads_kernel,
        [
            shape(block, F32),
            shape(block, BF),
            shape((4 * rows, units // 4 + LANES), BF),
            shape((4 * rows, wide + 2 * LANES), BF),
        ],
        idx, *low_parts, *grad_parts, text_up, text_down, quarters, pack,
        scratch=[
            pltpu.VMEM((4 * rows, wide + 2 * LANES), BF),
            pltpu.VMEM((wide, units // 4), BF),
            pltpu.VMEM((units // 4, wide), BF),
            pltpu.VMEM((thin, 2 * LANES), BF),
            pltpu.VMEM((16, units), F32),
            pltpu.VMEM((4,) + block[1:], F32),
            pltpu.SemaphoreType.DMA((14,)),
        ],
        smem=1, anys=range(1, 15), flops=18 * 10**8, room=24, pin=[2, 3],
    )
    up_far = exchange(up_send, 4)
    attended_far = tied(attended_far, up_send)
    attended_back = over_cores(attended_far)
    down_keep, down_send = call(
        down_grads_kernel,
        [shape(block, F32), shape(block, BF)],
        idx, activated, grad_rows, scratch=[pltpu.VMEM((4,) + block[1:], F32)], smem=1,
        flops=7 * 10**8, after=[attended_far],
    )
    down_far = exchange(down_send, 4)

    dq, dk, dv, context, attended_grad_other = call(
        attention_back_kernel,
        [shape((2 * rows, padded), BF)] * 4 + [shape((rows, whole), BF)],
        idx, k_all, v_all, text_in, layout_turned, text_other, layout_other, *qkv_weights, keys,
        text_out, layout_out, attended_grad, attended_far, attended_back,
        scratch=[pltpu.VMEM((2 * rows, padded), BF)] * 2, smem=1, flops=50 * 10**8, room=24,
        pin=[0, 1, 2, 4], after=[down_send],
    )
    up_total = up_keep + tied(up_far, context).astype(F32)
    up_part = up_total[1].astype(BF)
    used = 6 * len(pieces(whole, width)) + len(pieces(units, width)) + len(pieces(units_l, width))
    block = (4,) + block[1:]
    keep, send = call(
        partial(attention_grads_kernel, used),
        [shape(block, F32), shape(block, BF)],
        idx, dq, dk, dv, context, text_in, layout_turned, text_other, layout_other, attended_grad,
        attended_grad_other, small, small_other,
        scratch=[
            pltpu.VMEM((4, thin, LANES), F32),
            pltpu.VMEM((8,) + block[1:], F32),
            pltpu.VMEM(small.shape, F32),
        ],
        smem=1, flops=10**9, room=24, after=[up_part],
    )
    send_far = exchange(send, 2)
    (input_part,) = call(
        input_part_kernel, [sent], dq, dk, dv, text_qkv, layout_qkv, flops=5 * 10**8, after=[send],
    )
    text_in_grad, layout_in_grad = call(
        input_grad_kernel,
        [shape((rows, wide), BF), shape((thin, rows), BF)],
        first, input_part, over_cores(input_part),
    )
    units_pieces, attention_pieces = reduced_and_gathered(
        keep, up_total[0], exchange(up_part, 12), down_keep, down_far, keep, send_far
    )

    up_t, up_l, down_t, down_l, token = call(
        units_result_kernel,
        [shape(a.shape, F32) for a in (text_up, layout_up, text_down, down_turned)]
        + [shape((8, LANES), F32)],
        idx, *units_pieces, scratch=[pltpu.VMEM((4, thin, LANES), F32)] * 2, smem=1,
        pin=[4], room=32,
    )
    one_row = (units,), (units_l,)
    kinds = [text_out_bias.shape] * 3 + [one_row[0], text_qv_bias.shape]
    kinds += [layout_out_bias.shape] * 3 + [one_row[1], layout_qv_bias.shape]
    (
        qkv_t, out_t, qkv_l, out_l,
        out_bias_t, gains_t, shifts_t, ub_t, qv_t, out_bias_l, gains_l, shifts_l, ub_l, qv_l,
    ) = call(
        attention_result_kernel,
        [shape(a.shape, F32) for a in (text_qkv, text_out, layout_qkv, layout_out)]
        + [shape(dims, F32) for dims in kinds],
        idx, *attention_pieces, after=[token],
        scratch=[pltpu.VMEM((4, thin, LANES), F32), pltpu.VMEM((2, 8, 8, width), F32)], smem=1,
    )
    return (
        text_result,
        layout_result.T,
        text_in_grad,
        layout_in_grad.T,
        qkv_t,
        qv_t,
        out_t,
        out_bias_t,
        gains_t,
        shifts_t,
        up_t,
        ub_t,
        down_t,
        qkv_l,
        qv_l,
        out_l,
        out_bias_l,
        gains_l,
        shifts_l,
        up_l,
        ub_l,
        down_l.T,
    )


def solution(mesh):
    rows, both, halves = P("seq", None), P(), P("tensor", None)
    stack, columns, one = P(None, None, "tensor"), P(None, "tensor"), P("tensor")
    weights_in = (stack, columns, halves, both, both, both, columns, one, halves)
    return jax.shard_map(
        per_device,
        mesh=mesh,
        in_specs=(rows,) * 4 + (P("seq"),) * 3 + weights_in * 2,
        out_specs=(rows,) * 4 + weights_in * 2,
        check_vma=False,
    )
```
